32 devices in a mesh: dp: 8 (over z, y), rows: 4 (over x, core).
Axes of the slice: x: 2, y: 2, z: 4, core: 2. Of those that a mesh axis runs over, the one named last changes fastest.
Arguments:
- images: bfloat16 [16, 40, 48, 512], P('dp', 'rows'), may hold values from -6 to 6
- size_ids: int32 [16], replicated, may hold values from 0 to 1, as said below
- shared_conv: bfloat16 [2, 4608, 512], replicated, may hold values from -0.09375 to 0.09375
- task_conv: bfloat16 [3, 4608, 512], replicated, may hold values from -0.09375 to 0.09375
- task_down: bfloat16 [3, 512, 512], replicated, may hold values from -0.25 to 0.25
- task_up: bfloat16 [3, 512, 512], replicated, may hold values from -0.25 to 0.25
- shared_gain: float32 [2, 512], replicated, may hold values from 0.5 to 1.5
- shared_shift: float32 [2, 512], replicated, may hold values from -3 to 3
- down_gain: float32 [3, 512], replicated, may hold values from 0.5 to 1.5
- down_shift: float32 [3, 512], replicated, may hold values from -3 to 3
- up_gain: float32 [3, 512], replicated, may hold values from 0.5 to 1.5
- up_shift: float32 [3, 512], replicated, may hold values from -3 to 3
- conv_gain: float32 [3, 512], replicated, may hold values from 0.5 to 1.5
- conv_shift: float32 [3, 512], replicated, may hold values from -3 to 3
- cotangent: bfloat16 [3, 16, 20, 24, 512], P(None, 'dp', 'rows'), may hold values from -6 to 6
Outputs:
- task_maps: bfloat16 [3, 16, 20, 24, 512], P(None, 'dp', 'rows')
- input_grad: float32 [16, 40, 48, 512], P('dp', 'rows')
- shared_conv_grad: float32 [2, 4608, 512], P(None, 'dp')
- task_conv_grad: float32 [3, 4608, 512], P(None, 'dp')
- down_grad: float32 [3, 512, 512], P(None, 'dp')
- up_grad: float32 [3, 512, 512], P(None, None, 'dp')
- shared_gain_grad: float32 [2, 512], replicated
- shared_shift_grad: float32 [2, 512], replicated
- down_gain_grad: float32 [3, 512], replicated
- down_shift_grad: float32 [3, 512], replicated
- up_gain_grad: float32 [3, 512], replicated
- up_shift_grad: float32 [3, 512], replicated
- conv_gain_grad: float32 [3, 512], replicated
- conv_shift_grad: float32 [3, 512], replicated
The draws below stay inside these ranges and needn't reach their ends.
Inputs may be any that keep to these rules, and one draw needn't show every extreme that they name: `size_ids`: 0 names a 36 x 48 map and 1 a 18 x 24 map, each placed at the frame's first rows and columns; every aligned group of 2 slots holds at least one map of the first kind.
All inputs are finite; a program needn't handle non-finite values.
Results may differ from the reference program's by a relative error of at most 0.02.
Values may be sent and summed in bfloat16 or wider, within the bound.
No kernel may reach another device: no remote copies, remote signals or barrier semaphores. Data moves between devices by JAX's collectives and lax.ppermute only.
A program may use at most 256 MiB of HBM per device.

```python
import jax
import jax.numpy as jnp
from jax import lax

C = 512
CR = 512
TASKS = 3
H_BIG = 36
W_BIG = 48
H_SMALL = 18
W_SMALL = 24
FH = 40
S_DEV = 2
W = 48
PH = 20
B_ALL = 16


def draw_size_ids(key, part):
    key = jax.random.fold_in(key, 7)
    coin_key, pick_key = jax.random.split(key)
    groups = B_ALL // S_DEV
    coins = jax.random.randint(coin_key, (groups, S_DEV), 0, 2)
    chosen = jax.random.randint(pick_key, (groups, 1), 0, S_DEV)
    places = jnp.arange(S_DEV)[None, :]
    labels = jnp.where(places == chosen, 0, coins)
    return labels.reshape(-1).astype(jnp.int32)


def level_of(rng, extent, cuts, least, top_value):
    def one(position, blocks):
        draws = jax.random.uniform(jax.random.fold_in(jax.random.fold_in(rng, 6), position), (blocks,), jnp.float32, least / len(cuts), top_value / len(cuts))
        return jnp.repeat(jnp.exp(draws), extent[position] // blocks).reshape((-1,) + (1,) * (len(extent) - position - 1))

    loudness = one(*cuts[0])
    for cut in cuts[1:]:
        loudness = loudness * one(*cut)
    return loudness


def normal_values(rng, shape, deviation, bound, pieces=(), dtype=jnp.bfloat16):
    loudness = level_of(rng, shape, pieces, -0.22, 0.18) if pieces else 1.0
    values = jax.random.normal(rng, shape, jnp.float32) * deviation * loudness
    return jnp.minimum(jnp.maximum(values, -bound), bound).astype(dtype)


def setup_inputs(seed: int = 0) -> dict:
    streams_of = jax.random.split(jax.random.key(seed), 16)
    images = normal_values(streams_of[0], (B_ALL, FH, W, C), 1.0, 6.0, ((0, 8), (1, 4)))
    size_ids = draw_size_ids(jax.random.fold_in(streams_of[15], 71), 0)
    shared_conv = normal_values(streams_of[2], (2, 9 * C, C), (9 * C) ** -0.5, 0.09375)
    task_conv = normal_values(streams_of[3], (TASKS, 9 * C, C), (9 * C) ** -0.5, 0.09375)
    task_down = normal_values(streams_of[4], (TASKS, C, CR), C ** -0.5, 0.25)
    task_up = normal_values(streams_of[5], (TASKS, CR, C), CR ** -0.5, 0.25)
    shared_gain = jnp.clip(jax.random.uniform(streams_of[6], (2, C), jnp.float32, 0.5, 1.5), 0.5, 1.5)
    shared_shift = normal_values(streams_of[7], (2, C), 0.5, 3.0, (), jnp.float32)
    down_gain = jnp.clip(jax.random.uniform(streams_of[8], (TASKS, CR), jnp.float32, 0.5, 1.5), 0.5, 1.5)
    down_shift = normal_values(streams_of[9], (TASKS, CR), 0.5, 3.0, (), jnp.float32)
    up_gain = jnp.clip(jax.random.uniform(streams_of[10], (TASKS, C), jnp.float32, 0.5, 1.5), 0.5, 1.5)
    up_shift = normal_values(streams_of[11], (TASKS, C), 0.5, 3.0, (), jnp.float32)
    conv_gain = jnp.clip(jax.random.uniform(streams_of[12], (TASKS, C), jnp.float32, 0.5, 1.5), 0.5, 1.5)
    conv_shift = normal_values(streams_of[13], (TASKS, C), 0.5, 3.0, (), jnp.float32)
    cotangent = normal_values(streams_of[14], (TASKS, B_ALL, PH, W // 2, C), 1.0, 6.0, ((1, 8), (2, 4)))
    return {"images": images, "size_ids": size_ids, "shared_conv": shared_conv, "task_conv": task_conv, "task_down": task_down, "task_up": task_up, "shared_gain": shared_gain, "shared_shift": shared_shift, "down_gain": down_gain, "down_shift": down_shift, "up_gain": up_gain, "up_shift": up_shift, "conv_gain": conv_gain, "conv_shift": conv_shift, "cotangent": cotangent}


EPSILON = 1e-05
PRECISE = lax.Precision.HIGHEST

@jax.custom_vjp
def low(v):
    return lax.optimization_barrier(v.astype(jnp.bfloat16)).astype(jnp.float32)

@jax.custom_vjp
def low_back(v):
    return v

def low_keep(v):
    return (low(v), None)

def low_pass(kept, grad):
    return (grad,)

def back_keep(v):
    return (v, None)

def back_low(kept, grad):
    return (low(grad),)
low.defvjp(low_keep, low_pass)
low_back.defvjp(back_keep, back_low)

def conv_three(values, weight):
    channels = values.shape[3]
    height = values.shape[1]
    breadth = values.shape[2]
    padded = jnp.pad(values, ((0, 0), (1, 1), (1, 1), (0, 0)))
    total = jnp.zeros(values.shape[:3] + (weight.shape[1],), jnp.float32)
    for tap_row in range(3):
        for tap_col in range(3):
            offset = (tap_row * 3 + tap_col) * channels
            window = padded[:, tap_row:tap_row + height, tap_col:tap_col + breadth]
            total = total + jnp.einsum('bhwc,cd->bhwd', window, weight[offset:offset + channels], precision=PRECISE)
    return total

def batch_norm(values, valid_mask, pixel_count, gain, shift):
    masked = values * valid_mask
    average = lax.optimization_barrier(jnp.sum(masked, axis=(0, 1, 2))) / pixel_count
    variance = lax.optimization_barrier(jnp.sum(masked * values, axis=(0, 1, 2))) / pixel_count - average * average
    return gain * (values - average) * lax.rsqrt(variance + EPSILON) + shift

def project(values, weight):
    return jnp.einsum('bhwc,cd->bhwd', values, weight, precision=PRECISE)

def reference(images, size_ids, shared_conv, task_conv, task_down, task_up, shared_gain, shared_shift, down_gain, down_shift, up_gain, up_shift, conv_gain, conv_shift, cotangent):
    heights = jnp.where(size_ids == 0, H_BIG, H_SMALL)
    breadths = jnp.where(size_ids == 0, W_BIG, W_SMALL)
    row_place = jnp.arange(FH)
    col_place = jnp.arange(W)
    inside = (row_place[None, :, None] < heights[:, None, None]) & (col_place[None, None, :] < breadths[:, None, None])
    valid_mask = inside.astype(jnp.float32)[..., None]
    pixel_count = jnp.sum(valid_mask)

    def forward(pixels, shared_weight, conv_weight, down_weight, up_weight, shared_scale, shared_bias, down_scale, down_bias, up_scale, up_bias, conv_scale, conv_bias):
        first_out = low_back(conv_three(pixels * valid_mask, shared_weight[0]))
        hidden = low(jax.nn.silu(batch_norm(first_out, valid_mask, pixel_count, shared_scale[0], shared_bias[0])) * valid_mask)
        second = low_back(conv_three(hidden, shared_weight[1]))
        shared = low(jax.nn.silu(batch_norm(second, valid_mask, pixel_count, shared_scale[1], shared_bias[1])) * valid_mask)
        pooled_maps = []
        for branch in range(TASKS):
            lowered = low_back(project(shared, down_weight[branch]))
            squeezed = low(jax.nn.silu(batch_norm(lowered, valid_mask, pixel_count, down_scale[branch], down_bias[branch])) * valid_mask)
            raised = low_back(project(squeezed, up_weight[branch]))
            attention = jax.nn.sigmoid(batch_norm(raised, valid_mask, pixel_count, up_scale[branch], up_bias[branch]))
            gated = low(attention * shared)
            convolved = low_back(conv_three(gated, conv_weight[branch]))
            active = jax.nn.silu(batch_norm(convolved, valid_mask, pixel_count, conv_scale[branch], conv_bias[branch])) * valid_mask
            pooled_maps.append(active.reshape(B_ALL, FH // 2, 2, W // 2, 2, C).mean(axis=(2, 4)))
        return jnp.stack(pooled_maps)
    primals = tuple((element.astype(jnp.float32) for element in (images, shared_conv, task_conv, task_down, task_up, shared_gain, shared_shift, down_gain, down_shift, up_gain, up_shift, conv_gain, conv_shift)))
    outputs, pullback = jax.vjp(forward, *primals)
    gradients = pullback(cotangent.astype(jnp.float32))
    return (outputs.astype(jnp.bfloat16), gradients[0], gradients[1], gradients[2], gradients[3], gradients[4], gradients[5], gradients[6], gradients[7], gradients[8], gradients[9], gradients[10], gradients[11], gradients[12])
```

```python
import jax
import jax.numpy as jnp
from jax import lax
from jax.sharding import PartitionSpec as P

H_BIG = 36
W_BIG = 48
H_SMALL = 18
W_SMALL = 24


EPSILON = 1e-05


def with_halo(cells, sides, width):
    for axis, dim in sides:
        count = lax.axis_size(axis)
        ends = count - 1
        head = lax.slice_in_dim(cells, 0, width, axis=dim)
        tail = lax.slice_in_dim(cells, cells.shape[dim] - width, cells.shape[dim], axis=dim)
        cells = jnp.concatenate(
            [
                lax.ppermute(tail, axis, [(i, (i + 1) % count) for i in range(ends)]),
                cells,
                lax.ppermute(head, axis, [((i + 1) % count, i) for i in range(ends)]),
            ],
            axis=dim,
        )
    return cells


def silu_slope(values):
    logistic = jax.nn.sigmoid(values)
    return logistic * (1.0 + values * (1.0 - logistic))


def widen(values):
    padded = with_halo(values, (("rows", 1),), 1)
    return jnp.pad(padded, ((0, 0), (0, 0), (1, 1), (0, 0)))


def windows(padded, height, breadth, flipped):
    pieces = []
    for tap_row in range(3):
        for tap_col in range(3):
            top_row = 2 - tap_row if flipped else tap_row
            left_col = 2 - tap_col if flipped else tap_col
            pieces.append(padded[:, top_row : top_row + height, left_col : left_col + breadth])
    return jnp.concatenate(pieces, axis=-1)


def conv_apply(values, weight):
    slot_count, height, breadth, channels = values.shape
    padded = widen(values)
    columns = windows(padded, height, breadth, False).reshape(-1, 9 * channels)
    result = jnp.dot(columns, weight, preferred_element_type=jnp.float32)
    return (result.reshape(slot_count, height, breadth, weight.shape[1]), padded)


def conv_back(grad_out, weight, padded):
    slot_count, height, breadth, out_channels = grad_out.shape
    channels = weight.shape[0] // 9
    columns = windows(padded, height, breadth, False).reshape(-1, 9 * channels)
    weight_grad = lax.dot_general(
        columns,
        grad_out.reshape(-1, out_channels),
        (((0,), (0,)), ((), ())),
        preferred_element_type=jnp.float32,
    )
    grad_padded = widen(grad_out)
    grad_columns = windows(grad_padded, height, breadth, True).reshape(-1, 9 * out_channels)
    turned = (
        weight.reshape(9, channels, out_channels)
        .transpose(0, 2, 1)
        .reshape(9 * out_channels, channels)
    )
    grad_in = jnp.dot(grad_columns, turned, preferred_element_type=jnp.float32)
    return (weight_grad, grad_in.reshape(slot_count, height, breadth, channels))


AXES = ("dp", "rows")


def swapped(values, flip):
    count = lax.axis_size("dp") * lax.axis_size("rows")
    return lax.ppermute(values, AXES, [(i, i ^ flip) for i in range(count)])


def exchange_sum(values):
    count = lax.axis_size("dp") * lax.axis_size("rows")
    bits = count.bit_length() - 1
    assert count == 1 << bits
    values = values + swapped(values, 1)
    place = 1
    while place < bits:
        low = 1 << place
        if place + 1 < bits:
            high = low * 2
            values = (values + swapped(values, low)) + (
                swapped(values, high) + swapped(values, high + low)
            )
            place += 2
        else:
            values = values + swapped(values, low)
            place += 1
    return values


def scattered_sum(values):
    parts, height, breadth = values.shape
    dp_count = lax.axis_size("dp")
    row_count = lax.axis_size("rows")
    dp_bits = dp_count.bit_length() - 1
    row_bits = row_count.bit_length() - 1
    place = lax.axis_index("dp") * row_count + lax.axis_index("rows")
    bits = dp_bits + row_bits
    folded = values.reshape((parts,) + (2,) * bits + (height >> bits, breadth))
    left = list(range(bits - 1, -1, -1))
    halves = jnp.split(folded, 2, axis=-1)

    def halve(piece, left, bit):
        axis = 1 + left.index(bit)
        mine = (place >> bit) & 1
        keep = lax.dynamic_index_in_dim(piece, mine, axis, keepdims=False)
        send = lax.dynamic_index_in_dim(piece, 1 - mine, axis, keepdims=False)
        got = swapped(send, 1 << bit)
        total = keep.astype(jnp.float32) + got.astype(jnp.float32)
        return total.astype(values.dtype), [b for b in left if b != bit]

    done = []
    for turn, piece in enumerate(halves):
        order = list(range(bits))
        if turn and bits > 2:
            order[1], order[2] = order[2], order[1]
        kept = left
        for bit in order:
            piece, kept = halve(piece, kept, bit)
        done.append(piece)
    piece = jnp.concatenate(done, axis=-1)
    piece = piece.reshape((parts,) + (1,) * row_bits + piece.shape[1:])
    for bit in range(row_bits - 1, -1, -1):
        other = swapped(piece, 1 << bit)
        mine = (place >> bit) & 1
        pair = jnp.where(mine == 0, jnp.stack([piece, other]), jnp.stack([other, piece]))
        axis = row_bits - bit
        piece = jnp.concatenate([pair[0], pair[1]], axis=axis)
    return piece.reshape(parts, height // dp_count, breadth).astype(jnp.float32)


def normalize(arrays, gains, shifts, valid_mask, pixel_count):
    partials = []
    for values in arrays:
        masked = values * valid_mask
        partials.append(jnp.sum(masked, axis=(0, 1, 2)))
        partials.append(jnp.sum(masked * values, axis=(0, 1, 2)))
    totals = exchange_sum(jnp.stack(partials))
    outputs = []
    saved = []
    for member, values in enumerate(arrays):
        average = totals[2 * member] / pixel_count
        variance = totals[2 * member + 1] / pixel_count - average * average
        inverse = lax.rsqrt(variance + EPSILON)
        centred = (values - average) * inverse
        outputs.append(gains[member] * centred + shifts[member])
        saved.append((centred, inverse))
    return (outputs, saved)


def restore(gradients, saved, gains, valid_mask, pixel_count):
    partials = []
    for grad_out, pair in zip(gradients, saved):
        partials.append(jnp.sum(grad_out, axis=(0, 1, 2)))
        partials.append(jnp.sum(grad_out * pair[0], axis=(0, 1, 2)))
    totals = exchange_sum(jnp.stack(partials))
    inputs = []
    for member, grad_out in enumerate(gradients):
        centred, inverse = saved[member]
        correction = (
            valid_mask * (totals[2 * member] + centred * totals[2 * member + 1]) / pixel_count
        )
        inputs.append((gains[member] * inverse * (grad_out - correction)).astype(jnp.bfloat16))
    return (inputs, totals)


def local(
    images,
    size_ids,
    shared_conv,
    task_conv,
    task_down,
    task_up,
    shared_gain,
    shared_shift,
    down_gain,
    down_shift,
    up_gain,
    up_shift,
    conv_gain,
    conv_shift,
    cotangent,
):
    slot_count, part_rows, breadth, channels = images.shape
    task_count = task_conv.shape[0]
    heights_all = jnp.where(size_ids == 0, H_BIG, H_SMALL).astype(jnp.int32)
    breadths_all = jnp.where(size_ids == 0, W_BIG, W_SMALL).astype(jnp.int32)
    pixel_count = jnp.sum(heights_all * breadths_all).astype(jnp.float32)
    first_slot = lax.axis_index("dp") * slot_count
    heights = lax.dynamic_slice_in_dim(heights_all, first_slot, slot_count)
    breadths = lax.dynamic_slice_in_dim(breadths_all, first_slot, slot_count)
    row_place = lax.axis_index("rows") * part_rows + jnp.arange(part_rows, dtype=jnp.int32)
    col_place = jnp.arange(breadth, dtype=jnp.int32)
    inside = (row_place[None, :, None] < heights[:, None, None]) & (
        col_place[None, None, :] < breadths[:, None, None]
    )
    valid_mask = inside.astype(jnp.float32)[..., None]
    masked_input = jnp.where(inside[..., None], images, jnp.zeros_like(images))
    first_out, first_pad = conv_apply(masked_input, shared_conv[0])
    first_norm, first_saved = normalize(
        [first_out], shared_gain[0:1], shared_shift[0:1], valid_mask, pixel_count
    )
    hidden = (jax.nn.silu(first_norm[0]) * valid_mask).astype(jnp.bfloat16)
    second_out, second_pad = conv_apply(hidden, shared_conv[1])
    second_norm, second_saved = normalize(
        [second_out], shared_gain[1:2], shared_shift[1:2], valid_mask, pixel_count
    )
    shared_feat = (jax.nn.silu(second_norm[0]) * valid_mask).astype(jnp.bfloat16)
    shared_wide = shared_feat.astype(jnp.float32)
    lowered = [
        jnp.dot(shared_feat, task_down[branch], preferred_element_type=jnp.float32)
        for branch in range(task_count)
    ]
    down_norm, down_saved = normalize(lowered, down_gain, down_shift, valid_mask, pixel_count)
    squeezed = [(jax.nn.silu(element) * valid_mask).astype(jnp.bfloat16) for element in down_norm]
    raised = [
        jnp.dot(squeezed[branch], task_up[branch], preferred_element_type=jnp.float32)
        for branch in range(task_count)
    ]
    up_norm, up_saved = normalize(raised, up_gain, up_shift, valid_mask, pixel_count)
    attention = [jax.nn.sigmoid(element) for element in up_norm]
    gated = [(attention[branch] * shared_wide).astype(jnp.bfloat16) for branch in range(task_count)]
    conv_results = [conv_apply(gated[branch], task_conv[branch]) for branch in range(task_count)]
    conv_norm, conv_saved = normalize(
        [element[0] for element in conv_results], conv_gain, conv_shift, valid_mask, pixel_count
    )
    pooled_maps = []
    for branch in range(task_count):
        active = jax.nn.silu(conv_norm[branch]) * valid_mask
        pooled_maps.append(
            active.reshape(slot_count, part_rows // 2, 2, breadth // 2, 2, channels).mean(
                axis=(2, 4)
            )
        )
    maps_out = jnp.stack(pooled_maps).astype(jnp.bfloat16)
    cot_wide = cotangent.astype(jnp.float32)
    conv_incoming = []
    for branch in range(task_count):
        spread_grad = jnp.repeat(jnp.repeat(cot_wide[branch], 2, axis=1), 2, axis=2) * 0.25
        conv_incoming.append(spread_grad * valid_mask * silu_slope(conv_norm[branch]))
    conv_dz, conv_totals = restore(conv_incoming, conv_saved, conv_gain, valid_mask, pixel_count)
    shared_grad = jnp.zeros(shared_feat.shape, jnp.float32)
    conv_weight_grads = []
    up_incoming = []
    for branch in range(task_count):
        weight_grad, gated_grad = conv_back(
            conv_dz[branch], task_conv[branch], conv_results[branch][1]
        )
        conv_weight_grads.append(weight_grad)
        shared_grad = shared_grad + gated_grad * attention[branch]
        attention_grad = gated_grad * shared_wide
        up_incoming.append(attention_grad * attention[branch] * (1.0 - attention[branch]))
    up_dz, up_totals = restore(up_incoming, up_saved, up_gain, valid_mask, pixel_count)
    up_weight_grads = []
    down_incoming = []
    for branch in range(task_count):
        reduced = squeezed[branch].shape[-1]
        up_weight_grads.append(
            lax.dot_general(
                up_dz[branch].reshape(-1, channels),
                squeezed[branch].reshape(-1, reduced),
                (((0,), (0,)), ((), ())),
                preferred_element_type=jnp.float32,
            )
        )
        squeezed_grad = lax.dot_general(
            up_dz[branch],
            task_up[branch],
            (((3,), (1,)), ((), ())),
            preferred_element_type=jnp.float32,
        )
        down_incoming.append(squeezed_grad * valid_mask * silu_slope(down_norm[branch]))
    down_dz, down_totals = restore(down_incoming, down_saved, down_gain, valid_mask, pixel_count)
    down_weight_grads = []
    flat_shared = shared_feat.reshape(-1, channels)
    for branch in range(task_count):
        reduced = down_dz[branch].shape[-1]
        down_weight_grads.append(
            lax.dot_general(
                flat_shared,
                down_dz[branch].reshape(-1, reduced),
                (((0,), (0,)), ((), ())),
                preferred_element_type=jnp.float32,
            )
        )
        shared_grad = shared_grad + lax.dot_general(
            down_dz[branch],
            task_down[branch],
            (((3,), (1,)), ((), ())),
            preferred_element_type=jnp.float32,
        )
    second_dz, second_totals = restore(
        [shared_grad * valid_mask * silu_slope(second_norm[0])],
        second_saved,
        shared_gain[1:2],
        valid_mask,
        pixel_count,
    )
    second_weight_grad, hidden_grad = conv_back(second_dz[0], shared_conv[1], second_pad)
    first_dz, first_totals = restore(
        [hidden_grad * valid_mask * silu_slope(first_norm[0])],
        first_saved,
        shared_gain[0:1],
        valid_mask,
        pixel_count,
    )
    first_weight_grad, input_back = conv_back(first_dz[0], shared_conv[0], first_pad)
    input_grad = input_back * valid_mask
    low = jnp.bfloat16
    conv_part = scattered_sum(jnp.stack([g.astype(low) for g in conv_weight_grads]))
    thin = scattered_sum(
        jnp.stack([g.astype(low) for g in down_weight_grads + up_weight_grads])
    )
    down_part, up_part = thin[:task_count], thin[task_count:]
    second_part = scattered_sum(second_weight_grad.astype(low)[None])
    first_part = scattered_sum(first_weight_grad.astype(low)[None])
    shared_part = jnp.concatenate([first_part, second_part])
    up_grad = up_part.transpose(0, 2, 1)
    shared_gain_grad = jnp.stack([first_totals[1], second_totals[1]])
    shared_shift_grad = jnp.stack([first_totals[0], second_totals[0]])
    return (
        maps_out,
        input_grad,
        shared_part,
        conv_part,
        down_part,
        up_grad,
        shared_gain_grad,
        shared_shift_grad,
        down_totals[1::2],
        down_totals[0::2],
        up_totals[1::2],
        up_totals[0::2],
        conv_totals[1::2],
        conv_totals[0::2],
    )


def solution(mesh):
    placed = (
        P("dp", "rows", None, None),
        P(),
        P(),
        P(),
        P(),
        P(),
        P(),
        P(),
        P(),
        P(),
        P(),
        P(),
        P(),
        P(),
        P(None, "dp", "rows", None, None),
    )
    return jax.shard_map(
        local,
        mesh=mesh,
        in_specs=placed,
        out_specs=(
            P(None, "dp", "rows", None, None),
            P("dp", "rows", None, None),
            P(None, "dp", None),
            P(None, "dp", None),
            P(None, "dp", None),
            P(None, None, "dp"),
            P(),
            P(),
            P(),
            P(),
            P(),
            P(),
            P(),
            P(),
        ),
        check_vma=False,
    )
```

```python
import functools

import jax
import jax.numpy as jnp
from jax import lax
from jax.experimental import pallas as pl
from jax.experimental.pallas import tpu as pltpu
from jax.sharding import PartitionSpec as P

H_BIG = 36
W_BIG = 48
H_SMALL = 18
W_SMALL = 24
EPSILON = 1e-05
AXES = ("dp", "rows")
F32 = jnp.float32
BF16 = jnp.bfloat16
VMEM_BYTES = 56 * 1024 * 1024


def swapped(values, flip):
    count = lax.axis_size("dp") * lax.axis_size("rows")
    return lax.ppermute(values, AXES, [(i, i ^ flip) for i in range(count)])


def exchange_sum(values):
    count = lax.axis_size("dp") * lax.axis_size("rows")
    bits = count.bit_length() - 1
    assert count == 1 << bits
    values = values + swapped(values, 1)
    place = 1
    while place < bits:
        low = 1 << place
        if place + 1 < bits:
            high = low * 2
            values = (values + swapped(values, low)) + (
                swapped(values, high) + swapped(values, high + low)
            )
            place += 2
        else:
            values = values + swapped(values, low)
            place += 1
    return values


def gathered_sum(values):
    count = lax.axis_size("dp") * lax.axis_size("rows")
    spread = jnp.broadcast_to(values[None], (count,) + values.shape)
    return jnp.sum(lax.all_to_all(spread, AXES, 0, 0), axis=0)


def edges_swapped(edges):
    count = lax.axis_size("rows")
    above = lax.ppermute(edges[1], "rows", [(i, i + 1) for i in range(count - 1)])
    below = lax.ppermute(edges[0], "rows", [(i + 1, i) for i in range(count - 1)])
    return above, below


def core_bit():
    return lax.axis_index("rows") & 1


def scattered_sum(values, whole, swap_first=False):
    parts, height, breadth = values.shape
    dp_count = lax.axis_size("dp")
    row_count = lax.axis_size("rows")
    place = lax.axis_index("dp") * row_count + lax.axis_index("rows")
    first = 0 if whole else 1
    bits = (dp_count * row_count).bit_length() - 1
    row_bits = row_count.bit_length() - 1
    left = list(range(bits - 1, first - 1, -1))
    piece = values.reshape((parts,) + (2,) * len(left) + (height >> len(left), breadth))
    order = list(range(first, bits))
    if swap_first and bits > 2:
        low = 1 - first
        order[low], order[low + 1] = order[low + 1], order[low]
    for bit in order:
        axis = 1 + left.index(bit)
        mine = (place >> bit) & 1
        keep = lax.dynamic_index_in_dim(piece, mine, axis, keepdims=False)
        send = lax.dynamic_index_in_dim(piece, 1 - mine, axis, keepdims=False)
        got = swapped(send, 1 << bit)
        piece = (keep.astype(F32) + got.astype(F32)).astype(values.dtype)
        left.remove(bit)
    return piece


def rejoined(piece, whole):
    parts = piece.shape[0]
    row_count = lax.axis_size("rows")
    row_bits = row_count.bit_length() - 1
    first = 0 if whole else 1
    piece = piece.reshape((parts,) + (1,) * (row_bits - first) + piece.shape[-2:])

    def joined(piece, bit, axis):
        other = swapped(piece, 1 << bit)
        mine = (lax.axis_index("rows") >> bit) & 1
        lower = jnp.where(mine == 0, piece, other)
        upper = jnp.where(mine == 0, other, piece)
        return jnp.concatenate([lower, upper], axis=axis)

    for bit in range(row_bits - 1, first - 1, -1):
        piece = joined(piece, bit, row_bits - bit)
    piece = piece.reshape(parts, -1, piece.shape[-1])
    if not whole:
        piece = joined(piece, 0, 2)
    return piece.astype(F32)


def dot(left, right):
    return jnp.dot(left, right, preferred_element_type=F32)


def dot_turned(left, right):
    return lax.dot_general(left, right, (((1,), (1,)), ((), ())), preferred_element_type=F32)


def inside_row(limits, place, breadth, channels):
    return lax.broadcasted_iota(jnp.int32, (breadth, channels), 0) < limits[place]


def moments(totals, member, count):
    average = totals[2 * member : 2 * member + 1, :] / count
    variance = totals[2 * member + 1 : 2 * member + 2, :] / count - average * average
    return average, lax.rsqrt(variance + EPSILON)


def sigmoid(values):
    return 1.0 / (1.0 + jnp.exp(-values))


def silu_slope(values):
    logistic = sigmoid(values)
    return logistic * (1.0 + values * (1.0 - logistic))


def fold(values):
    return jnp.sum(values.reshape(-1, 8, values.shape[-1]), axis=0)


def shifted(values):
    breadth = values.shape[0]
    col = lax.broadcasted_iota(jnp.int32, values.shape, 0)
    before = jnp.where(col == 0, 0.0, pltpu.roll(values, 1, 0))
    after = jnp.where(col == breadth - 1, 0.0, pltpu.roll(values, breadth - 1, 0))
    return before, after


def put_three(ref, slot, row, values, flipped):
    channels = values.shape[1]
    before, after = shifted(values)
    if flipped:
        before, after = after, before
    ref[slot, row, :, 0:channels] = before.astype(BF16)
    ref[slot, row, :, channels : 2 * channels] = values.astype(BF16)
    ref[slot, row, :, 2 * channels :] = after.astype(BF16)


def each_row(slots, rows, body):
    def step(index, carry):
        body(index // rows, index % rows)
        return carry

    lax.fori_loop(0, slots * rows, step, 0)


def each_row_summed(slots, rows, channels, body):
    def step(index, carry):
        one, two = body(index // rows, index % rows)
        return carry[0] + fold(one), carry[1] + fold(two)

    zero = jnp.zeros((8, channels), F32)
    one, two = lax.fori_loop(0, slots * rows, step, (zero, zero))
    return jnp.sum(one, axis=0, keepdims=True), jnp.sum(two, axis=0, keepdims=True)


def put_pair(ref, pair, lead=()):
    ref[lead + (slice(0, 1), slice(None))] = pair[0]
    ref[lead + (slice(1, 2), slice(None))] = pair[1]


def add_taps(step, sums, lead, parts):
    slots = sums.shape[len(lead)]
    shape = sums.shape[len(lead) + 1 :]
    for slot in range(slots):
        part = parts(slot).reshape(shape)

        @pl.when(step == 0)
        def _():
            sums[lead + (slot,)] = part

        @pl.when(step > 0)
        def _():
            sums[lead + (slot,)] += part


def forward_taps(step, three, weight, sums, lead=()):
    rows, breadth, channels = sums.shape[-3:]

    def part(slot):
        window = three[slot, pl.ds(step, rows)].reshape(rows * breadth, -1)
        return dot(window, weight)

    add_taps(step, sums, lead, part)


def backward_taps(step, three, weight, sums):
    rows, breadth, channels = sums.shape[-3:]

    def part(slot):
        window = three[slot, pl.ds(2 - step, rows)].reshape(rows * breadth, -1)
        wide = window.shape[1] // 3
        total = None
        for tap in range(3):
            one = dot_turned(
                window[:, tap * wide : (tap + 1) * wide],
                weight[tap * channels : (tap + 1) * channels],
            )
            total = one if total is None else total + one
        return total

    add_taps(step, sums, (), part)


def conv_sums(sums, lead, limits, stats, edges, stat_lead):
    slots, rows, breadth, channels = sums.shape[-4:]

    def body(slot, row):
        values = sums[lead + (slot, row)]
        kept = jnp.where(
            inside_row(limits, slot * (rows + 2) + row + 1, breadth, channels), values, 0.0
        )
        return kept, kept * values

    put_pair(stats, each_row_summed(slots, rows, channels, body), stat_lead)
    for slot in range(slots):
        edges[stat_lead + (0, slot)] = sums[lead + (slot, 0)]
        edges[stat_lead + (1, slot)] = sums[lead + (slot, rows - 1)]


def first_kernel(limits, images, above, below, weight, sums, stats, edges, three):
    step = pl.program_id(0)
    slots, rows, breadth, channels = images.shape

    @pl.when(step == 0)
    def _():
        def put(slot, row, values):
            inside = inside_row(limits, slot * (rows + 2) + row, breadth, channels)
            put_three(three, slot, row, jnp.where(inside, values.astype(F32), 0.0), False)

        each_row(slots, rows, lambda slot, row: put(slot, row + 1, images[slot, row]))
        for slot in range(slots):
            put(slot, 0, above[slot])
            put(slot, rows + 1, below[slot])

    forward_taps(step, three, weight[...], sums)

    @pl.when(step == 2)
    def _():
        conv_sums(sums, (), limits, stats, edges, ())


def activation(values, inside, average, inverse, gain, shift):
    normed = gain * ((values - average) * inverse) + shift
    return jnp.where(inside, normed * sigmoid(normed), 0.0)


def second_kernel(
    limits, count, source, above, below, totals, gain, shift, weight, sums, stats, edges, hidden, three
):
    step = pl.program_id(0)
    slots, rows, breadth, channels = source.shape

    @pl.when(step == 0)
    def _():
        average, inverse = moments(totals, 0, count[0])

        def act(slot, row, values):
            inside = inside_row(limits, slot * (rows + 2) + row, breadth, channels)
            result = activation(values, inside, average, inverse, gain[...], shift[...])
            put_three(three, slot, row, result, False)
            return result

        def own(slot, row):
            hidden[slot, row] = act(slot, row + 1, source[slot, row]).astype(BF16)

        each_row(slots, rows, own)
        for slot in range(slots):
            act(slot, 0, above[slot])
            act(slot, rows + 1, below[slot])

    forward_taps(step, three, weight[...], sums)

    @pl.when(step == 2)
    def _():
        conv_sums(sums, (), limits, stats, edges, ())


def plain_sums(source, slots, rows, breadth, channels):
    def body(slot, row):
        values = source[pl.ds(pl.multiple_of((slot * rows + row) * breadth, breadth), breadth), :]
        return values, values * values

    return each_row_summed(slots, rows, channels, body)


def lower_kernel(
    limits, count, source, above, below, totals, gain, shift, down, shared, stats, lowered
):
    branch = pl.program_id(0)
    slots, rows, breadth, channels = source.shape

    @pl.when(branch == 0)
    def _():
        average, inverse = moments(totals, 0, count[0])

        def act(slot, row, values):
            inside = inside_row(limits, slot * (rows + 2) + row, breadth, channels)
            result = activation(values, inside, average, inverse, gain[...], shift[...])
            shared[slot, row] = result.astype(BF16)

        each_row(slots, rows, lambda slot, row: act(slot, row + 1, source[slot, row]))
        for slot in range(slots):
            act(slot, 0, above[slot])
            act(slot, rows + 1, below[slot])

    part = rows * breadth
    for slot in range(slots):
        lowered[slot * part : (slot + 1) * part, :] = dot(
            shared[slot, 1 : rows + 1].reshape(part, channels), down[0]
        )
    put_pair(stats, plain_sums(lowered, slots, rows, breadth, channels), (0,))


def raise_kernel(
    limits, count, shared, down, up, totals, gain, shift, squeezed, stats, wide, raised
):
    slots, tall, breadth, channels = shared.shape
    rows = tall - 2
    narrow = down.shape[2]
    wide[...] = dot(shared[...].reshape(slots * tall * breadth, channels), down[0])
    average, inverse = moments(totals[0], 0, count[0])

    def act(slot, row):
        inside = inside_row(limits, slot * tall + row, breadth, narrow)
        values = wide[pl.ds(pl.multiple_of((slot * tall + row) * breadth, breadth), breadth), :]
        result = activation(values, inside, average, inverse, gain[0], shift[0])
        squeezed[0, slot, row] = result.astype(BF16)

    each_row(slots, tall, act)
    part = rows * breadth
    for slot in range(slots):
        raised[slot * part : (slot + 1) * part, :] = dot(
            squeezed[0, slot, 1 : rows + 1].reshape(part, narrow), up[0]
        )
    put_pair(stats, plain_sums(raised, slots, rows, breadth, channels), (0,))


def task_kernel(
    limits, count, squeezed, up, shared, totals, gain, shift, weight, sums, stats, edges, gated, wide, three
):
    step = pl.program_id(1)
    slots, tall, breadth, channels = shared.shape
    rows = tall - 2

    @pl.when(step == 0)
    def _():
        wide[...] = dot(squeezed[0].reshape(slots * tall * breadth, -1), up[0])
        average, inverse = moments(totals[0], 0, count[0])

        def gate(slot, row):
            values = wide[pl.ds(pl.multiple_of((slot * tall + row) * breadth, breadth), breadth), :]
            normed = gain[0] * ((values - average) * inverse) + shift[0]
            result = sigmoid(normed) * shared[slot, row].astype(F32)
            put_three(three, slot, row, result, False)
            return result

        def own(slot, row):
            gated[0, slot, row] = gate(slot, row + 1).astype(BF16)

        each_row(slots, rows, own)
        for slot in range(slots):
            gate(slot, 0)
            gate(slot, rows + 1)

    forward_taps(step, three, weight[0], sums, (0,))

    @pl.when(step == 2)
    def _():
        conv_sums(sums, (0,), limits, stats, edges, (0,))


def pool_kernel(
    limits, count, source, cotangent, totals, gain, shift, maps, slope, stats, edges, spread, pairs
):
    slots, rows, breadth, channels = source.shape[1:]
    average, inverse = moments(totals[0], 0, count[0])
    half = breadth // 2
    groups = channels // 128

    def body(slot, pooled):
        block = cotangent[0, slot, pooled].astype(F32) * 0.25
        for group in range(groups):
            lanes = block[:, group * 128 : (group + 1) * 128]
            spread[group, pl.ds(0, half, stride=2), :] = lanes
            spread[group, pl.ds(1, half, stride=2), :] = lanes
        wide = jnp.concatenate([spread[group] for group in range(groups)], axis=1)
        one = two = total = None
        for parity in range(2):
            row = 2 * pooled + parity
            inside = inside_row(limits, slot * (rows + 2) + row + 1, breadth, channels)
            centred = (source[0, slot, row] - average) * inverse
            normed = gain[0] * centred + shift[0]
            logistic = sigmoid(normed)
            active = jnp.where(inside, normed * logistic, 0.0)
            grad = wide * (logistic * (1.0 + normed * (1.0 - logistic)))
            grad = jnp.where(inside, grad, 0.0)
            slope[0, slot, row] = grad
            along = grad * centred
            if parity == 0:
                one, two, total = grad, along, active
            else:
                one, two, total = one + grad, two + along, total + active
        for group in range(groups):
            pairs[group] = total[:, group * 128 : (group + 1) * 128]
            even = pairs[group, pl.ds(0, half, stride=2), :]
            odd = pairs[group, pl.ds(1, half, stride=2), :]
            lanes = slice(group * 128, (group + 1) * 128)
            maps[0, slot, pooled, :, lanes] = ((even + odd) * 0.25).astype(BF16)
        return one, two

    put_pair(stats, each_row_summed(slots, rows // 2, channels, body), (0,))
    for slot in range(slots):
        edges[0, 0, slot] = slope[0, slot, 0]
        edges[0, 1, slot] = slope[0, slot, rows - 1]


def norm_back(grad, values, inside, average, inverse, gain, back, count):
    centred = (values - average) * inverse
    correction = jnp.where(inside, (back[0:1] + centred * back[1:2]) / count, 0.0)
    return gain * inverse * (grad - correction)


def put_halves(ref, lead, slot, row, values):
    half = values.shape[1] // 2
    ref[lead + (0, slot, row)] = values[:, :half].astype(BF16)
    ref[lead + (1, slot, row)] = values[:, half:].astype(BF16)


def fill_back(
    limits, count, grads, grad_above, grad_below, source, above, below, totals, back, gain, three, halves, lead
):
    slots, rows, breadth, channels = source.shape[-4:]
    average, inverse = moments(totals, 0, count)

    def put(slot, row, grad, values):
        inside = inside_row(limits, slot * (rows + 2) + row, breadth, channels)
        result = norm_back(grad, values, inside, average, inverse, gain, back, count)
        if three is not None:
            put_three(three, slot, row, result, True)
        put_halves(halves, lead, slot, row, result)

    def own(slot, row):
        put(slot, row + 1, grads[lead + (slot, row)], source[lead + (slot, row)])

    each_row(slots, rows, own)
    for slot in range(slots):
        put(slot, 0, grad_above[lead + (slot,)], above[lead + (slot,)])
        put(slot, rows + 1, grad_below[lead + (slot,)], below[lead + (slot,)])


def gate_back_kernel(
    limits, count, grads, grad_above, grad_below, source, above, below, totals, back, gain, weight,
    squeezed, up, shared, up_totals, up_gain, up_shift,
    halves, incoming, shared_grad, stats, three, sums, raised,
):
    branch, step = pl.program_id(0), pl.program_id(1)
    slots, rows, breadth, channels = sums.shape

    @pl.when(step == 0)
    def _():
        fill_back(
            limits, count[0], grads, grad_above, grad_below, source, above, below,
            totals[0], back[0], gain[0], three, halves, (0,),
        )

    backward_taps(step, three, weight[0], sums)

    @pl.when(step == 2)
    def _():
        part = rows * breadth
        for slot in range(slots):
            raised[slot * part : (slot + 1) * part, :] = dot(
                squeezed[0, slot, 1 : rows + 1].reshape(part, -1), up[0]
            )
        average, inverse = moments(up_totals[0], 0, count[0])

        def body(slot, row):
            values = raised[pl.ds(pl.multiple_of((slot * rows + row) * breadth, breadth), breadth), :]
            centred = (values - average) * inverse
            attention = sigmoid(up_gain[0] * centred + up_shift[0])
            grad = sums[slot, row]
            result = grad * shared[slot, row + 1].astype(F32) * attention * (1.0 - attention)
            incoming[0, slot, row] = result
            onward = grad * attention

            @pl.when(branch == 0)
            def _():
                shared_grad[slot, row] = onward

            @pl.when(branch > 0)
            def _():
                shared_grad[slot, row] += onward

            return result, result * centred

        put_pair(stats, each_row_summed(slots, rows, channels, body), (0,))


def raise_back_kernel(
    limits, count, grads, squeezed, up, shared, down, up_totals, up_back, up_gain, down_totals, down_gain,
    down_shift, raised_grad, incoming, stats, wide, sums,
):
    slots, rows, breadth, channels = grads.shape[1:]
    part = rows * breadth
    for slot in range(slots):
        wide[slot * part : (slot + 1) * part, :] = dot(
            squeezed[0, slot, 1 : rows + 1].reshape(part, -1), up[0]
        )
    average, inverse = moments(up_totals[0], 0, count[0])

    def place(slot, row):
        return pl.ds(pl.multiple_of((slot * rows + row) * breadth, breadth), breadth)

    def back(slot, row):
        inside = inside_row(limits, slot * (rows + 2) + row + 1, breadth, channels)
        result = norm_back(
            grads[0, slot, row], wide[place(slot, row), :], inside, average, inverse, up_gain[0],
            up_back[0], count[0],
        )
        raised_grad[0, slot, row] = result.astype(BF16)

    each_row(slots, rows, back)
    for slot in range(slots):
        sums[slot * part : (slot + 1) * part, :] = dot_turned(
            raised_grad[0, slot].reshape(part, channels), up[0]
        )
        wide[slot * part : (slot + 1) * part, :] = dot(
            shared[slot, 1 : rows + 1].reshape(part, channels), down[0]
        )
    average2, inverse2 = moments(down_totals[0], 0, count[0])

    def body(slot, row):
        inside = inside_row(limits, slot * (rows + 2) + row + 1, breadth, channels)
        centred = (wide[place(slot, row), :] - average2) * inverse2
        normed = down_gain[0] * centred + down_shift[0]
        result = jnp.where(inside, sums[place(slot, row), :] * silu_slope(normed), 0.0)
        incoming[0, slot, row] = result
        return result, result * centred

    put_pair(stats, each_row_summed(slots, rows, channels, body), (0,))


def lower_back_kernel(
    limits, count, grads, shared, down, down_totals, down_back, down_gain, shared_grad, source, totals, gain,
    shift, lowered_grad, incoming, stats, edges, wide, sums,
):
    branch = pl.program_id(0)
    slots, rows, breadth, channels = source.shape
    part = rows * breadth
    for slot in range(slots):
        wide[slot * part : (slot + 1) * part, :] = dot(
            shared[slot, 1 : rows + 1].reshape(part, channels), down[0]
        )
    average, inverse = moments(down_totals[0], 0, count[0])

    def place(slot, row):
        return pl.ds(pl.multiple_of((slot * rows + row) * breadth, breadth), breadth)

    def back(slot, row):
        inside = inside_row(limits, slot * (rows + 2) + row + 1, breadth, channels)
        result = norm_back(
            grads[0, slot, row], wide[place(slot, row), :], inside, average, inverse, down_gain[0],
            down_back[0], count[0],
        )
        lowered_grad[0, slot, row] = result.astype(BF16)

    each_row(slots, rows, back)
    for slot in range(slots):
        span = slice(slot * part, (slot + 1) * part)
        term = dot_turned(lowered_grad[0, slot].reshape(part, -1), down[0])

        @pl.when(branch == 0)
        def _():
            sums[span, :] = term + shared_grad[slot].reshape(part, channels)

        @pl.when(branch > 0)
        def _():
            sums[span, :] += term

    @pl.when(branch == pl.num_programs(0) - 1)
    def _():
        average2, inverse2 = moments(totals, 0, count[0])

        def body(slot, row):
            inside = inside_row(limits, slot * (rows + 2) + row + 1, breadth, channels)
            centred = (source[slot, row] - average2) * inverse2
            normed = gain[...] * centred + shift[...]
            result = jnp.where(inside, sums[place(slot, row), :] * silu_slope(normed), 0.0)
            incoming[slot, row] = result
            return result, result * centred

        put_pair(stats, each_row_summed(slots, rows, channels, body))
        for slot in range(slots):
            edges[0, slot] = incoming[slot, 0]
            edges[1, slot] = incoming[slot, rows - 1]


def hidden_back_kernel(
    limits, count, grads, grad_above, grad_below, source, above, below, totals, back, gain, weight,
    first, first_totals, first_gain, first_shift, halves, incoming, stats, edges, three, sums,
):
    step = pl.program_id(0)
    slots, rows, breadth, channels = sums.shape

    @pl.when(step == 0)
    def _():
        fill_back(
            limits, count[0], grads, grad_above, grad_below, source, above, below,
            totals[...], back[...], gain[...], three, halves, (),
        )

    backward_taps(step, three, weight[...], sums)

    @pl.when(step == 2)
    def _():
        average, inverse = moments(first_totals, 0, count[0])

        def body(slot, row):
            inside = inside_row(limits, slot * (rows + 2) + row + 1, breadth, channels)
            centred = (first[slot, row] - average) * inverse
            normed = first_gain[...] * centred + first_shift[...]
            result = jnp.where(inside, sums[slot, row] * silu_slope(normed), 0.0)
            incoming[slot, row] = result
            return result, result * centred

        put_pair(stats, each_row_summed(slots, rows, channels, body))
        for slot in range(slots):
            edges[0, slot] = incoming[slot, 0]
            edges[1, slot] = incoming[slot, rows - 1]


def first_grad_kernel(
    limits, count, grads, grad_above, grad_below, source, above, below, totals, back, gain, halves
):
    fill_back(
        limits, count[0], grads, grad_above, grad_below, source, above, below,
        totals[...], back[...], gain[...], None, halves, (),
    )


def input_back_kernel(limits, halves, weight, out, three):
    step = pl.program_id(0)
    slots, rows, breadth, channels = out.shape

    @pl.when(step == 0)
    def _():
        def put(slot, row):
            values = jnp.concatenate([halves[0, slot, row], halves[1, slot, row]], axis=1)
            put_three(three, slot, row, values.astype(F32), True)

        each_row(slots, rows + 2, put)

    backward_taps(step, three, weight[...], out)

    @pl.when(step == 2)
    def _():
        def mask(slot, row):
            inside = inside_row(limits, slot * (rows + 2) + row + 1, breadth, channels)
            out[slot, row] = jnp.where(inside, out[slot, row], 0.0)

        each_row(slots, rows, mask)


def weight_grad_kernel(half, turned, turned_other, grads, grads_other, out, three):
    step = pl.program_id(0)
    slots, tall, breadth, channels = grads_other.shape
    rows = tall - 2

    @pl.when(step == 0)
    def _():
        def own(slot, row):
            put_three(three, slot, row, grads[0, slot, row].astype(F32), True)

        def other(slot, row):
            put_three(three, slots + slot, row, grads_other[slot, row].astype(F32), True)

        each_row(slots, tall, own)
        each_row(slots, tall, other)

    height = turned.shape[1]
    for tap in range(3):
        total = None
        for slot in range(2 * slots):
            left = turned[slot] if slot < slots else turned_other[slot - slots]
            window = three[slot, pl.ds(2 - step, rows), :, tap * channels : (tap + 1) * channels]
            one = dot(left, window.reshape(rows * breadth, channels))
            total = one if total is None else total + one
        out[tap * height : (tap + 1) * height, :] = total.astype(BF16)


def thin_grad_kernel(turned, right, out):
    slots = turned.shape[1]
    total = None
    for slot in range(slots):
        one = dot(turned[0, slot], right[0, slot])
        total = one if total is None else total + one
    out[0] = total.astype(BF16)


SCALARS = pl.BlockSpec(memory_space=pltpu.SMEM)


def fixed(shape):
    zeros = (0,) * len(shape)
    return pl.BlockSpec(tuple(shape), lambda *_: zeros)


def by_branch(shape):
    zeros = (0,) * (len(shape) - 1)
    return pl.BlockSpec((1,) + tuple(shape[1:]), lambda branch, *_: (branch,) + zeros)


def call(name, body, grid, inputs, outputs, scratch, flops, prefetch=0):
    total = sum(a.size * a.dtype.itemsize for a, _ in inputs)
    spec = dict(
        grid=grid,
        in_specs=[s for _, s in inputs[prefetch:]],
        out_specs=[s for _, _, s in outputs],
        scratch_shapes=scratch,
    )
    if prefetch:
        spec = dict(grid_spec=pltpu.PrefetchScalarGridSpec(num_scalar_prefetch=prefetch, **spec))
    return pl.pallas_call(
        body,
        name=name,
        out_shape=[jax.ShapeDtypeStruct(s, d) for s, d, _ in outputs],
        compiler_params=pltpu.CompilerParams(
            vmem_limit_bytes=VMEM_BYTES, dimension_semantics=("arbitrary",) * len(grid)
        ),
        cost_estimate=pl.CostEstimate(flops=flops, bytes_accessed=total, transcendentals=0),
        **spec,
    )(*[a for a, _ in inputs])


def local(
    images,
    size_ids,
    shared_conv,
    task_conv,
    task_down,
    task_up,
    shared_gain,
    shared_shift,
    down_gain,
    down_shift,
    up_gain,
    up_shift,
    conv_gain,
    conv_shift,
    cotangent,
):
    slots, rows, breadth, channels = images.shape
    tasks = task_conv.shape[0]
    tall = rows + 2
    part = rows * breadth
    heights_all = jnp.where(size_ids == 0, H_BIG, H_SMALL).astype(jnp.int32)
    breadths_all = jnp.where(size_ids == 0, W_BIG, W_SMALL).astype(jnp.int32)
    count = jnp.sum(heights_all * breadths_all).astype(F32).reshape(1)
    first_slot = lax.axis_index("dp") * slots
    heights = lax.dynamic_slice_in_dim(heights_all, first_slot, slots)
    breadths = lax.dynamic_slice_in_dim(breadths_all, first_slot, slots)
    row_place = lax.axis_index("rows") * rows + jnp.arange(-1, rows + 1, dtype=jnp.int32)
    within = (row_place[None, :] >= 0) & (row_place[None, :] < heights[:, None])
    limits = jnp.where(within, breadths[:, None], 0).astype(jnp.int32).reshape(-1)
    scalars = [(limits, SCALARS), (count, SCALARS)]

    map_shape = (slots, rows, breadth, channels)
    tall_shape = (slots, tall, breadth, channels)
    edge_shape = (2, slots, breadth, channels)
    half_shape = (2, slots, tall, breadth, channels // 2)
    pair_shape = (2, channels)
    conv_flops = 2 * slots * part * 9 * channels * channels
    thin_flops = conv_flops // 9

    def whole(a):
        return (a, fixed(a.shape))

    def branch(a):
        return (a, by_branch(a.shape))

    def out(shape, dtype):
        return (shape, dtype, fixed(shape))

    def out_branch(shape, dtype):
        shape = (tasks,) + tuple(shape)
        return (shape, dtype, by_branch(shape))

    def shared_weight(index):
        stacked = shared_conv.reshape(-1, channels)
        block = 3 * channels
        return (stacked, pl.BlockSpec((block, channels), lambda step: (3 * index + step, 0)))

    def task_weight():
        block = 3 * channels
        return (task_conv, pl.BlockSpec((1, block, channels), lambda t, step: (t, step, 0)))

    def pairs(totals):
        return totals.reshape(tasks, 2, channels)

    def triple(gains):
        return gains.reshape(tasks, 1, channels)

    three = pltpu.VMEM((slots, tall, breadth, 3 * channels), BF16)
    flat = pltpu.VMEM((slots * part, channels), F32)
    flat_tall = pltpu.VMEM((slots * tall * breadth, channels), F32)
    square = pltpu.VMEM(map_shape, F32)

    count_rows = lax.axis_size("rows")
    image_above = lax.ppermute(
        images[:, rows - 1], "rows", [(i, i + 1) for i in range(count_rows - 1)]
    )
    image_below = lax.ppermute(images[:, 0], "rows", [(i + 1, i) for i in range(count_rows - 1)])
    first_out, first_stats, first_edges = call(
        "first_conv",
        first_kernel,
        (3,),
        [scalars[0], whole(images), whole(image_above), whole(image_below), shared_weight(0)],
        [out(map_shape, F32), out(pair_shape, F32), out(edge_shape, F32)],
        [three],
        conv_flops,
    )
    first_above, first_below = edges_swapped(first_edges)
    first_totals = gathered_sum(first_stats)

    second_out, second_stats, second_edges, hidden = call(
        "second_conv",
        second_kernel,
        (3,),
        scalars
        + [
            whole(a)
            for a in (
                first_out, first_above, first_below, first_totals, shared_gain[0:1], shared_shift[0:1]
            )
        ]
        + [shared_weight(1)],
        [
            out(map_shape, F32),
            out(pair_shape, F32),
            out(edge_shape, F32),
            out(map_shape, BF16),
        ],
        [three],
        conv_flops,
    )
    second_above, second_below = edges_swapped(second_edges)
    second_totals = gathered_sum(second_stats)

    shared, down_stats = call(
        "lower",
        lower_kernel,
        (tasks,),
        scalars
        + [
            whole(a)
            for a in (
                second_out, second_above, second_below, second_totals, shared_gain[1:2], shared_shift[1:2]
            )
        ]
        + [branch(task_down)],
        [out(tall_shape, BF16), out_branch(pair_shape, F32)],
        [flat],
        3 * thin_flops,
    )
    down_totals = exchange_sum(down_stats.reshape(2 * tasks, channels))

    squeezed, up_stats = call(
        "raise",
        raise_kernel,
        (tasks,),
        scalars
        + [whole(shared), branch(task_down), branch(task_up), branch(pairs(down_totals))]
        + [branch(triple(down_gain)), branch(triple(down_shift))],
        [out_branch(tall_shape, BF16), out_branch(pair_shape, F32)],
        [flat_tall, flat],
        6 * thin_flops,
    )
    up_totals = exchange_sum(up_stats.reshape(2 * tasks, channels))

    conv_out, conv_stats, conv_edges, gated = call(
        "task_conv",
        task_kernel,
        (tasks, 3),
        scalars
        + [branch(squeezed), branch(task_up), whole(shared), branch(pairs(up_totals))]
        + [branch(triple(up_gain)), branch(triple(up_shift)), task_weight()],
        [
            out_branch(map_shape, F32),
            out_branch(pair_shape, F32),
            out_branch(edge_shape, F32),
            out_branch(map_shape, BF16),
        ],
        [flat_tall, three],
        tasks * conv_flops,
    )
    conv_above, conv_below = edges_swapped(jnp.moveaxis(conv_edges, 1, 0))
    conv_totals = exchange_sum(conv_stats.reshape(2 * tasks, channels))

    maps, conv_grad, conv_back_stats, conv_grad_edges = call(
        "pool",
        pool_kernel,
        (tasks,),
        scalars
        + [branch(conv_out), branch(cotangent), branch(pairs(conv_totals))]
        + [branch(triple(conv_gain)), branch(triple(conv_shift))],
        [
            out_branch((slots, rows // 2, breadth // 2, channels), BF16),
            out_branch(map_shape, F32),
            out_branch(pair_shape, F32),
            out_branch(edge_shape, F32),
        ],
        [pltpu.VMEM((channels // 128, breadth, 128), F32)] * 2,
        thin_flops,
    )
    conv_grad_above, conv_grad_below = edges_swapped(jnp.moveaxis(conv_grad_edges, 1, 0))
    conv_back = exchange_sum(conv_back_stats.reshape(2 * tasks, channels))

    conv_halves, up_grad_in, shared_grad, up_back_stats = call(
        "gate_back",
        gate_back_kernel,
        (tasks, 3),
        scalars
        + [
            branch(a)
            for a in (
                conv_grad, conv_grad_above, conv_grad_below, conv_out, conv_above, conv_below,
                pairs(conv_totals), pairs(conv_back), triple(conv_gain),
            )
        ]
        + [task_weight(), branch(squeezed), branch(task_up), whole(shared)]
        + [branch(pairs(up_totals)), branch(triple(up_gain)), branch(triple(up_shift))],
        [
            out_branch(half_shape, BF16),
            out_branch(map_shape, F32),
            out(map_shape, F32),
            out_branch(pair_shape, F32),
        ],
        [three, square, flat],
        tasks * conv_flops,
    )
    up_back = exchange_sum(up_back_stats.reshape(2 * tasks, channels))

    raised_grad, down_grad_in, down_back_stats = call(
        "raise_back",
        raise_back_kernel,
        (tasks,),
        scalars
        + [branch(up_grad_in), branch(squeezed), branch(task_up), whole(shared), branch(task_down)]
        + [
            branch(a)
            for a in (
                pairs(up_totals), pairs(up_back), triple(up_gain), pairs(down_totals), triple(down_gain),
                triple(down_shift),
            )
        ],
        [
            out_branch(map_shape, BF16),
            out_branch(map_shape, F32),
            out_branch(pair_shape, F32),
        ],
        [flat, flat],
        9 * thin_flops,
    )
    down_back = exchange_sum(down_back_stats.reshape(2 * tasks, channels))

    lowered_grad, second_grad, second_back_stats, second_grad_edges = call(
        "lower_back",
        lower_back_kernel,
        (tasks,),
        scalars
        + [branch(down_grad_in), whole(shared), branch(task_down)]
        + [branch(pairs(down_totals)), branch(pairs(down_back)), branch(triple(down_gain))]
        + [whole(a) for a in (shared_grad, second_out, second_totals)]
        + [whole(shared_gain[1:2]), whole(shared_shift[1:2])],
        [
            out_branch(map_shape, BF16),
            out(map_shape, F32),
            out(pair_shape, F32),
            out(edge_shape, F32),
        ],
        [flat, flat],
        6 * thin_flops,
    )
    second_grad_above, second_grad_below = edges_swapped(second_grad_edges)
    second_back = gathered_sum(second_back_stats)

    second_halves, first_grad, first_back_stats, first_grad_edges = call(
        "hidden_back",
        hidden_back_kernel,
        (3,),
        scalars
        + [
            whole(a)
            for a in (
                second_grad, second_grad_above, second_grad_below, second_out, second_above, second_below,
                second_totals, second_back, shared_gain[1:2],
            )
        ]
        + [shared_weight(1)]
        + [whole(a) for a in (first_out, first_totals, shared_gain[0:1], shared_shift[0:1])],
        [
            out(half_shape, BF16),
            out(map_shape, F32),
            out(pair_shape, F32),
            out(edge_shape, F32),
        ],
        [three, square],
        conv_flops,
    )
    first_grad_above, first_grad_below = edges_swapped(first_grad_edges)
    first_back = gathered_sum(first_back_stats)

    (first_halves,) = call(
        "first_grad",
        first_grad_kernel,
        (1,),
        scalars
        + [
            whole(a)
            for a in (
                first_grad, first_grad_above, first_grad_below, first_out, first_above, first_below,
                first_totals, first_back, shared_gain[0:1],
            )
        ],
        [out(half_shape, BF16)],
        [],
        0,
    )

    (input_grad,) = call(
        "input_back",
        input_back_kernel,
        (3,),
        [scalars[0], whole(first_halves), shared_weight(0)],
        [out(map_shape, F32)],
        [three],
        conv_flops,
    )

    core = core_bit()

    def turned(values):
        lead = values.shape[:-3]
        return jnp.swapaxes(values.reshape(lead + (part, values.shape[-1])), -1, -2)

    def wide_grad(source, source_other, halves):
        other = swapped(lax.dynamic_index_in_dim(halves, 1 - core, 0, keepdims=False), 1)
        wide = half_shape[1:]
        return call(
            "weight_grad",
            weight_grad_kernel,
            (3,),
            [
                (core.reshape(1), None),
                whole_p(source),
                whole_p(source_other),
                (halves, pl.BlockSpec((1,) + wide, lambda step, c: (c[0], 0, 0, 0, 0))),
                whole_p(other),
            ],
            [((9 * channels, channels // 2), BF16, pl.BlockSpec((3 * channels, channels // 2), lambda step, c: (step, 0)))],
            [pltpu.VMEM((2 * slots, tall, breadth, 3 * channels // 2), BF16)],
            conv_flops,
            prefetch=1,
        )[0]

    def whole_p(a):
        return (a, fixed(a.shape))

    def thin_grads(left, right):
        return call(
            "thin_grad",
            thin_grad_kernel,
            (tasks,),
            [branch(left), branch(right)],
            [out_branch((channels, channels), BF16)],
            [],
            3 * thin_flops,
        )[0]

    inside = jnp.arange(breadth)[None, None, :] < limits.reshape(slots, tall)[:, 1:-1, None]
    masked = jnp.where(inside[..., None], images, jnp.zeros_like(images))
    masked_turned = turned(masked)
    hidden_turned = turned(hidden)
    gated_turned = turned(gated)
    masked_other = swapped(masked_turned, 1)
    hidden_other = swapped(hidden_turned, 1)
    gated_other = swapped(gated_turned, 1)

    task_parts = [
        scattered_sum(
            wide_grad(gated_turned[t], gated_other[t], conv_halves[t])[None], False, t % 2 == 1
        )
        for t in range(tasks)
    ]
    down_grads = thin_grads(
        jnp.broadcast_to(turned(shared[:, 1:-1])[None], (tasks, slots, channels, part)),
        lowered_grad.reshape(tasks, slots, part, channels),
    )
    up_grads = thin_grads(
        turned(raised_grad), squeezed[:, :, 1:-1].reshape(tasks, slots, part, channels)
    )
    thin_parts = scattered_sum(jnp.concatenate([down_grads, up_grads]), True)
    second_part = scattered_sum(wide_grad(hidden_turned, hidden_other, second_halves)[None], False, True)
    first_part = scattered_sum(wide_grad(masked_turned, masked_other, first_halves)[None], False)
    wide_sums = rejoined(jnp.concatenate([first_part, second_part] + task_parts), False)
    thin_sums = rejoined(thin_parts, True)

    return (
        maps,
        input_grad,
        wide_sums[:2],
        wide_sums[2:],
        thin_sums[:tasks],
        thin_sums[tasks:].transpose(0, 2, 1),
        jnp.stack([first_back[1], second_back[1]]),
        jnp.stack([first_back[0], second_back[0]]),
        down_back[1::2],
        down_back[0::2],
        up_back[1::2],
        up_back[0::2],
        conv_back[1::2],
        conv_back[0::2],
    )


def solution(mesh):
    placed = (P("dp", "rows", None, None),) + (P(),) * 13 + (P(None, "dp", "rows", None, None),)
    return jax.shard_map(
        local,
        mesh=mesh,
        in_specs=placed,
        out_specs=(
            P(None, "dp", "rows", None, None),
            P("dp", "rows", None, None),
            P(None, "dp", None),
            P(None, "dp", None),
            P(None, "dp", None),
            P(None, None, "dp"),
        )
        + (P(),) * 8,
        check_vma=False,
    )
```

```python
import functools

import jax
import jax.numpy as jnp
from jax import lax
from jax.experimental import pallas as pl
from jax.experimental.pallas import tpu as pltpu
from jax.sharding import PartitionSpec as P

H_BIG = 36
W_BIG = 48
H_SMALL = 18
W_SMALL = 24
EPSILON = 1e-05
AXES = ("dp", "rows")
F32 = jnp.float32
BF16 = jnp.bfloat16
MIB = 1024 * 1024
SUMS = 8


def places():
    return lax.axis_size("dp") * lax.axis_size("rows")


def swapped(values, flip):
    return lax.ppermute(values, AXES, [(i, i ^ flip) for i in range(places())])


def swapped_far(values):
    count = lax.axis_size("rows")
    pairs = [(i, i + 1) for i in range(1, count - 1, 2)]
    return lax.ppermute(values, "rows", pairs + [(j, i) for i, j in pairs])


def exchange_sum(values, got):
    bits = places().bit_length() - 1
    assert places() == 1 << bits
    values = values + got
    place = 1
    while place < bits:
        low = 1 << place
        if place + 1 < bits:
            high = low * 2
            values = (values + swapped(values, low)) + (
                swapped(values, high) + swapped(values, high + low)
            )
            place += 2
        else:
            values = values + swapped(values, low)
            place += 1
    return values


def norm_totals(packed, far=None):
    got = swapped(packed, 1)
    edges = packed.shape[0] - SUMS
    totals = exchange_sum(packed[edges:], got[edges:])
    if far is None:
        return totals
    return totals, got, swapped_far(far)


def dot(left, right):
    return jnp.dot(left, right, preferred_element_type=F32)


def dot_turned(left, right):
    return lax.dot_general(left, right, (((1,), (1,)), ((), ())), preferred_element_type=F32)


def dot_over_rows(left, right):
    return lax.dot_general(left, right, (((0,), (0,)), ((), ())), preferred_element_type=F32)


class Frame:
    def __init__(self, info, slots, rows, breadth, channels):
        self.info, self.slots, self.rows = info, slots, rows
        self.breadth, self.channels = breadth, channels
        self.tall = rows + 2
        odd = self.bit(0) == 1
        self.near_rim = jnp.where(odd, 0, rows + 1)
        self.far_rim = rows + 1 - self.near_rim
        self.near_row = jnp.where(odd, 0, rows - 1)
        self.far_row = rows - 1 - self.near_row

    def bit(self, index):
        return self.info[self.slots * self.tall + index]

    def inside(self, slot, tall_row):
        shape = (self.breadth, self.channels)
        limit = self.info[slot * self.tall + tall_row]
        return lax.broadcasted_iota(jnp.int32, shape, 0) < limit

    def each(self, body):
        def step(row, carry):
            for slot in range(self.slots):
                body(slot, row)
            return carry

        lax.fori_loop(0, self.rows, step, 0)

    def summed(self, body, rows=None):
        def step(row, carry):
            one, two = carry
            for slot in range(self.slots):
                first, second = body(slot, row)
                one, two = one + fold(first), two + fold(second)
            return one, two

        zero = jnp.zeros((8, self.channels), F32)
        one, two = lax.fori_loop(0, rows or self.rows, step, (zero, zero))
        return jnp.sum(one, axis=0, keepdims=True), jnp.sum(two, axis=0, keepdims=True)

    def rims(self, sources, body, group=0):
        for slot in range(self.slots):
            index = group * self.slots + slot
            start = index * self.breadth
            if not isinstance(start, int):
                start = pl.multiple_of(start, 8)
            body(slot, self.near_rim, *[near[pl.ds(start, self.breadth), :] for near, _ in sources])
            body(slot, self.far_rim, *[far[index].astype(F32) for _, far in sources])

    def pack(self, packed, far, rows_of, sums, group=0):
        edges = packed.shape[0] - SUMS

        @pl.when(jnp.equal(group, 0))
        def _():
            packed[edges:, :] = jnp.zeros((SUMS, self.channels), F32)

        packed[pl.ds(edges + 2 * group, 1), :] = sums[0]
        packed[pl.ds(edges + 2 * group + 1, 1), :] = sums[1]
        if far is None:
            return
        for slot in range(self.slots):
            index = group * self.slots + slot
            start = index * self.breadth
            if not isinstance(start, int):
                start = pl.multiple_of(start, 8)
            packed[pl.ds(start, self.breadth), :] = rows_of(slot, self.near_row)
            far[index] = rows_of(slot, self.far_row).astype(far.dtype)

    def pixels(self, slot, row, rows=None):
        start = (slot * (rows or self.rows) + row) * self.breadth
        return pl.ds(pl.multiple_of(start, 8), self.breadth)

    def span(self, slot, rows=None):
        part = (rows or self.rows) * self.breadth
        return slice(slot * part, (slot + 1) * part)


def moments(totals, member, count):
    average = totals[pl.ds(2 * member, 1), :] / count
    variance = totals[pl.ds(2 * member + 1, 1), :] / count - average * average
    return average, lax.rsqrt(variance + EPSILON)


def line(ref, member):
    return ref[pl.ds(member, 1), :]


def sigmoid(values):
    return 1.0 / (1.0 + jnp.exp(-values))


def silu_slope(values):
    logistic = sigmoid(values)
    return logistic * (1.0 + values * (1.0 - logistic))


def fold(values):
    return jnp.sum(values.reshape(-1, 8, values.shape[-1]), axis=0)


def put_three(ref, slot, row, values, flipped):
    breadth, channels = values.shape
    col = lax.broadcasted_iota(jnp.int32, values.shape, 0)
    before = jnp.where(col == 0, 0.0, pltpu.roll(values, 1, 0))
    after = jnp.where(col == breadth - 1, 0.0, pltpu.roll(values, breadth - 1, 0))
    if flipped:
        before, after = after, before
    ref[slot, row, :, 0:channels] = before.astype(BF16)
    ref[slot, row, :, channels : 2 * channels] = values.astype(BF16)
    ref[slot, row, :, 2 * channels :] = after.astype(BF16)


def weight_copies(source, target, arrived, lead=()):
    third = target.shape[-2] // 3
    return [
        pltpu.make_async_copy(
            source.at[lead + (pl.ds(part * third, third),)],
            target.at[pl.ds(part * third, third)],
            arrived.at[part],
        )
        for part in range(3)
    ]


def forward_conv(three, weight, sums, lead=()):
    slots, rows, breadth, channels = sums.shape[-4:]
    third = weight.shape[0] // 3
    for slot in range(slots):
        total = None
        for step in range(3):
            window = three[slot, step : step + rows].reshape(rows * breadth, third)
            one = dot(window, weight[step * third : (step + 1) * third, :])
            total = one if total is None else total + one
        sums[lead + (slot,)] = total.reshape(rows, breadth, channels)


def backward_conv(three, weight, sums):
    slots, rows, breadth, channels = sums.shape[-4:]
    wide = three.shape[-1] // 3
    for slot in range(slots):
        total = None
        for step in range(3):
            window = three[slot, 2 - step : 2 - step + rows].reshape(rows * breadth, 3 * wide)
            for tap in range(3):
                start = (3 * step + tap) * channels
                one = dot_turned(
                    window[:, tap * wide : (tap + 1) * wide], weight[start : start + channels, :]
                )
                total = one if total is None else total + one
        sums[slot] = total.reshape(rows, breadth, channels)


def conv_sums(frame, sums, lead, packed, far, group=0):
    def body(slot, row):
        values = sums[lead + (slot, row)]
        kept = jnp.where(frame.inside(slot, row + 1), values, 0.0)
        return kept, kept * values

    result = frame.summed(body)
    frame.pack(packed, far, lambda slot, row: sums[lead + (slot, row)], result, group)


def plain_sums(frame, source):
    def body(slot, row):
        values = source[frame.pixels(slot, row), :]
        return values, values * values

    return frame.summed(body)


def activation(values, inside, average, inverse, gain, shift):
    normed = gain * ((values - average) * inverse) + shift
    return jnp.where(inside, normed * sigmoid(normed), 0.0)


class NormBack:
    def __init__(self, totals, back, gain, member, count):
        self.average, self.inverse = moments(totals, member, count)
        self.slope = gain * self.inverse
        self.level = self.slope * back[pl.ds(2 * member, 1), :] / count
        self.along = self.slope * back[pl.ds(2 * member + 1, 1), :] / count

    def __call__(self, grad, values, inside):
        centred = (values - self.average) * self.inverse
        return self.slope * grad - jnp.where(inside, self.level + centred * self.along, 0.0)


def first_kernel(
    info, images, above, below, weight, sums, packed, far, masked, three, held, arrived
):
    slots, rows, breadth, channels = images.shape
    frame = Frame(info, slots, rows, breadth, channels)
    copies = weight_copies(weight, held, arrived, (0,))
    for copy in copies:
        copy.start()

    def put(slot, row, values):
        kept = jnp.where(frame.inside(slot, row), values.astype(F32), 0.0)
        put_three(three, slot, row, kept, False)
        return kept

    def own(slot, row):
        masked[slot, row] = put(slot, row + 1, images[slot, row]).astype(BF16)

    frame.each(own)
    for slot in range(slots):
        put(slot, 0, above[slot])
        put(slot, rows + 1, below[slot])
    for copy in copies:
        copy.wait()
    forward_conv(three, held, sums)
    conv_sums(frame, sums, (), packed, far)


def second_kernel(
    info, count, source, near, outer, totals, gain, shift, weight, sums, packed, far, hidden, three, held, arrived
):
    slots, rows, breadth, channels = source.shape
    frame = Frame(info, slots, rows, breadth, channels)
    copies = weight_copies(weight, held, arrived, (1,))
    for copy in copies:
        copy.start()
    average, inverse = moments(totals, 0, count[0])

    def act(slot, row, values):
        inside = frame.inside(slot, row)
        result = activation(values, inside, average, inverse, line(gain, 0), line(shift, 0))
        put_three(three, slot, row, result, False)
        return result

    def own(slot, row):
        hidden[slot, row] = act(slot, row + 1, source[slot, row]).astype(BF16)

    frame.each(own)
    frame.rims([(near, outer)], act)
    for copy in copies:
        copy.wait()
    forward_conv(three, held, sums)
    conv_sums(frame, sums, (), packed, far)


def lower_kernel(
    info, count, source, near, outer, totals, gain, shift, down, shared, packed, lowered
):
    branch = pl.program_id(0)
    slots, rows, breadth, channels = source.shape
    frame = Frame(info, slots, rows, breadth, channels)

    @pl.when(branch == 0)
    def _():
        average, inverse = moments(totals, 0, count[0])

        def act(slot, row, values):
            inside = frame.inside(slot, row)
            result = activation(values, inside, average, inverse, line(gain, 1), line(shift, 1))
            shared[slot, row] = result.astype(BF16)

        frame.each(lambda slot, row: act(slot, row + 1, source[slot, row]))
        frame.rims([(near, outer)], act)

    for slot in range(slots):
        lowered[frame.span(slot), :] = dot(
            shared[slot, 1 : rows + 1].reshape(rows * breadth, channels), down[0]
        )
    frame.pack(packed, None, None, plain_sums(frame, lowered), branch)


def raise_kernel(
    info, count, shared, down, up, totals, gain, shift, squeezed, packed, wide, raised
):
    branch = pl.program_id(0)
    slots, tall, breadth, channels = shared.shape
    rows = tall - 2
    frame = Frame(info, slots, rows, breadth, channels)
    wide[...] = dot(shared[...].reshape(slots * tall * breadth, channels), down[0])
    average, inverse = moments(totals, branch, count[0])

    def act(row, carry):
        for slot in range(slots):
            values = wide[frame.pixels(slot, row, tall), :]
            result = activation(
                values, frame.inside(slot, row), average, inverse, line(gain, branch), line(shift, branch)
            )
            squeezed[0, slot, row] = result.astype(BF16)
        return carry

    lax.fori_loop(0, tall, act, 0)
    for slot in range(slots):
        raised[frame.span(slot), :] = dot(
            squeezed[0, slot, 1 : rows + 1].reshape(rows * breadth, -1), up[0]
        )
    frame.pack(packed, None, None, plain_sums(frame, raised), branch)


def task_weight(branch, weight, held, arrived):
    def copies(which):
        buffer = which % 2
        return weight_copies(weight, held.at[buffer], arrived.at[buffer], (which,))

    @pl.when(branch == 0)
    def _():
        for copy in copies(branch):
            copy.start()

    def ready():
        for copy in copies(branch):
            copy.wait()

        @pl.when(branch + 1 < pl.num_programs(0))
        def _():
            for copy in copies(branch + 1):
                copy.start()

    return ready


def task_kernel(
    info, count, squeezed, up, shared, totals, gain, shift, weight, sums, packed, far, gated,
    wide, three, held, arrived,
):
    branch = pl.program_id(0)
    slots, tall, breadth, channels = shared.shape
    rows = tall - 2
    frame = Frame(info, slots, rows, breadth, channels)
    ready = task_weight(branch, weight, held, arrived)
    wide[...] = dot(squeezed[0].reshape(slots * tall * breadth, -1), up[0])
    average, inverse = moments(totals, branch, count[0])

    def gate(slot, row):
        values = wide[frame.pixels(slot, row, tall), :]
        normed = line(gain, branch) * ((values - average) * inverse) + line(shift, branch)
        result = sigmoid(normed) * shared[slot, row].astype(F32)
        put_three(three, slot, row, result, False)
        return result

    def own(slot, row):
        gated[0, slot, row] = gate(slot, row + 1).astype(BF16)

    frame.each(own)
    for slot in range(slots):
        gate(slot, 0)
        gate(slot, rows + 1)
    ready()
    forward_conv(three, held.at[branch % 2], sums, (0,))
    conv_sums(frame, sums, (0,), packed, far, branch)


def pool_kernel(
    info, count, source, cotangent, totals, gain, shift, maps, slope, packed, far, spread, pairs
):
    branch = pl.program_id(0)
    slots, rows, breadth, channels = source.shape[1:]
    frame = Frame(info, slots, rows, breadth, channels)
    average, inverse = moments(totals, branch, count[0])
    half = breadth // 2
    groups = channels // 128

    def body(slot, pooled):
        block = cotangent[0, slot, pooled].astype(F32) * 0.25
        for group in range(groups):
            lanes = block[:, group * 128 : (group + 1) * 128]
            spread[slot, group, pl.ds(0, half, stride=2), :] = lanes
            spread[slot, group, pl.ds(1, half, stride=2), :] = lanes
        wide = jnp.concatenate([spread[slot, group] for group in range(groups)], axis=1)
        one = two = total = None
        for parity in range(2):
            row = 2 * pooled + parity
            inside = frame.inside(slot, row + 1)
            centred = (source[0, slot, row] - average) * inverse
            normed = line(gain, branch) * centred + line(shift, branch)
            logistic = sigmoid(normed)
            active = jnp.where(inside, normed * logistic, 0.0)
            grad = wide * (logistic * (1.0 + normed * (1.0 - logistic)))
            grad = jnp.where(inside, grad, 0.0)
            slope[0, slot, row] = grad
            along = grad * centred
            if parity == 0:
                one, two, total = grad, along, active
            else:
                one, two, total = one + grad, two + along, total + active
        for group in range(groups):
            lanes = slice(group * 128, (group + 1) * 128)
            pairs[slot, group] = total[:, lanes]
            even = pairs[slot, group, pl.ds(0, half, stride=2), :]
            odd = pairs[slot, group, pl.ds(1, half, stride=2), :]
            maps[0, slot, pooled, :, lanes] = ((even + odd) * 0.25).astype(BF16)
        return one, two

    sums = frame.summed(body, rows // 2)
    frame.pack(packed, far, lambda slot, row: slope[0, slot, row], sums, branch)


def fill_back(
    frame, count, grads, grad_near, grad_far, source, near, outer, totals, back, gain, three, kept, sent, lead, member
):
    norm = NormBack(totals, back, gain, member, count)
    odd = frame.bit(0) == 1
    half = frame.channels // 2

    def put(slot, row, grad, values):
        result = norm(grad, values, frame.inside(slot, row))
        if three is not None:
            put_three(three, slot, row, result, True)
        low, high = result[:, :half], result[:, half:]
        kept[lead + (slot, row)] = jnp.where(odd, high, low).astype(BF16)
        sent[lead + (slot, row)] = jnp.where(odd, low, high).astype(BF16)

    def own(slot, row):
        put(slot, row + 1, grads[lead + (slot, row)], source[lead + (slot, row)])

    frame.each(own)
    frame.rims([(grad_near, grad_far), (near, outer)], put, member if lead else 0)


def conv_grad_kernel(
    info, count, grads, grad_near, grad_far, source, near, outer, totals, back, gain, kept, sent
):
    branch = pl.program_id(0)
    frame = Frame(info, *source.shape[1:])
    fill_back(
        frame, count[0], grads, grad_near, grad_far, source, near, outer,
        totals, back, line(gain, branch), None, kept, sent, (0,), branch,
    )


def fill_halves(frame, kept, sent, three, lead=()):
    odd = frame.bit(0) == 1

    def put(row, carry):
        for slot in range(frame.slots):
            mine = kept[lead + (slot, row)].astype(F32)
            other = sent[lead + (slot, row)].astype(F32)
            low, high = jnp.where(odd, other, mine), jnp.where(odd, mine, other)
            put_three(three, slot, row, jnp.concatenate([low, high], axis=1), True)
        return carry

    lax.fori_loop(0, frame.tall, put, 0)


def gate_back_kernel(
    info, count, kept, sent, weight, squeezed, up, shared, up_totals, up_gain, up_shift,
    incoming, shared_grad, packed, three, sums, raised, held, arrived,
):
    branch = pl.program_id(0)
    slots, rows, breadth, channels = sums.shape
    frame = Frame(info, slots, rows, breadth, channels)
    ready = task_weight(branch, weight, held, arrived)
    fill_halves(frame, kept, sent, three, (0,))
    for slot in range(slots):
        raised[frame.span(slot), :] = dot(
            squeezed[0, slot, 1 : rows + 1].reshape(rows * breadth, -1), up[0]
        )
    ready()
    backward_conv(three, held.at[branch % 2], sums)
    average, inverse = moments(up_totals, branch, count[0])

    @pl.when(branch == 0)
    def _():
        shared_grad[...] = jnp.zeros(shared_grad.shape, F32)

    def body(slot, row):
        centred = (raised[frame.pixels(slot, row), :] - average) * inverse
        attention = sigmoid(line(up_gain, branch) * centred + line(up_shift, branch))
        onward = sums[slot, row] * attention
        result = onward * shared[slot, row + 1].astype(F32) * (1.0 - attention)
        incoming[0, slot, row] = result
        shared_grad[slot, row] += onward
        return result, result * centred

    frame.pack(packed, None, None, frame.summed(body), branch)


def raise_back_kernel(
    info, count, grads, squeezed, up, shared, down, up_totals, up_back, up_gain, down_totals, down_gain,
    down_shift, raised_grad, incoming, packed, wide, sums,
):
    branch = pl.program_id(0)
    slots, rows, breadth, channels = grads.shape[1:]
    part = rows * breadth
    frame = Frame(info, slots, rows, breadth, channels)
    for slot in range(slots):
        wide[frame.span(slot), :] = dot(squeezed[0, slot, 1 : rows + 1].reshape(part, -1), up[0])
    norm = NormBack(up_totals, up_back, line(up_gain, branch), branch, count[0])

    def back(slot, row):
        result = norm(
            grads[0, slot, row], wide[frame.pixels(slot, row), :], frame.inside(slot, row + 1)
        )
        raised_grad[0, slot, row] = result.astype(BF16)

    frame.each(back)
    for slot in range(slots):
        sums[frame.span(slot), :] = dot_turned(raised_grad[0, slot].reshape(part, channels), up[0])
        wide[frame.span(slot), :] = dot(
            shared[slot, 1 : rows + 1].reshape(part, channels), down[0]
        )
    average2, inverse2 = moments(down_totals, branch, count[0])

    def body(slot, row):
        centred = (wide[frame.pixels(slot, row), :] - average2) * inverse2
        normed = line(down_gain, branch) * centred + line(down_shift, branch)
        result = sums[frame.pixels(slot, row), :] * silu_slope(normed)
        result = jnp.where(frame.inside(slot, row + 1), result, 0.0)
        incoming[0, slot, row] = result
        return result, result * centred

    frame.pack(packed, None, None, frame.summed(body), branch)


def lower_back_kernel(
    info, count, grads, shared, down, down_totals, down_back, down_gain, shared_grad, source, totals, gain,
    shift, lowered_grad, incoming, packed, far, wide, sums,
):
    branch = pl.program_id(0)
    slots, rows, breadth, channels = source.shape
    part = rows * breadth
    frame = Frame(info, slots, rows, breadth, channels)
    for slot in range(slots):
        wide[frame.span(slot), :] = dot(
            shared[slot, 1 : rows + 1].reshape(part, channels), down[0]
        )
    norm = NormBack(down_totals, down_back, line(down_gain, branch), branch, count[0])

    def back(slot, row):
        result = norm(
            grads[0, slot, row], wide[frame.pixels(slot, row), :], frame.inside(slot, row + 1)
        )
        lowered_grad[0, slot, row] = result.astype(BF16)

    frame.each(back)
    for slot in range(slots):
        span = frame.span(slot)
        term = dot_turned(lowered_grad[0, slot].reshape(part, -1), down[0])

        @pl.when(branch == 0)
        def _():
            sums[span, :] = term + shared_grad[slot].reshape(part, channels)

        @pl.when(branch > 0)
        def _():
            sums[span, :] += term

    @pl.when(branch == pl.num_programs(0) - 1)
    def _():
        average2, inverse2 = moments(totals, 0, count[0])

        def body(slot, row):
            centred = (source[slot, row] - average2) * inverse2
            normed = line(gain, 1) * centred + line(shift, 1)
            result = sums[frame.pixels(slot, row), :] * silu_slope(normed)
            result = jnp.where(frame.inside(slot, row + 1), result, 0.0)
            incoming[slot, row] = result
            return result, result * centred

        result = frame.summed(body)
        frame.pack(packed, far, lambda slot, row: incoming[slot, row], result)


def hidden_back_kernel(
    info, count, kept, sent, gain, shift, weight, first, first_totals, incoming, packed, far,
    three, sums, held, arrived,
):
    slots, rows, breadth, channels = sums.shape
    frame = Frame(info, slots, rows, breadth, channels)
    copies = weight_copies(weight, held, arrived, (1,))
    for copy in copies:
        copy.start()
    fill_halves(frame, kept, sent, three)
    for copy in copies:
        copy.wait()
    backward_conv(three, held, sums)
    average, inverse = moments(first_totals, 0, count[0])

    def body(slot, row):
        centred = (first[slot, row] - average) * inverse
        normed = line(gain, 0) * centred + line(shift, 0)
        result = sums[slot, row] * silu_slope(normed)
        result = jnp.where(frame.inside(slot, row + 1), result, 0.0)
        incoming[slot, row] = result
        return result, result * centred

    result = frame.summed(body)
    frame.pack(packed, far, lambda slot, row: incoming[slot, row], result)


def one_grad_kernel(
    info, count, grads, grad_near, grad_far, source, near, outer, totals, back, gain, kept, sent, member
):
    frame = Frame(info, *source.shape)
    fill_back(
        frame, count[0], grads, grad_near, grad_far, source, near, outer,
        totals, back, line(gain, member), None, kept, sent, (), 0,
    )


def input_back_kernel(info, kept, sent, weight, out, three, held, arrived):
    slots, rows, breadth, channels = out.shape
    frame = Frame(info, slots, rows, breadth, channels)
    copies = weight_copies(weight, held, arrived, (0,))
    for copy in copies:
        copy.start()
    fill_halves(frame, kept, sent, three)
    for copy in copies:
        copy.wait()
    backward_conv(three, held, out)

    def mask(slot, row):
        out[slot, row] = jnp.where(frame.inside(slot, row + 1), out[slot, row], 0.0)

    frame.each(mask)


def weight_grad_kernel(source, source_other, grads, grads_other, out, three):
    slots, tall, breadth, channels = grads.shape
    rows = tall - 2

    def put(row, carry):
        for slot in range(slots):
            put_three(three, slot, row, grads[slot, row].astype(F32), True)
            put_three(three, slots + slot, row, grads_other[slot, row].astype(F32), True)
        return carry

    lax.fori_loop(0, tall, put, 0)
    height = source.shape[3]
    for step in range(3):
        for tap in range(3):
            total = None
            for slot in range(2 * slots):
                left = source[slot] if slot < slots else source_other[slot - slots]
                lanes = slice(tap * channels, (tap + 1) * channels)
                window = three[slot, 2 - step : 2 - step + rows, :, lanes]
                one = dot_over_rows(
                    left.reshape(rows * breadth, height), window.reshape(rows * breadth, channels)
                )
                total = one if total is None else total + one
            start = (3 * step + tap) * height
            out[start : start + height, :] = total.astype(BF16)


def split_grad_kernel(info, source, source_other, grads, grads_other, *refs, cuts, bits_at):
    three, whole = refs[-2:]
    weight_grad_kernel(source, source_other, grads, grads_other, whole, three)
    width = whole.shape[1] // len(cuts)
    first = 0
    for index, (low, count) in enumerate(cuts):
        outs = refs[first : first + (1 << count)]
        first += 1 << count
        blocks, height, _ = outs[0].shape
        lanes = slice(index * width, (index + 1) * width)
        for flip, out in enumerate(outs):
            chosen = which_block(info, bits_at, low, count, flip)
            for block in range(blocks):
                start = ((block << count) + chosen) * height
                out[block] = whole[pl.ds(pl.multiple_of(start, 16), height), lanes]


def which_block(info, bits_at, low, count, flip):
    number = 0
    for index in range(count):
        bit = info[bits_at + low + index]
        number = number + ((1 - bit if flip >> index & 1 else bit) << index)
    return number


def spread_kernel(info, *refs, low, count, lanes, members, bits_at):
    terms, outs = refs[: -(1 << count)], refs[-(1 << count) :]
    each = len(terms) // members
    for flip, out in enumerate(outs):
        chosen = which_block(info, bits_at, low, count, flip)
        blocks = out.shape[0] // members
        for member in range(members):
            group = terms[member * each : (member + 1) * each]
            for block in range(blocks):
                place = member * blocks + block
                if each == 1:
                    out[place] = group[0][block, chosen, :, lanes]
                    continue
                total = group[0][block, chosen].astype(F32)
                for term in group[1:]:
                    total = total + term[block, chosen].astype(F32)
                out[place] = total.astype(BF16)


def relay_kernel(value, same):
    pass


def settle_kernel(*refs, plan):
    out = refs[-1]
    start = 0
    for row, height, columns, count in plan:
        terms = refs[start : start + count]
        start += count
        width = terms[0].shape[1]
        for column in range(columns):
            span = slice(column * height, (column + 1) * height)
            total = terms[0][span, :].astype(F32)
            for term in terms[1:]:
                total = total + term[span, :].astype(F32)
            lanes = slice(column * width, (column + 1) * width)
            out[row : row + height, lanes] = total.astype(BF16)


def thin_grad_kernel(info, shared, lowered_grad, raised_grad, squeezed, kept, sent, bits_at):
    slots, tall, _, channels = shared.shape
    odd = info[bits_at] == 1
    half = kept.shape[-1]

    def flat(block):
        return block.reshape(-1, block.shape[-1])

    for index in range(2):
        total = None
        for slot in range(slots):
            if index == 0:
                one = dot_over_rows(flat(shared[slot, 1 : tall - 1]), flat(lowered_grad[0, slot]))
            else:
                one = dot_over_rows(
                    flat(raised_grad[0, slot]), flat(squeezed[0, slot, 1 : tall - 1])
                )
            total = one if total is None else total + one
        low, high = total[:, :half], total[:, half:]
        kept[0, index] = jnp.where(odd, high, low).astype(BF16)
        sent[0, index] = jnp.where(odd, low, high).astype(BF16)


def join_kernel(info, *refs, bits_at):
    gathered = len(refs[0].shape) == 3
    pieces, outs = (refs[:1], refs[1:]) if gathered else (refs[:4], refs[4:])
    odd = info[bits_at] == 1
    upper = info[bits_at + 1]
    half = pieces[0].shape[-1]
    start = 0
    for out in outs:
        height = out.shape[2]
        for member in range(out.shape[0]):
            span = slice(start, start + height)
            for flip in range(2):
                if gathered:
                    for core in range(2):
                        lanes = slice(core * half, (core + 1) * half)
                        out[member, flip, :, lanes] = pieces[0][2 * flip + core, span, :].astype(F32)
                    continue
                mine = pieces[2 * flip][span, :].astype(F32)
                other = pieces[2 * flip + 1][span, :].astype(F32)
                row = jnp.where(upper == flip, 0, 1)
                out[member, row, :, :half] = jnp.where(odd, other, mine)
                out[member, row, :, half:] = jnp.where(odd, mine, other)
            start += height


def outputs_kernel(first, second, down, up, conv, *outs):
    for index in range(2):
        outs[index][0:1, :] = first[1 - index : 2 - index, :]
        outs[index][1:2, :] = second[1 - index : 2 - index, :]
    for place, totals in ((2, down), (4, up), (6, conv)):
        for member in range(outs[place].shape[0]):
            for index in range(2):
                row = 2 * member + 1 - index
                outs[place + index][member : member + 1, :] = totals[row : row + 1, :]


SCALARS = pl.BlockSpec(memory_space=pltpu.SMEM)
ELSEWHERE = pl.BlockSpec(memory_space=pl.ANY)


def fixed(shape):
    zeros = (0,) * len(shape)
    return pl.BlockSpec(tuple(shape), lambda *_: zeros)


def by_branch(shape):
    zeros = (0,) * (len(shape) - 1)
    return pl.BlockSpec((1,) + tuple(shape[1:]), lambda branch, *_: (branch,) + zeros)


def call(name, body, grid, inputs, outputs, scratch, flops, room=16, after=(), aliases={}):
    total = sum(a.size * a.dtype.itemsize for a, _ in inputs)
    if after:
        count, inner = len(inputs), body

        def body(*refs):
            inner(*refs[:count], *refs[count + len(after) :])

        inputs = inputs + [(a, ELSEWHERE) for a in after]
    return pl.pallas_call(
        body,
        name=name,
        grid=grid,
        in_specs=[s for _, s in inputs],
        out_specs=[s for _, _, s in outputs],
        out_shape=[jax.ShapeDtypeStruct(s, d) for s, d, _ in outputs],
        scratch_shapes=scratch,
        compiler_params=pltpu.CompilerParams(
            vmem_limit_bytes=room * MIB, dimension_semantics=("arbitrary",) * len(grid)
        ),
        input_output_aliases=aliases,
        cost_estimate=pl.CostEstimate(flops=flops, bytes_accessed=total, transcendentals=0),
    )(*[a for a, _ in inputs])


def whole(a):
    return (a, fixed(a.shape))


def branch_of(a):
    return (a, by_branch(a.shape))


def out(shape, dtype):
    return (tuple(shape), dtype, fixed(shape))


def out_branch(shape, dtype):
    return (tuple(shape), dtype, by_branch(shape))


def in_hbm(a):
    return (pltpu.with_memory_space_constraint(a, pltpu.HBM), ELSEWHERE)


class Halving:
    def __init__(self, reducer, parts, order, rows):
        self.reducer, self.order, self.rows = reducer, list(order), rows
        self.kept, self.sent = parts[0], parts[1:]
        self.columns = 1

    def received(self):
        low, _ = self.order[0]
        return [swapped(a, (flip + 1) << low) for flip, a in enumerate(self.sent)]

    def terms(self):
        return [self.kept] + self.received()

    def step(self):
        terms = self.terms()
        self.order = self.order[1:]
        self.kept, *self.sent = self.reducer.spread([terms], self.rows, self.order)


def merged(halvings, columns=1):
    first = halvings[0]
    groups = [one.terms() for one in halvings]
    order = first.order[1:]
    parts = first.reducer.spread(groups, first.rows, order)
    result = Halving(first.reducer, parts, order, first.rows)
    result.columns = columns
    return result


class Reducer:
    def __init__(self, info, bits_at):
        self.info = info
        self.bits_at = bits_at
        self.bits = places().bit_length() - 1
        self.dp = lax.axis_size("dp")
        self.last = ()
        assert lax.axis_size("rows") == 4

    def call(self, *args, after=(), **kwargs):
        result = call(*args, after=(*after, *self.last), **kwargs)
        self.last = tuple(result[-1:])
        return result

    def relay(self, value):
        return self.call(
            "relay",
            relay_kernel,
            (1,),
            [(value, ELSEWHERE)],
            [(value.shape, value.dtype, ELSEWHERE)],
            [],
            0,
            room=4,
            aliases={0: 0},
        )[0]

    def spread(self, groups, rows, order, after=(), lanes=None):
        low, count = order[0]
        height, width = self.block_rows(rows, order), groups[0][0].shape[-1]
        lanes = lanes or (0, width)
        view = (-1, 1 << count, height, width)
        terms = [term.reshape(view) for group in groups for term in group]
        blocks = terms[0].shape[0]
        steps = 1
        if len(groups) == 1:
            steps = next(n for n in (4, 3, 2, 1) if blocks % n == 0)

        def cut(shape):
            return pl.BlockSpec(
                (shape[0] // steps,) + shape[1:], lambda step: (step,) + (0,) * (len(shape) - 1)
            )

        result = (blocks * len(groups), height, lanes[1] - lanes[0])
        return self.call(
            "spread",
            functools.partial(
                spread_kernel,
                low=low,
                count=count,
                lanes=slice(*lanes),
                members=len(groups),
                bits_at=self.bits_at,
            ),
            (steps,),
            [(self.info, SCALARS)] + [(term, cut(term.shape)) for term in terms],
            [(result, BF16, cut(result))] * (1 << count),
            [],
            0,
            room=8,
            after=after,
        )

    def settle(self, halvings):
        arrays, plan, row = [], [], 0
        for one in halvings:
            flat = (-1, one.kept.shape[-1])
            terms = [term.reshape(flat) for term in one.terms()]
            height = terms[0].shape[0] // one.columns
            plan.append((row, height, one.columns, len(terms)))
            arrays += terms
            row += height
        width = arrays[0].shape[1] * halvings[0].columns
        return self.call(
            "settle",
            functools.partial(settle_kernel, plan=plan),
            (1,),
            [whole(a) for a in arrays],
            [out((row, width), BF16)],
            [],
            0,
            room=8,
        )[0]

    def order(self, axis):
        if axis == "xy":
            return [(low, min(2, self.bits - low)) for low in range(1, self.bits, 2)]
        rest = list(range(3, self.bits))
        order = {"x": [1, 2] + rest, "y": [2, 1] + rest, "z": rest + [1, 2]}[axis]
        return [(bit, 1) for bit in order]

    def block_rows(self, rows, order):
        below = sum(count for low, count in order if low < order[0][0])
        return rows << below

    def pieces(self, piece):
        beside = swapped(piece, 2)
        return [piece, swapped(piece, 1), beside, swapped(beside, 1)]

    def join(self, pieces, members):
        width = pieces[0].shape[-1]
        shapes = []
        for count, rows in members:
            shapes.append((count, 2, rows // 2, 2 * width))
        results = self.call(
            "join",
            functools.partial(join_kernel, bits_at=self.bits_at),
            (1,),
            [(self.info, SCALARS)] + [whole(piece) for piece in pieces],
            [out(shape, F32) for shape in shapes],
            [],
            0,
            room=12,
        )
        return [r.reshape(r.shape[0], -1, r.shape[-1]) for r in results]


def local(
    images,
    size_ids,
    shared_conv,
    task_conv,
    task_down,
    task_up,
    shared_gain,
    shared_shift,
    down_gain,
    down_shift,
    up_gain,
    up_shift,
    conv_gain,
    conv_shift,
    cotangent,
):
    slots, rows, breadth, channels = images.shape
    tasks = task_conv.shape[0]
    tall = rows + 2
    part = rows * breadth
    half = channels // 2
    heights_all = jnp.where(size_ids == 0, H_BIG, H_SMALL).astype(jnp.int32)
    breadths_all = jnp.where(size_ids == 0, W_BIG, W_SMALL).astype(jnp.int32)
    count = jnp.sum(heights_all * breadths_all).astype(F32).reshape(1)
    first_slot = lax.axis_index("dp") * slots
    heights = lax.dynamic_slice_in_dim(heights_all, first_slot, slots)
    breadths = lax.dynamic_slice_in_dim(breadths_all, first_slot, slots)
    row_place = lax.axis_index("rows") * rows + jnp.arange(-1, rows + 1, dtype=jnp.int32)
    within = (row_place[None, :] >= 0) & (row_place[None, :] < heights[:, None])
    limits = jnp.where(within, breadths[:, None], 0).astype(jnp.int32).reshape(-1)
    bits_at = slots * tall
    place = lax.axis_index("dp") * lax.axis_size("rows") + lax.axis_index("rows")
    bits = (place >> jnp.arange(places().bit_length() - 1, dtype=jnp.int32)) & 1
    info = jnp.concatenate([limits, bits.astype(jnp.int32)])
    scalars = [(info, SCALARS), (count, SCALARS)]

    map_shape = (slots, rows, breadth, channels)
    tall_shape = (slots, tall, breadth, channels)
    half_shape = (slots, tall, breadth, half)
    conv_flops = 2 * slots * part * 9 * channels * channels
    thin_flops = conv_flops // 9

    def all_tasks(shape):
        return (tasks,) + tuple(shape)

    def sums_only():
        return out((SUMS, channels), F32)

    def packed(groups):
        return [
            out((groups * slots * breadth + SUMS, channels), F32),
            out((groups * slots, breadth, channels), F32 if groups == 1 else BF16),
        ]

    three = pltpu.VMEM((slots, tall, breadth, 3 * channels), BF16)
    flat = pltpu.VMEM((slots * part, channels), F32)
    flat_tall = pltpu.VMEM((slots * tall * breadth, channels), F32)
    square = pltpu.VMEM(map_shape, F32)
    one_weight = [pltpu.VMEM((9 * channels, channels), BF16), pltpu.SemaphoreType.DMA((3,))]
    two_weights = [pltpu.VMEM((2, 9 * channels, channels), BF16), pltpu.SemaphoreType.DMA((2, 3))]

    count_rows = lax.axis_size("rows")
    image_above = lax.ppermute(
        images[:, rows - 1], "rows", [(i, i + 1) for i in range(count_rows - 1)]
    )
    image_below = lax.ppermute(images[:, 0], "rows", [(i + 1, i) for i in range(count_rows - 1)])
    first_out, first_packed, first_far, masked = call(
        "first_conv",
        first_kernel,
        (1,),
        [scalars[0], whole(images), whole(image_above), whole(image_below), in_hbm(shared_conv)],
        [out(map_shape, F32)] + packed(1) + [out(map_shape, BF16)],
        [three] + one_weight,
        conv_flops,
    )
    first_totals, first_near, first_outer = norm_totals(first_packed, first_far)

    second_out, second_packed, second_far, hidden = call(
        "second_conv",
        second_kernel,
        (1,),
        scalars
        + [whole(a) for a in (first_out, first_near, first_outer, first_totals)]
        + [whole(shared_gain), whole(shared_shift), in_hbm(shared_conv)],
        [out(map_shape, F32)] + packed(1) + [out(map_shape, BF16)],
        [three] + one_weight,
        conv_flops,
    )
    second_totals, second_near, second_outer = norm_totals(second_packed, second_far)

    shared, down_packed = call(
        "lower",
        lower_kernel,
        (tasks,),
        scalars
        + [whole(a) for a in (second_out, second_near, second_outer, second_totals)]
        + [whole(shared_gain), whole(shared_shift), branch_of(task_down)],
        [out(tall_shape, BF16), sums_only()],
        [flat],
        3 * thin_flops,
    )
    down_totals = norm_totals(down_packed)

    squeezed, up_packed = call(
        "raise",
        raise_kernel,
        (tasks,),
        scalars
        + [whole(shared), branch_of(task_down), branch_of(task_up)]
        + [whole(a) for a in (down_totals, down_gain, down_shift)],
        [out_branch(all_tasks(tall_shape), BF16), sums_only()],
        [flat_tall, flat],
        6 * thin_flops,
    )
    up_totals = norm_totals(up_packed)

    conv_out, conv_packed, conv_far, gated = call(
        "task_conv",
        task_kernel,
        (tasks,),
        scalars
        + [branch_of(squeezed), branch_of(task_up)]
        + [whole(a) for a in (shared, up_totals, up_gain, up_shift)]
        + [in_hbm(task_conv)],
        [out_branch(all_tasks(map_shape), F32)]
        + packed(tasks)
        + [out_branch(all_tasks(map_shape), BF16)],
        [flat_tall, three] + two_weights,
        tasks * conv_flops,
        room=22,
    )
    conv_totals, conv_near, conv_outer = norm_totals(conv_packed, conv_far)

    maps, conv_grad, conv_back_packed, conv_grad_far = call(
        "pool",
        pool_kernel,
        (tasks,),
        scalars
        + [branch_of(conv_out), branch_of(cotangent)]
        + [whole(a) for a in (conv_totals, conv_gain, conv_shift)],
        [
            out_branch(all_tasks((slots, rows // 2, breadth // 2, channels)), BF16),
            out_branch(all_tasks(map_shape), F32),
        ]
        + packed(tasks),
        [pltpu.VMEM((slots, channels // 128, breadth, 128), F32)] * 2,
        thin_flops,
    )
    conv_back, conv_grad_near, conv_grad_outer = norm_totals(conv_back_packed, conv_grad_far)

    reducer = Reducer(info, bits_at)
    dp_count = reducer.dp
    wide_rows = 9 * channels // dp_count

    share_rows = wide_rows // 2

    def weight_whole(source, source_other, kept, sent, after=()):
        return reducer.call(
            "weight_grad",
            weight_grad_kernel,
            (1,),
            [whole(a) for a in (source, source_other, kept, swapped(sent, 1))],
            [out((9 * channels, half), BF16)],
            [pltpu.VMEM((2 * slots, tall, breadth, 3 * half), BF16)],
            conv_flops,
            after=after,
        )[0]

    def weight_sum(source, source_other, kept, sent, axes, after=()):
        orders = [reducer.order(axis) for axis in axes]
        width = half // len(orders)
        if share_rows % 16:
            total = weight_whole(source, source_other, kept, sent, after)
            parts = [
                reducer.spread([[total]], share_rows, order, (), (index * width, (index + 1) * width))
                for index, order in enumerate(orders)
            ]
        else:
            shapes = []
            for order in orders:
                height = reducer.block_rows(share_rows, order)
                shape = ((9 * channels // height) >> order[0][1], height, width)
                shapes += [shape] * (1 << order[0][1])
            results = reducer.call(
                "weight_grad",
                functools.partial(
                    split_grad_kernel, cuts=[order[0] for order in orders], bits_at=bits_at
                ),
                (1,),
                [(info, SCALARS)]
                + [whole(a) for a in (source, source_other, kept, swapped(sent, 1))],
                [out(shape, BF16) for shape in shapes],
                [
                    pltpu.VMEM((2 * slots, tall, breadth, 3 * half), BF16),
                    pltpu.VMEM((9 * channels, half), BF16),
                ],
                conv_flops,
                after=after,
            )
            parts = []
            for order in orders:
                parts.append(results[: 1 << order[0][1]])
                results = results[1 << order[0][1] :]
        return [Halving(reducer, part, order, share_rows) for part, order in zip(parts, orders)]

    masked_other, hidden_other, gated_other = (swapped(a, 1) for a in (masked, hidden, gated))

    conv_kept, conv_sent = reducer.call(
        "conv_grad",
        conv_grad_kernel,
        (tasks,),
        scalars
        + [branch_of(conv_grad), whole(conv_grad_near), whole(conv_grad_outer)]
        + [branch_of(conv_out), whole(conv_near), whole(conv_outer)]
        + [whole(a) for a in (conv_totals, conv_back, conv_gain)],
        [out_branch(all_tasks(half_shape), BF16)] * 2,
        [],
        0,
    )

    def step(*halvings):
        for one in halvings:
            one.step()

    def task_grads(t):
        return gated[t], gated_other[t], conv_kept[t], conv_sent[t]

    early = [weight_sum(*task_grads(t), ["xy"[t]])[0] for t in range(2)]
    up_grad_in, shared_grad, up_back_packed = reducer.call(
        "gate_back",
        gate_back_kernel,
        (tasks,),
        scalars
        + [branch_of(conv_kept), branch_of(conv_sent)]
        + [in_hbm(task_conv), branch_of(squeezed), branch_of(task_up)]
        + [whole(a) for a in (shared, up_totals, up_gain, up_shift)],
        [
            out_branch(all_tasks(map_shape), F32),
            out(map_shape, F32),
            sums_only(),
        ],
        [three, square, flat] + two_weights,
        tasks * conv_flops,
        room=22,
        after=[masked_other, hidden_other],
    )
    step(*early)
    up_back = norm_totals(reducer.relay(up_back_packed))
    raised_grad, down_grad_in, down_back_packed = reducer.call(
        "raise_back",
        raise_back_kernel,
        (tasks,),
        scalars
        + [branch_of(up_grad_in), branch_of(squeezed), branch_of(task_up), whole(shared)]
        + [branch_of(task_down)]
        + [
            whole(a)
            for a in (up_totals, up_back, up_gain, down_totals, down_gain, down_shift)
        ],
        [
            out_branch(all_tasks(map_shape), BF16),
            out_branch(all_tasks(map_shape), F32),
            sums_only(),
        ],
        [flat, flat],
        9 * thin_flops,
    )
    early = merged(early)
    down_back = norm_totals(reducer.relay(down_back_packed))
    late = weight_sum(*task_grads(2), "xy", after=[down_back])

    lowered_grad, second_grad, second_back_packed, second_grad_far = reducer.call(
        "lower_back",
        lower_back_kernel,
        (tasks,),
        scalars
        + [branch_of(down_grad_in), whole(shared), branch_of(task_down)]
        + [whole(a) for a in (down_totals, down_back, down_gain, shared_grad, second_out)]
        + [whole(a) for a in (second_totals, shared_gain, shared_shift)],
        [out_branch(all_tasks(map_shape), BF16), out(map_shape, F32)] + packed(1),
        [flat, flat],
        6 * thin_flops,
    )
    square_shape = (tasks, 2, channels, half)
    thin_kept, thin_sent = reducer.call(
        "thin_grad",
        functools.partial(thin_grad_kernel, bits_at=bits_at),
        (tasks,),
        [(info, SCALARS), whole(shared)]
        + [branch_of(a) for a in (lowered_grad, raised_grad, squeezed)],
        [out_branch(square_shape, BF16)] * 2,
        [],
        6 * thin_flops,
    )
    thin_got = swapped(thin_sent, 1)
    step(early, *late)
    second_back, second_grad_near, second_grad_outer = norm_totals(
        reducer.relay(second_back_packed), second_grad_far
    )

    second_kept, second_sent = reducer.call(
        "second_grad",
        functools.partial(one_grad_kernel, member=1),
        (1,),
        scalars
        + [
            whole(a)
            for a in (
                second_grad, second_grad_near, second_grad_outer, second_out, second_near, second_outer,
                second_totals, second_back, shared_gain,
            )
        ],
        [out(half_shape, BF16)] * 2,
        [],
        0,
    )
    second_sum = weight_sum(hidden, hidden_other, second_kept, second_sent, "xy")
    late = merged(late, 2)
    thin_order = reducer.order("y")
    thin_rows = channels // dp_count // 2
    thin_parts = reducer.spread([[thin_kept, thin_got]], thin_rows, thin_order)
    thin = Halving(reducer, thin_parts, thin_order, thin_rows)
    first_grad, first_back_packed, first_grad_far = reducer.call(
        "hidden_back",
        hidden_back_kernel,
        (1,),
        scalars
        + [whole(second_kept), whole(second_sent), whole(shared_gain), whole(shared_shift)]
        + [in_hbm(shared_conv), whole(first_out), whole(first_totals)],
        [out(map_shape, F32)] + packed(1),
        [three, square] + one_weight,
        conv_flops,
    )
    step(*second_sum, late)
    first_back, first_grad_near, first_grad_outer = norm_totals(
        reducer.relay(first_back_packed), first_grad_far
    )

    first_kept, first_sent = reducer.call(
        "first_grad",
        functools.partial(one_grad_kernel, member=0),
        (1,),
        scalars
        + [
            whole(a)
            for a in (
                first_grad, first_grad_near, first_grad_outer, first_out, first_near, first_outer,
                first_totals, first_back, shared_gain,
            )
        ],
        [out(half_shape, BF16)] * 2,
        [],
        0,
    )
    first_sum = weight_sum(masked, masked_other, first_kept, first_sent, ["xy"])

    task_share = reducer.settle([early, late])
    second_sum = merged(second_sum, 2)
    step(thin, *first_sum)
    step(second_sum, thin)
    (input_grad,) = reducer.call(
        "input_back",
        input_back_kernel,
        (1,),
        [scalars[0], whole(first_kept), whole(first_sent), in_hbm(shared_conv)],
        [out(map_shape, F32)],
        [three] + one_weight,
        conv_flops,
    )

    step(thin)
    shared_sums, thin_sums = reducer.join(
        reducer.pieces(reducer.settle(first_sum + [second_sum, thin])),
        [(2, wide_rows), (2 * tasks, channels // dp_count)],
    )
    (task_sums,) = reducer.join([lax.all_gather(task_share, "rows")], [(tasks, wide_rows)])

    pair_shape = (2, channels)
    many_shape = (tasks, channels)
    small = call(
        "outputs",
        outputs_kernel,
        (1,),
        [whole(a) for a in (first_back, second_back, down_back, up_back, conv_back)],
        [out(pair_shape, F32)] * 2 + [out(many_shape, F32)] * 6,
        [],
        0,
        room=4,
    )
    return (
        maps,
        input_grad,
        shared_sums,
        task_sums,
        thin_sums[0::2],
        thin_sums[1::2].transpose(0, 2, 1),
        *small,
    )


def solution(mesh):
    placed = (P("dp", "rows", None, None),) + (P(),) * 13 + (P(None, "dp", "rows", None, None),)
    return jax.shard_map(
        local,
        mesh=mesh,
        in_specs=placed,
        out_specs=(
            P(None, "dp", "rows", None, None),
            P("dp", "rows", None, None),
            P(None, "dp", None),
            P(None, "dp", None),
            P(None, "dp", None),
            P(None, None, "dp"),
        )
        + (P(),) * 8,
        check_vma=False,
    )
```

```python
import functools

import jax
import jax.numpy as jnp
from jax import lax
from jax.experimental import pallas as pl
from jax.experimental.pallas import tpu as pltpu
from jax.sharding import PartitionSpec as P

H_BIG = 36
W_BIG = 48
H_SMALL = 18
W_SMALL = 24
EPSILON = 1e-05
AXES = ("dp", "rows")
F32 = jnp.float32
BF16 = jnp.bfloat16
MIB = 1024 * 1024
SUMS = 8


def places():
    return lax.axis_size("dp") * lax.axis_size("rows")


def swapped(values, flip):
    return lax.ppermute(values, AXES, [(i, i ^ flip) for i in range(places())])


def swapped_far(values):
    count = lax.axis_size("rows")
    pairs = [(i, i + 1) for i in range(1, count - 1, 2)]
    return lax.ppermute(values, "rows", pairs + [(j, i) for i, j in pairs])


def exchange_sum(values, got):
    bits = places().bit_length() - 1
    assert places() == 1 << bits
    values = values + got
    place = 1
    while place < bits:
        low = 1 << place
        if place + 1 < bits:
            high = low * 2
            values = (values + swapped(values, low)) + (
                swapped(values, high) + swapped(values, high + low)
            )
            place += 2
        else:
            values = values + swapped(values, low)
            place += 1
    return values


def norm_totals(packed, far=None):
    got = swapped(packed, 1)
    edges = packed.shape[0] - SUMS
    totals = exchange_sum(packed[edges:], got[edges:])
    if far is None:
        return totals
    return totals, got, swapped_far(far)


def dot(left, right):
    return jnp.dot(left, right, preferred_element_type=F32)


def dot_turned(left, right):
    return lax.dot_general(left, right, (((1,), (1,)), ((), ())), preferred_element_type=F32)


def dot_over_rows(left, right):
    return lax.dot_general(left, right, (((0,), (0,)), ((), ())), preferred_element_type=F32)


class Frame:
    def __init__(self, info, slots, rows, breadth, channels):
        self.info, self.slots, self.rows = info, slots, rows
        self.breadth, self.channels = breadth, channels
        self.tall = rows + 2
        odd = self.bit(0) == 1
        self.near_rim = jnp.where(odd, 0, rows + 1)
        self.far_rim = rows + 1 - self.near_rim
        self.near_row = jnp.where(odd, 0, rows - 1)
        self.far_row = rows - 1 - self.near_row

    def bit(self, index):
        return self.info[self.slots * self.tall + index]

    def inside(self, slot, tall_row):
        shape = (self.breadth, self.channels)
        limit = self.info[slot * self.tall + tall_row]
        return lax.broadcasted_iota(jnp.int32, shape, 0) < limit

    def each(self, body):
        self.rows_of(self.rows, body)

    def rows_of(self, rows, body):
        group = 2 if rows % 2 == 0 else 1

        def step(index, carry):
            for part in range(group):
                for slot in range(self.slots):
                    body(slot, index * group + part)
            return carry

        lax.fori_loop(0, rows // group, step, 0)

    def summed(self, body, rows=None):
        rows = rows or self.rows
        group = 2 if rows % 2 == 0 else 1

        def step(index, carry):
            one, two = carry
            for part in range(group):
                for slot in range(self.slots):
                    first, second = body(slot, index * group + part)
                    one, two = one + fold(first), two + fold(second)
            return one, two

        zero = jnp.zeros((8, self.channels), F32)
        one, two = lax.fori_loop(0, rows // group, step, (zero, zero))
        return jnp.sum(one, axis=0, keepdims=True), jnp.sum(two, axis=0, keepdims=True)

    def rims(self, sources, body, group=0):
        for slot in range(self.slots):
            index = group * self.slots + slot
            start = index * self.breadth
            if not isinstance(start, int):
                start = pl.multiple_of(start, 8)
            body(slot, self.near_rim, *[near[pl.ds(start, self.breadth), :] for near, _ in sources])
            body(slot, self.far_rim, *[far[index].astype(F32) for _, far in sources])

    def pack(self, packed, far, rows_of, sums, group=0):
        edges = packed.shape[0] - SUMS

        @pl.when(jnp.equal(group, 0))
        def _():
            packed[edges:, :] = jnp.zeros((SUMS, self.channels), F32)

        packed[pl.ds(edges + 2 * group, 1), :] = sums[0]
        packed[pl.ds(edges + 2 * group + 1, 1), :] = sums[1]
        if far is None:
            return
        for slot in range(self.slots):
            index = group * self.slots + slot
            start = index * self.breadth
            if not isinstance(start, int):
                start = pl.multiple_of(start, 8)
            packed[pl.ds(start, self.breadth), :] = rows_of(slot, self.near_row)
            far[index] = rows_of(slot, self.far_row).astype(far.dtype)

    def pixels(self, slot, row, rows=None):
        start = (slot * (rows or self.rows) + row) * self.breadth
        return pl.ds(pl.multiple_of(start, 8), self.breadth)

    def span(self, slot, rows=None):
        part = (rows or self.rows) * self.breadth
        return slice(slot * part, (slot + 1) * part)


def moments(totals, member, count):
    average = totals[pl.ds(2 * member, 1), :] / count
    variance = totals[pl.ds(2 * member + 1, 1), :] / count - average * average
    return average, lax.rsqrt(variance + EPSILON)


def line(ref, member):
    return ref[pl.ds(member, 1), :]


def sigmoid(values):
    return jax.nn.sigmoid(values)


def silu_slope(values):
    logistic = sigmoid(values)
    return logistic * (1.0 + values * (1.0 - logistic))


def fold(values):
    return jnp.sum(values.reshape(-1, 8, values.shape[-1]), axis=0)


def put_three(ref, slot, row, values, flipped):
    breadth, channels = values.shape
    col = lax.broadcasted_iota(jnp.int32, values.shape, 0)
    before = jnp.where(col == 0, 0.0, pltpu.roll(values, 1, 0))
    after = jnp.where(col == breadth - 1, 0.0, pltpu.roll(values, breadth - 1, 0))
    if flipped:
        before, after = after, before
    ref[slot, row, :, 0:channels] = before.astype(BF16)
    ref[slot, row, :, channels : 2 * channels] = values.astype(BF16)
    ref[slot, row, :, 2 * channels :] = after.astype(BF16)


def weight_copies(source, target, arrived, lead=()):
    third = target.shape[-2] // 3
    return [
        pltpu.make_async_copy(
            source.at[lead + (pl.ds(part * third, third),)],
            target.at[pl.ds(part * third, third)],
            arrived.at[part],
        )
        for part in range(3)
    ]


def forward_conv(three, weight, sums, lead=()):
    slots, rows, breadth, channels = sums.shape[-4:]
    third = weight.shape[0] // 3
    for slot in range(slots):
        total = None
        for step in range(3):
            window = three[slot, step : step + rows].reshape(rows * breadth, third)
            one = dot(window, weight[step * third : (step + 1) * third, :])
            total = one if total is None else total + one
        sums[lead + (slot,)] = total.reshape(rows, breadth, channels)


def backward_conv(three, weight, sums):
    slots, rows, breadth, channels = sums.shape[-4:]
    wide = three.shape[-1] // 3
    for slot in range(slots):
        total = None
        for step in range(3):
            window = three[slot, 2 - step : 2 - step + rows].reshape(rows * breadth, 3 * wide)
            for tap in range(3):
                start = (3 * step + tap) * channels
                one = dot_turned(
                    window[:, tap * wide : (tap + 1) * wide], weight[start : start + channels, :]
                )
                total = one if total is None else total + one
        sums[slot] = total.reshape(rows, breadth, channels)


def conv_sums(frame, sums, lead, packed, far, group=0):
    def body(slot, row):
        values = sums[lead + (slot, row)]
        kept = jnp.where(frame.inside(slot, row + 1), values, 0.0)
        return kept, kept * values

    result = frame.summed(body)
    frame.pack(packed, far, lambda slot, row: sums[lead + (slot, row)], result, group)


def plain_sums(frame, source):
    def body(slot, row):
        values = source[frame.pixels(slot, row), :]
        return values, values * values

    return frame.summed(body)


def activation(values, inside, average, inverse, gain, shift):
    normed = gain * ((values - average) * inverse) + shift
    return jnp.where(inside, normed * sigmoid(normed), 0.0)


class NormBack:
    def __init__(self, totals, back, gain, member, count):
        self.average, self.inverse = moments(totals, member, count)
        self.slope = gain * self.inverse
        self.level = self.slope * back[pl.ds(2 * member, 1), :] / count
        self.along = self.slope * back[pl.ds(2 * member + 1, 1), :] / count

    def __call__(self, grad, values, inside):
        centred = (values - self.average) * self.inverse
        return self.slope * grad - jnp.where(inside, self.level + centred * self.along, 0.0)


def first_kernel(
    info, images, above, below, weight, sums, packed, far, masked, three, held, arrived
):
    slots, rows, breadth, channels = images.shape
    frame = Frame(info, slots, rows, breadth, channels)
    copies = weight_copies(weight, held, arrived, (0,))
    for copy in copies:
        copy.start()

    def put(slot, row, values):
        kept = jnp.where(frame.inside(slot, row), values.astype(F32), 0.0)
        put_three(three, slot, row, kept, False)
        return kept

    def own(slot, row):
        masked[slot, row] = put(slot, row + 1, images[slot, row]).astype(BF16)

    frame.each(own)
    for slot in range(slots):
        put(slot, 0, above[slot])
        put(slot, rows + 1, below[slot])
    for copy in copies:
        copy.wait()
    forward_conv(three, held, sums)
    conv_sums(frame, sums, (), packed, far)


def second_kernel(
    info, count, source, near, outer, totals, gain, shift, weight, sums, packed, far, hidden, three, held, arrived
):
    slots, rows, breadth, channels = source.shape
    frame = Frame(info, slots, rows, breadth, channels)
    copies = weight_copies(weight, held, arrived, (1,))
    for copy in copies:
        copy.start()
    average, inverse = moments(totals, 0, count[0])

    def act(slot, row, values):
        inside = frame.inside(slot, row)
        result = activation(values, inside, average, inverse, line(gain, 0), line(shift, 0))
        put_three(three, slot, row, result, False)
        return result

    def own(slot, row):
        hidden[slot, row] = act(slot, row + 1, source[slot, row]).astype(BF16)

    frame.each(own)
    frame.rims([(near, outer)], act)
    for copy in copies:
        copy.wait()
    forward_conv(three, held, sums)
    conv_sums(frame, sums, (), packed, far)


def lower_kernel(
    info, count, source, near, outer, totals, gain, shift, down, shared, packed, lowered
):
    branch = pl.program_id(0)
    slots, rows, breadth, channels = source.shape
    frame = Frame(info, slots, rows, breadth, channels)

    @pl.when(branch == 0)
    def _():
        average, inverse = moments(totals, 0, count[0])

        def act(slot, row, values):
            inside = frame.inside(slot, row)
            result = activation(values, inside, average, inverse, line(gain, 1), line(shift, 1))
            shared[slot, row] = result.astype(BF16)

        frame.each(lambda slot, row: act(slot, row + 1, source[slot, row]))
        frame.rims([(near, outer)], act)

    for slot in range(slots):
        lowered[frame.span(slot), :] = dot(
            shared[slot, 1 : rows + 1].reshape(rows * breadth, channels), down[0]
        )
    frame.pack(packed, None, None, plain_sums(frame, lowered), branch)


def raise_kernel(
    info, count, shared, down, up, totals, gain, shift, squeezed, packed, wide, raised
):
    branch = pl.program_id(0)
    slots, tall, breadth, channels = shared.shape
    rows = tall - 2
    frame = Frame(info, slots, rows, breadth, channels)
    wide[...] = dot(shared[...].reshape(slots * tall * breadth, channels), down[0])
    average, inverse = moments(totals, branch, count[0])

    def act(slot, row):
        values = wide[frame.pixels(slot, row, tall), :]
        result = activation(
            values, frame.inside(slot, row), average, inverse, line(gain, branch), line(shift, branch)
        )
        squeezed[0, slot, row] = result.astype(BF16)

    frame.rows_of(tall, act)
    for slot in range(slots):
        raised[frame.span(slot), :] = dot(
            squeezed[0, slot, 1 : rows + 1].reshape(rows * breadth, -1), up[0]
        )
    frame.pack(packed, None, None, plain_sums(frame, raised), branch)


def task_weight(branch, weight, held, arrived):
    def copies(which):
        buffer = which % 2
        return weight_copies(weight, held.at[buffer], arrived.at[buffer], (which,))

    @pl.when(branch == 0)
    def _():
        for copy in copies(branch):
            copy.start()

    def ready():
        for copy in copies(branch):
            copy.wait()

        @pl.when(branch + 1 < pl.num_programs(0))
        def _():
            for copy in copies(branch + 1):
                copy.start()

    return ready


def task_kernel(
    info, count, squeezed, up, shared, totals, gain, shift, weight, sums, packed, far, gated,
    wide, three, held, arrived,
):
    branch = pl.program_id(0)
    slots, tall, breadth, channels = shared.shape
    rows = tall - 2
    frame = Frame(info, slots, rows, breadth, channels)
    ready = task_weight(branch, weight, held, arrived)
    wide[...] = dot(squeezed[0].reshape(slots * tall * breadth, -1), up[0])
    average, inverse = moments(totals, branch, count[0])

    def gate(slot, row):
        values = wide[frame.pixels(slot, row, tall), :]
        normed = line(gain, branch) * ((values - average) * inverse) + line(shift, branch)
        result = sigmoid(normed) * shared[slot, row].astype(F32)
        put_three(three, slot, row, result, False)
        return result

    def own(slot, row):
        gated[0, slot, row] = gate(slot, row + 1).astype(BF16)

    frame.each(own)
    for slot in range(slots):
        gate(slot, 0)
        gate(slot, rows + 1)
    ready()
    forward_conv(three, held.at[branch % 2], sums, (0,))
    conv_sums(frame, sums, (0,), packed, far, branch)


def pool_kernel(
    info, count, source, cotangent, totals, gain, shift, maps, slope, packed, far, spread, pairs
):
    branch = pl.program_id(0)
    slots, rows, breadth, channels = source.shape[1:]
    frame = Frame(info, slots, rows, breadth, channels)
    average, inverse = moments(totals, branch, count[0])
    half = breadth // 2
    groups = channels // 128

    def body(slot, pooled):
        block = cotangent[0, slot, pooled].astype(F32) * 0.25
        for group in range(groups):
            lanes = block[:, group * 128 : (group + 1) * 128]
            spread[slot, group, pl.ds(0, half, stride=2), :] = lanes
            spread[slot, group, pl.ds(1, half, stride=2), :] = lanes
        wide = jnp.concatenate([spread[slot, group] for group in range(groups)], axis=1)
        one = two = total = None
        for parity in range(2):
            row = 2 * pooled + parity
            inside = frame.inside(slot, row + 1)
            centred = (source[0, slot, row] - average) * inverse
            normed = line(gain, branch) * centred + line(shift, branch)
            logistic = sigmoid(normed)
            active = jnp.where(inside, normed * logistic, 0.0)
            grad = wide * (logistic * (1.0 + normed * (1.0 - logistic)))
            grad = jnp.where(inside, grad, 0.0)
            slope[0, slot, row] = grad
            along = grad * centred
            if parity == 0:
                one, two, total = grad, along, active
            else:
                one, two, total = one + grad, two + along, total + active
        for group in range(groups):
            lanes = slice(group * 128, (group + 1) * 128)
            pairs[slot, group] = total[:, lanes]
            even = pairs[slot, group, pl.ds(0, half, stride=2), :]
            odd = pairs[slot, group, pl.ds(1, half, stride=2), :]
            maps[0, slot, pooled, :, lanes] = ((even + odd) * 0.25).astype(BF16)
        return one, two

    sums = frame.summed(body, rows // 2)
    frame.pack(packed, far, lambda slot, row: slope[0, slot, row], sums, branch)


def fill_back(
    frame, count, grads, grad_near, grad_far, source, near, outer, totals, back, gain, three, kept, sent, lead, member
):
    norm = NormBack(totals, back, gain, member, count)
    odd = frame.bit(0) == 1
    half = frame.channels // 2

    def put(slot, row, grad, values):
        result = norm(grad, values, frame.inside(slot, row))
        if three is not None:
            put_three(three, slot, row, result, True)
        low, high = result[:, :half], result[:, half:]
        kept[lead + (slot, row)] = jnp.where(odd, high, low).astype(BF16)
        sent[lead + (slot, row)] = jnp.where(odd, low, high).astype(BF16)

    def own(slot, row):
        put(slot, row + 1, grads[lead + (slot, row)], source[lead + (slot, row)])

    frame.each(own)
    frame.rims([(grad_near, grad_far), (near, outer)], put, member if lead else 0)


def conv_grad_kernel(
    info, count, grads, grad_near, grad_far, source, near, outer, totals, back, gain, kept, sent
):
    branch = pl.program_id(0)
    frame = Frame(info, *source.shape[1:])
    fill_back(
        frame, count[0], grads, grad_near, grad_far, source, near, outer,
        totals, back, line(gain, branch), None, kept, sent, (0,), branch,
    )


def fill_halves(frame, kept, sent, three, lead=()):
    odd = frame.bit(0) == 1

    def put(slot, row):
        mine = kept[lead + (slot, row)].astype(F32)
        other = sent[lead + (slot, row)].astype(F32)
        low, high = jnp.where(odd, other, mine), jnp.where(odd, mine, other)
        put_three(three, slot, row, jnp.concatenate([low, high], axis=1), True)

    frame.rows_of(frame.tall, put)


def gate_back_kernel(
    info, count, kept, sent, weight, squeezed, up, shared, up_totals, up_gain, up_shift,
    incoming, shared_grad, packed, three, sums, raised, held, arrived,
):
    branch = pl.program_id(0)
    slots, rows, breadth, channels = sums.shape
    frame = Frame(info, slots, rows, breadth, channels)
    ready = task_weight(branch, weight, held, arrived)
    fill_halves(frame, kept, sent, three, (0,))
    for slot in range(slots):
        raised[frame.span(slot), :] = dot(
            squeezed[0, slot, 1 : rows + 1].reshape(rows * breadth, -1), up[0]
        )
    ready()
    backward_conv(three, held.at[branch % 2], sums)
    average, inverse = moments(up_totals, branch, count[0])

    @pl.when(branch == 0)
    def _():
        shared_grad[...] = jnp.zeros(shared_grad.shape, F32)

    def body(slot, row):
        centred = (raised[frame.pixels(slot, row), :] - average) * inverse
        attention = sigmoid(line(up_gain, branch) * centred + line(up_shift, branch))
        onward = sums[slot, row] * attention
        result = onward * shared[slot, row + 1].astype(F32) * (1.0 - attention)
        incoming[0, slot, row] = result
        shared_grad[slot, row] += onward
        return result, result * centred

    frame.pack(packed, None, None, frame.summed(body), branch)


def raise_back_kernel(
    info, count, grads, squeezed, up, shared, down, up_totals, up_back, up_gain, down_totals, down_gain,
    down_shift, raised_grad, incoming, packed, wide, sums,
):
    branch = pl.program_id(0)
    slots, rows, breadth, channels = grads.shape[1:]
    part = rows * breadth
    frame = Frame(info, slots, rows, breadth, channels)
    for slot in range(slots):
        wide[frame.span(slot), :] = dot(squeezed[0, slot, 1 : rows + 1].reshape(part, -1), up[0])
    norm = NormBack(up_totals, up_back, line(up_gain, branch), branch, count[0])

    def back(slot, row):
        result = norm(
            grads[0, slot, row], wide[frame.pixels(slot, row), :], frame.inside(slot, row + 1)
        )
        raised_grad[0, slot, row] = result.astype(BF16)

    frame.each(back)
    for slot in range(slots):
        sums[frame.span(slot), :] = dot_turned(raised_grad[0, slot].reshape(part, channels), up[0])
        wide[frame.span(slot), :] = dot(
            shared[slot, 1 : rows + 1].reshape(part, channels), down[0]
        )
    average2, inverse2 = moments(down_totals, branch, count[0])

    def body(slot, row):
        centred = (wide[frame.pixels(slot, row), :] - average2) * inverse2
        normed = line(down_gain, branch) * centred + line(down_shift, branch)
        result = sums[frame.pixels(slot, row), :] * silu_slope(normed)
        result = jnp.where(frame.inside(slot, row + 1), result, 0.0)
        incoming[0, slot, row] = result
        return result, result * centred

    frame.pack(packed, None, None, frame.summed(body), branch)


def lower_back_kernel(
    info, count, grads, shared, down, down_totals, down_back, down_gain, shared_grad, source, totals, gain,
    shift, lowered_grad, incoming, packed, far, wide, sums,
):
    branch = pl.program_id(0)
    slots, rows, breadth, channels = source.shape
    part = rows * breadth
    frame = Frame(info, slots, rows, breadth, channels)
    for slot in range(slots):
        wide[frame.span(slot), :] = dot(
            shared[slot, 1 : rows + 1].reshape(part, channels), down[0]
        )
    norm = NormBack(down_totals, down_back, line(down_gain, branch), branch, count[0])

    def back(slot, row):
        result = norm(
            grads[0, slot, row], wide[frame.pixels(slot, row), :], frame.inside(slot, row + 1)
        )
        lowered_grad[0, slot, row] = result.astype(BF16)

    frame.each(back)
    for slot in range(slots):
        span = frame.span(slot)
        term = dot_turned(lowered_grad[0, slot].reshape(part, -1), down[0])

        @pl.when(branch == 0)
        def _():
            sums[span, :] = term + shared_grad[slot].reshape(part, channels)

        @pl.when(branch > 0)
        def _():
            sums[span, :] += term

    @pl.when(branch == pl.num_programs(0) - 1)
    def _():
        average2, inverse2 = moments(totals, 0, count[0])

        def body(slot, row):
            centred = (source[slot, row] - average2) * inverse2
            normed = line(gain, 1) * centred + line(shift, 1)
            result = sums[frame.pixels(slot, row), :] * silu_slope(normed)
            result = jnp.where(frame.inside(slot, row + 1), result, 0.0)
            incoming[slot, row] = result
            return result, result * centred

        result = frame.summed(body)
        frame.pack(packed, far, lambda slot, row: incoming[slot, row], result)


def hidden_back_kernel(
    info, count, kept, sent, gain, shift, weight, first, first_totals, incoming, packed, far,
    three, sums, held, arrived,
):
    slots, rows, breadth, channels = sums.shape
    frame = Frame(info, slots, rows, breadth, channels)
    copies = weight_copies(weight, held, arrived, (1,))
    for copy in copies:
        copy.start()
    fill_halves(frame, kept, sent, three)
    for copy in copies:
        copy.wait()
    backward_conv(three, held, sums)
    average, inverse = moments(first_totals, 0, count[0])

    def body(slot, row):
        centred = (first[slot, row] - average) * inverse
        normed = line(gain, 0) * centred + line(shift, 0)
        result = sums[slot, row] * silu_slope(normed)
        result = jnp.where(frame.inside(slot, row + 1), result, 0.0)
        incoming[slot, row] = result
        return result, result * centred

    result = frame.summed(body)
    frame.pack(packed, far, lambda slot, row: incoming[slot, row], result)


def one_grad_kernel(
    info, count, grads, grad_near, grad_far, source, near, outer, totals, back, gain, kept, sent, member
):
    frame = Frame(info, *source.shape)
    fill_back(
        frame, count[0], grads, grad_near, grad_far, source, near, outer,
        totals, back, line(gain, member), None, kept, sent, (), 0,
    )


def input_back_kernel(info, kept, sent, weight, out, three, held, arrived):
    slots, rows, breadth, channels = out.shape
    frame = Frame(info, slots, rows, breadth, channels)
    copies = weight_copies(weight, held, arrived, (0,))
    for copy in copies:
        copy.start()
    fill_halves(frame, kept, sent, three)
    for copy in copies:
        copy.wait()
    backward_conv(three, held, out)

    def mask(slot, row):
        out[slot, row] = jnp.where(frame.inside(slot, row + 1), out[slot, row], 0.0)

    frame.each(mask)


def weight_grad_kernel(source, source_other, grads, grads_other, out, three):
    slots, tall, breadth, channels = grads.shape
    rows = tall - 2

    def put(row, carry):
        for slot in range(slots):
            put_three(three, slot, row, grads[slot, row].astype(F32), True)
            put_three(three, slots + slot, row, grads_other[slot, row].astype(F32), True)
        return carry

    lax.fori_loop(0, tall, put, 0)
    height = source.shape[3]
    for step in range(3):
        for tap in range(3):
            total = None
            for slot in range(2 * slots):
                left = source[slot] if slot < slots else source_other[slot - slots]
                lanes = slice(tap * channels, (tap + 1) * channels)
                window = three[slot, 2 - step : 2 - step + rows, :, lanes]
                one = dot_over_rows(
                    left.reshape(rows * breadth, height), window.reshape(rows * breadth, channels)
                )
                total = one if total is None else total + one
            start = (3 * step + tap) * height
            out[start : start + height, :] = total.astype(BF16)


def split_grad_kernel(info, source, source_other, grads, grads_other, *refs, cuts, bits_at):
    three, whole = refs[-2:]
    weight_grad_kernel(source, source_other, grads, grads_other, whole, three)
    width = whole.shape[1] // len(cuts)
    first = 0
    for index, (low, count) in enumerate(cuts):
        outs = refs[first : first + (1 << count)]
        first += 1 << count
        blocks, height, _ = outs[0].shape
        lanes = slice(index * width, (index + 1) * width)
        for flip, out in enumerate(outs):
            chosen = which_block(info, bits_at, low, count, flip)
            for block in range(blocks):
                start = ((block << count) + chosen) * height
                out[block] = whole[pl.ds(pl.multiple_of(start, 16), height), lanes]


def which_block(info, bits_at, low, count, flip):
    number = 0
    for index in range(count):
        bit = info[bits_at + low + index]
        number = number + ((1 - bit if flip >> index & 1 else bit) << index)
    return number


def spread_kernel(info, *refs, low, count, lanes, members, bits_at):
    terms, outs = refs[: -(1 << count)], refs[-(1 << count) :]
    each = len(terms) // members
    for flip, out in enumerate(outs):
        chosen = which_block(info, bits_at, low, count, flip)
        blocks = out.shape[0] // members
        for member in range(members):
            group = terms[member * each : (member + 1) * each]
            for block in range(blocks):
                place = member * blocks + block
                if each == 1:
                    out[place] = group[0][block, chosen, :, lanes]
                    continue
                total = group[0][block, chosen].astype(F32)
                for term in group[1:]:
                    total = total + term[block, chosen].astype(F32)
                out[place] = total.astype(BF16)


def relay_kernel(value, same):
    pass


def settle_kernel(*refs, plan):
    out = refs[-1]
    start = 0
    for row, height, columns, count in plan:
        terms = refs[start : start + count]
        start += count
        width = terms[0].shape[1]
        for column in range(columns):
            span = slice(column * height, (column + 1) * height)
            total = terms[0][span, :].astype(F32)
            for term in terms[1:]:
                total = total + term[span, :].astype(F32)
            lanes = slice(column * width, (column + 1) * width)
            out[row : row + height, lanes] = total.astype(BF16)


def thin_grad_kernel(info, shared, lowered_grad, raised_grad, squeezed, kept, sent, bits_at):
    slots, tall, _, channels = shared.shape
    odd = info[bits_at] == 1
    half = kept.shape[-1]

    def flat(block):
        return block.reshape(-1, block.shape[-1])

    for index in range(2):
        total = None
        for slot in range(slots):
            if index == 0:
                one = dot_over_rows(flat(shared[slot, 1 : tall - 1]), flat(lowered_grad[0, slot]))
            else:
                one = dot_over_rows(
                    flat(raised_grad[0, slot]), flat(squeezed[0, slot, 1 : tall - 1])
                )
            total = one if total is None else total + one
        low, high = total[:, :half], total[:, half:]
        kept[0, index] = jnp.where(odd, high, low).astype(BF16)
        sent[0, index] = jnp.where(odd, low, high).astype(BF16)


def join_kernel(info, *refs, bits_at):
    odd = info[bits_at] == 1
    upper = info[bits_at + 1]
    outs = refs[8:]

    def join(pieces, outs):
        start = 0
        half = pieces[0].shape[-1]
        for out in outs:
            height = out.shape[2]
            for member in range(out.shape[0]):
                span = slice(start, start + height)
                start += height
                for flip in range(2):
                    mine = pieces[2 * flip][span, :].astype(F32)
                    other = pieces[2 * flip + 1][span, :].astype(F32)
                    row = jnp.where(upper == flip, 0, 1)
                    out[member, row, :, :half] = jnp.where(odd, other, mine)
                    out[member, row, :, half:] = jnp.where(odd, mine, other)

    join(refs[:4], [outs[1]])
    join(refs[4:8], [outs[0], outs[2]])


def outputs_kernel(first, second, down, up, conv, *outs):
    for index in range(2):
        outs[index][0:1, :] = first[1 - index : 2 - index, :]
        outs[index][1:2, :] = second[1 - index : 2 - index, :]
    for place, totals in ((2, down), (4, up), (6, conv)):
        for member in range(outs[place].shape[0]):
            for index in range(2):
                row = 2 * member + 1 - index
                outs[place + index][member : member + 1, :] = totals[row : row + 1, :]


SCALARS = pl.BlockSpec(memory_space=pltpu.SMEM)
ELSEWHERE = pl.BlockSpec(memory_space=pl.ANY)


def fixed(shape):
    zeros = (0,) * len(shape)
    return pl.BlockSpec(tuple(shape), lambda *_: zeros)


def by_branch(shape):
    zeros = (0,) * (len(shape) - 1)
    return pl.BlockSpec((1,) + tuple(shape[1:]), lambda branch, *_: (branch,) + zeros)


def call(name, body, grid, inputs, outputs, scratch, flops, room=16, after=(), aliases={}):
    total = sum(a.size * a.dtype.itemsize for a, _ in inputs)
    if after:
        count, inner = len(inputs), body

        def body(*refs):
            inner(*refs[:count], *refs[count + len(after) :])

        inputs = inputs + [(a, ELSEWHERE) for a in after]
    return pl.pallas_call(
        body,
        name=name,
        grid=grid,
        in_specs=[s for _, s in inputs],
        out_specs=[s for _, _, s in outputs],
        out_shape=[jax.ShapeDtypeStruct(s, d) for s, d, _ in outputs],
        scratch_shapes=scratch,
        compiler_params=pltpu.CompilerParams(
            vmem_limit_bytes=room * MIB, dimension_semantics=("arbitrary",) * len(grid)
        ),
        input_output_aliases=aliases,
        cost_estimate=pl.CostEstimate(flops=flops, bytes_accessed=total, transcendentals=0),
    )(*[a for a, _ in inputs])


def whole(a):
    return (a, fixed(a.shape))


def branch_of(a):
    return (a, by_branch(a.shape))


def out(shape, dtype):
    return (tuple(shape), dtype, fixed(shape))


def out_branch(shape, dtype):
    return (tuple(shape), dtype, by_branch(shape))


def branch_weight(a):
    return (pltpu.with_memory_space_constraint(a, pltpu.HBM), by_branch(a.shape))


def in_hbm(a):
    return (pltpu.with_memory_space_constraint(a, pltpu.HBM), ELSEWHERE)


class Halving:
    def __init__(self, reducer, parts, order, rows):
        self.reducer, self.order, self.rows = reducer, list(order), rows
        self.kept, self.sent = parts[0], parts[1:]
        self.columns = 1

    def received(self):
        low, _ = self.order[0]
        return [swapped(a, (flip + 1) << low) for flip, a in enumerate(self.sent)]

    def terms(self):
        return [self.kept] + self.received()

    def step(self):
        terms = self.terms()
        self.order = self.order[1:]
        self.kept, *self.sent = self.reducer.spread([terms], self.rows, self.order)


def merged(halvings, columns=1):
    first = halvings[0]
    groups = [one.terms() for one in halvings]
    order = first.order[1:]
    parts = first.reducer.spread(groups, first.rows, order)
    result = Halving(first.reducer, parts, order, first.rows)
    result.columns = columns
    return result


class Reducer:
    def __init__(self, info, bits_at):
        self.info = info
        self.bits_at = bits_at
        self.bits = places().bit_length() - 1
        self.dp = lax.axis_size("dp")
        self.last = ()
        assert lax.axis_size("rows") == 4

    def call(self, *args, after=(), **kwargs):
        result = call(*args, after=(*after, *self.last), **kwargs)
        self.last = tuple(result[-1:])
        return result

    def relay(self, value):
        return self.call(
            "relay",
            relay_kernel,
            (1,),
            [(value, ELSEWHERE)],
            [(value.shape, value.dtype, ELSEWHERE)],
            [],
            0,
            room=4,
            aliases={0: 0},
        )[0]

    def spread(self, groups, rows, order, after=(), lanes=None):
        low, count = order[0]
        height, width = self.block_rows(rows, order), groups[0][0].shape[-1]
        lanes = lanes or (0, width)
        view = (-1, 1 << count, height, width)
        terms = [term.reshape(view) for group in groups for term in group]
        blocks = terms[0].shape[0]
        steps = 1
        if len(groups) == 1:
            steps = next(n for n in (4, 3, 2, 1) if blocks % n == 0)

        def cut(shape):
            return pl.BlockSpec(
                (shape[0] // steps,) + shape[1:], lambda step: (step,) + (0,) * (len(shape) - 1)
            )

        result = (blocks * len(groups), height, lanes[1] - lanes[0])
        return self.call(
            "spread",
            functools.partial(
                spread_kernel,
                low=low,
                count=count,
                lanes=slice(*lanes),
                members=len(groups),
                bits_at=self.bits_at,
            ),
            (steps,),
            [(self.info, SCALARS)] + [(term, cut(term.shape)) for term in terms],
            [(result, BF16, cut(result))] * (1 << count),
            [],
            0,
            room=8,
            after=after,
        )

    def settle(self, halvings):
        arrays, plan, row = [], [], 0
        for one in halvings:
            flat = (-1, one.kept.shape[-1])
            terms = [term.reshape(flat) for term in one.terms()]
            height = terms[0].shape[0] // one.columns
            plan.append((row, height, one.columns, len(terms)))
            arrays += terms
            row += height
        width = arrays[0].shape[1] * halvings[0].columns
        return self.call(
            "settle",
            functools.partial(settle_kernel, plan=plan),
            (1,),
            [whole(a) for a in arrays],
            [out((row, width), BF16)],
            [],
            0,
            room=8,
        )[0]

    def order(self, axis):
        if axis == "xy":
            return [(low, min(2, self.bits - low)) for low in range(1, self.bits, 2)]
        rest = list(range(3, self.bits))
        order = {"x": [1, 2] + rest, "y": [2, 1] + rest, "z": rest + [1, 2]}[axis]
        return [(bit, 1) for bit in order]

    def block_rows(self, rows, order):
        below = sum(count for low, count in order if low < order[0][0])
        return rows << below

    def pieces(self, piece):
        beside = swapped(piece, 2)
        return [piece, swapped(piece, 1), beside, swapped(beside, 1)]

    def join(self, gathered, pieces, members):
        width = pieces[0].shape[-1]
        results = self.call(
            "join",
            functools.partial(join_kernel, bits_at=self.bits_at),
            (1,),
            [(self.info, SCALARS)] + [whole(piece) for piece in [*gathered, *pieces]],
            [out((count, 2, rows // 2, 2 * width), F32) for count, rows in members],
            [],
            0,
            room=24,
        )
        return [r.reshape(r.shape[0], -1, r.shape[-1]) for r in results]


def local(
    images,
    size_ids,
    shared_conv,
    task_conv,
    task_down,
    task_up,
    shared_gain,
    shared_shift,
    down_gain,
    down_shift,
    up_gain,
    up_shift,
    conv_gain,
    conv_shift,
    cotangent,
):
    slots, rows, breadth, channels = images.shape
    tasks = task_conv.shape[0]
    tall = rows + 2
    part = rows * breadth
    half = channels // 2
    heights_all = jnp.where(size_ids == 0, H_BIG, H_SMALL).astype(jnp.int32)
    breadths_all = jnp.where(size_ids == 0, W_BIG, W_SMALL).astype(jnp.int32)
    count = jnp.sum(heights_all * breadths_all).astype(F32).reshape(1)
    first_slot = lax.axis_index("dp") * slots
    heights = lax.dynamic_slice_in_dim(heights_all, first_slot, slots)
    breadths = lax.dynamic_slice_in_dim(breadths_all, first_slot, slots)
    row_place = lax.axis_index("rows") * rows + jnp.arange(-1, rows + 1, dtype=jnp.int32)
    within = (row_place[None, :] >= 0) & (row_place[None, :] < heights[:, None])
    limits = jnp.where(within, breadths[:, None], 0).astype(jnp.int32).reshape(-1)
    bits_at = slots * tall
    place = lax.axis_index("dp") * lax.axis_size("rows") + lax.axis_index("rows")
    bits = (place >> jnp.arange(places().bit_length() - 1, dtype=jnp.int32)) & 1
    info = jnp.concatenate([limits, bits.astype(jnp.int32)])
    scalars = [(info, SCALARS), (count, SCALARS)]

    map_shape = (slots, rows, breadth, channels)
    tall_shape = (slots, tall, breadth, channels)
    half_shape = (slots, tall, breadth, half)
    conv_flops = 2 * slots * part * 9 * channels * channels
    thin_flops = conv_flops // 9

    def all_tasks(shape):
        return (tasks,) + tuple(shape)

    def sums_only():
        return out((SUMS, channels), F32)

    def packed(groups):
        return [
            out((groups * slots * breadth + SUMS, channels), F32),
            out((groups * slots, breadth, channels), F32 if groups == 1 else BF16),
        ]

    three = pltpu.VMEM((slots, tall, breadth, 3 * channels), BF16)
    flat = pltpu.VMEM((slots * part, channels), F32)
    flat_tall = pltpu.VMEM((slots * tall * breadth, channels), F32)
    square = pltpu.VMEM(map_shape, F32)
    one_weight = [pltpu.VMEM((9 * channels, channels), BF16), pltpu.SemaphoreType.DMA((3,))]
    two_weights = [pltpu.VMEM((2, 9 * channels, channels), BF16), pltpu.SemaphoreType.DMA((2, 3))]

    count_rows = lax.axis_size("rows")
    image_above = lax.ppermute(
        images[:, rows - 1], "rows", [(i, i + 1) for i in range(count_rows - 1)]
    )
    image_below = lax.ppermute(images[:, 0], "rows", [(i + 1, i) for i in range(count_rows - 1)])
    first_out, first_packed, first_far, masked = call(
        "first_conv",
        first_kernel,
        (1,),
        [scalars[0], whole(images), whole(image_above), whole(image_below), in_hbm(shared_conv)],
        [out(map_shape, F32)] + packed(1) + [out(map_shape, BF16)],
        [three] + one_weight,
        conv_flops,
    )
    first_totals, first_near, first_outer = norm_totals(first_packed, first_far)

    second_out, second_packed, second_far, hidden = call(
        "second_conv",
        second_kernel,
        (1,),
        scalars
        + [whole(a) for a in (first_out, first_near, first_outer, first_totals)]
        + [whole(shared_gain), whole(shared_shift), in_hbm(shared_conv)],
        [out(map_shape, F32)] + packed(1) + [out(map_shape, BF16)],
        [three] + one_weight,
        conv_flops,
    )
    second_totals, second_near, second_outer = norm_totals(second_packed, second_far)

    shared, down_packed = call(
        "lower",
        lower_kernel,
        (tasks,),
        scalars
        + [whole(a) for a in (second_out, second_near, second_outer, second_totals)]
        + [whole(shared_gain), whole(shared_shift), branch_weight(task_down)],
        [out(tall_shape, BF16), sums_only()],
        [flat],
        3 * thin_flops,
    )
    down_totals = norm_totals(down_packed)

    squeezed, up_packed = call(
        "raise",
        raise_kernel,
        (tasks,),
        scalars
        + [whole(shared), branch_weight(task_down), branch_weight(task_up)]
        + [whole(a) for a in (down_totals, down_gain, down_shift)],
        [out_branch(all_tasks(tall_shape), BF16), sums_only()],
        [flat_tall, flat],
        6 * thin_flops,
    )
    up_totals = norm_totals(up_packed)

    conv_out, conv_packed, conv_far, gated = call(
        "task_conv",
        task_kernel,
        (tasks,),
        scalars
        + [branch_of(squeezed), branch_weight(task_up)]
        + [whole(a) for a in (shared, up_totals, up_gain, up_shift)]
        + [in_hbm(task_conv)],
        [out_branch(all_tasks(map_shape), F32)]
        + packed(tasks)
        + [out_branch(all_tasks(map_shape), BF16)],
        [flat_tall, three] + two_weights,
        tasks * conv_flops,
        room=22,
    )
    conv_totals, conv_near, conv_outer = norm_totals(conv_packed, conv_far)

    maps, conv_grad, conv_back_packed, conv_grad_far = call(
        "pool",
        pool_kernel,
        (tasks,),
        scalars
        + [branch_of(conv_out), branch_of(cotangent)]
        + [whole(a) for a in (conv_totals, conv_gain, conv_shift)],
        [
            out_branch(all_tasks((slots, rows // 2, breadth // 2, channels)), BF16),
            out_branch(all_tasks(map_shape), F32),
        ]
        + packed(tasks),
        [pltpu.VMEM((slots, channels // 128, breadth, 128), F32)] * 2,
        thin_flops,
    )
    conv_back, conv_grad_near, conv_grad_outer = norm_totals(conv_back_packed, conv_grad_far)

    reducer = Reducer(info, bits_at)
    dp_count = reducer.dp
    wide_rows = 9 * channels // dp_count

    share_rows = wide_rows // 2

    def weight_whole(source, source_other, kept, sent, after=()):
        return reducer.call(
            "weight_grad",
            weight_grad_kernel,
            (1,),
            [whole(a) for a in (source, source_other, kept, swapped(sent, 1))],
            [out((9 * channels, half), BF16)],
            [pltpu.VMEM((2 * slots, tall, breadth, 3 * half), BF16)],
            conv_flops,
            after=after,
        )[0]

    def weight_sum(source, source_other, kept, sent, axes, after=()):
        orders = [reducer.order(axis) for axis in axes]
        width = half // len(orders)
        if share_rows % 16:
            total = weight_whole(source, source_other, kept, sent, after)
            parts = [
                reducer.spread([[total]], share_rows, order, (), (index * width, (index + 1) * width))
                for index, order in enumerate(orders)
            ]
        else:
            shapes = []
            for order in orders:
                height = reducer.block_rows(share_rows, order)
                shape = ((9 * channels // height) >> order[0][1], height, width)
                shapes += [shape] * (1 << order[0][1])
            results = reducer.call(
                "weight_grad",
                functools.partial(
                    split_grad_kernel, cuts=[order[0] for order in orders], bits_at=bits_at
                ),
                (1,),
                [(info, SCALARS)]
                + [whole(a) for a in (source, source_other, kept, swapped(sent, 1))],
                [out(shape, BF16) for shape in shapes],
                [
                    pltpu.VMEM((2 * slots, tall, breadth, 3 * half), BF16),
                    pltpu.VMEM((9 * channels, half), BF16),
                ],
                conv_flops,
                after=after,
            )
            parts = []
            for order in orders:
                parts.append(results[: 1 << order[0][1]])
                results = results[1 << order[0][1] :]
        return [Halving(reducer, part, order, share_rows) for part, order in zip(parts, orders)]

    masked_other, hidden_other, gated_other = (swapped(a, 1) for a in (masked, hidden, gated))

    conv_kept, conv_sent = reducer.call(
        "conv_grad",
        conv_grad_kernel,
        (tasks,),
        scalars
        + [branch_of(conv_grad), whole(conv_grad_near), whole(conv_grad_outer)]
        + [branch_of(conv_out), whole(conv_near), whole(conv_outer)]
        + [whole(a) for a in (conv_totals, conv_back, conv_gain)],
        [out_branch(all_tasks(half_shape), BF16)] * 2,
        [],
        0,
    )

    def step(*halvings):
        for one in halvings:
            one.step()

    def task_grads(t):
        return gated[t], gated_other[t], conv_kept[t], conv_sent[t]

    early = [weight_sum(*task_grads(t), ["xy"[t]])[0] for t in range(2)]
    up_grad_in, shared_grad, up_back_packed = reducer.call(
        "gate_back",
        gate_back_kernel,
        (tasks,),
        scalars
        + [branch_of(conv_kept), branch_of(conv_sent)]
        + [in_hbm(task_conv), branch_of(squeezed), branch_weight(task_up)]
        + [whole(a) for a in (shared, up_totals, up_gain, up_shift)],
        [
            out_branch(all_tasks(map_shape), F32),
            out(map_shape, F32),
            sums_only(),
        ],
        [three, square, flat] + two_weights,
        tasks * conv_flops,
        room=22,
        after=[masked_other, hidden_other],
    )
    step(*early)
    up_back = norm_totals(reducer.relay(up_back_packed))
    raised_grad, down_grad_in, down_back_packed = reducer.call(
        "raise_back",
        raise_back_kernel,
        (tasks,),
        scalars
        + [branch_of(up_grad_in), branch_of(squeezed), branch_weight(task_up), whole(shared)]
        + [branch_weight(task_down)]
        + [
            whole(a)
            for a in (up_totals, up_back, up_gain, down_totals, down_gain, down_shift)
        ],
        [
            out_branch(all_tasks(map_shape), BF16),
            out_branch(all_tasks(map_shape), F32),
            sums_only(),
        ],
        [flat, flat],
        9 * thin_flops,
    )
    early = merged(early)
    down_back = norm_totals(reducer.relay(down_back_packed))
    late = weight_sum(*task_grads(2), "xy", after=[down_back])

    lowered_grad, second_grad, second_back_packed, second_grad_far = reducer.call(
        "lower_back",
        lower_back_kernel,
        (tasks,),
        scalars
        + [branch_of(down_grad_in), whole(shared), branch_weight(task_down)]
        + [whole(a) for a in (down_totals, down_back, down_gain, shared_grad, second_out)]
        + [whole(a) for a in (second_totals, shared_gain, shared_shift)],
        [out_branch(all_tasks(map_shape), BF16), out(map_shape, F32)] + packed(1),
        [flat, flat],
        6 * thin_flops,
    )
    square_shape = (tasks, 2, channels, half)
    thin_kept, thin_sent = reducer.call(
        "thin_grad",
        functools.partial(thin_grad_kernel, bits_at=bits_at),
        (tasks,),
        [(info, SCALARS), whole(shared)]
        + [branch_of(a) for a in (lowered_grad, raised_grad, squeezed)],
        [out_branch(square_shape, BF16)] * 2,
        [],
        6 * thin_flops,
    )
    thin_got = swapped(thin_sent, 1)
    step(early, *late)
    second_back, second_grad_near, second_grad_outer = norm_totals(
        reducer.relay(second_back_packed), second_grad_far
    )

    second_kept, second_sent = reducer.call(
        "second_grad",
        functools.partial(one_grad_kernel, member=1),
        (1,),
        scalars
        + [
            whole(a)
            for a in (
                second_grad, second_grad_near, second_grad_outer, second_out, second_near, second_outer,
                second_totals, second_back, shared_gain,
            )
        ],
        [out(half_shape, BF16)] * 2,
        [],
        0,
    )
    second_sum = weight_sum(hidden, hidden_other, second_kept, second_sent, "xy")
    late = merged(late, 2)
    first_grad, first_back_packed, first_grad_far = reducer.call(
        "hidden_back",
        hidden_back_kernel,
        (1,),
        scalars
        + [whole(second_kept), whole(second_sent), whole(shared_gain), whole(shared_shift)]
        + [in_hbm(shared_conv), whole(first_out), whole(first_totals)],
        [out(map_shape, F32)] + packed(1),
        [three, square] + one_weight,
        conv_flops,
    )
    step(*second_sum, late)
    first_back, first_grad_near, first_grad_outer = norm_totals(
        reducer.relay(first_back_packed), first_grad_far
    )

    thin_order = reducer.order("y")
    thin_rows = channels // dp_count // 2
    thin_parts = reducer.spread([[thin_kept, thin_got]], thin_rows, thin_order, [first_back])
    thin = Halving(reducer, thin_parts, thin_order, thin_rows)
    first_kept, first_sent = reducer.call(
        "first_grad",
        functools.partial(one_grad_kernel, member=0),
        (1,),
        scalars
        + [
            whole(a)
            for a in (
                first_grad, first_grad_near, first_grad_outer, first_out, first_near, first_outer,
                first_totals, first_back, shared_gain,
            )
        ],
        [out(half_shape, BF16)] * 2,
        [],
        0,
    )
    second_sum = merged(second_sum, 2)
    first_sum = weight_sum(masked, masked_other, first_kept, first_sent, ["xy"])

    task_share = reducer.settle([early, late])
    beside = swapped(task_share, 2)
    (input_grad,) = reducer.call(
        "input_back",
        input_back_kernel,
        (1,),
        [scalars[0], whole(first_kept), whole(first_sent), in_hbm(shared_conv)],
        [out(map_shape, F32)],
        [three] + one_weight,
        8 * conv_flops,
    )

    step(thin, *first_sum, second_sum)
    beside = reducer.relay(beside)
    step(thin, thin)
    task_pieces = [task_share, swapped(task_share, 1), beside, swapped(beside, 1)]
    shared_sums, task_sums, thin_sums = reducer.join(
        task_pieces,
        reducer.pieces(reducer.settle(first_sum + [second_sum, thin])),
        [(2, wide_rows), (tasks, wide_rows), (2 * tasks, channels // dp_count)],
    )

    pair_shape = (2, channels)
    many_shape = (tasks, channels)
    small = call(
        "outputs",
        outputs_kernel,
        (1,),
        [whole(a) for a in (first_back, second_back, down_back, up_back, conv_back)],
        [out(pair_shape, F32)] * 2 + [out(many_shape, F32)] * 6,
        [],
        0,
        room=4,
    )
    return (
        maps,
        input_grad,
        shared_sums,
        task_sums,
        thin_sums[0::2],
        thin_sums[1::2].transpose(0, 2, 1),
        *small,
    )


def solution(mesh):
    placed = (P("dp", "rows", None, None),) + (P(),) * 13 + (P(None, "dp", "rows", None, None),)
    return jax.shard_map(
        local,
        mesh=mesh,
        in_specs=placed,
        out_specs=(
            P(None, "dp", "rows", None, None),
            P("dp", "rows", None, None),
            P(None, "dp", None),
            P(None, "dp", None),
            P(None, "dp", None),
            P(None, None, "dp"),
        )
        + (P(),) * 8,
        check_vma=False,
    )
```

```python
import functools

import jax
import jax.numpy as jnp
from jax import lax
from jax.experimental import pallas as pl
from jax.experimental.pallas import tpu as pltpu
from jax.sharding import PartitionSpec as P

H_BIG = 36
W_BIG = 48
H_SMALL = 18
W_SMALL = 24
EPSILON = 1e-05
AXES = ("dp", "rows")
F32 = jnp.float32
BF16 = jnp.bfloat16
MIB = 1024 * 1024
SUMS = 8


def places():
    return lax.axis_size("dp") * lax.axis_size("rows")


def swapped(values, flip):
    return lax.ppermute(values, AXES, [(i, i ^ flip) for i in range(places())])


def swapped_far(values):
    count = lax.axis_size("rows")
    pairs = [(i, i + 1) for i in range(1, count - 1, 2)]
    return lax.ppermute(values, "rows", pairs + [(j, i) for i, j in pairs])


def exchange_sum(values, got, beside=()):
    bits = places().bit_length() - 1
    assert places() == 1 << bits
    values = values + got
    place = 1
    while place < bits:
        low = 1 << place
        if place + 1 < bits:
            high = low * 2
            values = (values + swapped(values, low)) + (
                swapped(values, high) + swapped(values, high + low)
            )
            if place == 1 and beside:
                values = passed_on(values, beside)
            place += 2
        else:
            values = values + swapped(values, low)
            place += 1
    return values


def norm_totals(packed, far=None):
    got = swapped(packed, 1)
    edges = packed.shape[0] - SUMS
    if far is None:
        return exchange_sum(packed[edges:], got[edges:])
    outer = swapped_far(far)
    return exchange_sum(packed[edges:], got[edges:], [outer]), got, outer


def dot(left, right):
    return jnp.dot(left, right, preferred_element_type=F32)


def dot_turned(left, right):
    return lax.dot_general(left, right, (((1,), (1,)), ((), ())), preferred_element_type=F32)


def dot_over_rows(left, right):
    return lax.dot_general(left, right, (((0,), (0,)), ((), ())), preferred_element_type=F32)


class Frame:
    def __init__(self, info, slots, rows, breadth, channels):
        self.info, self.slots, self.rows = info, slots, rows
        self.breadth, self.channels = breadth, channels
        self.tall = rows + 2
        odd = self.bit(0) == 1
        self.near_rim = jnp.where(odd, 0, rows + 1)
        self.far_rim = rows + 1 - self.near_rim
        self.near_row = jnp.where(odd, 0, rows - 1)
        self.far_row = rows - 1 - self.near_row

    def bit(self, index):
        return self.info[self.slots * self.tall + index]

    def inside(self, slot, tall_row):
        shape = (self.breadth, self.channels)
        limit = self.info[slot * self.tall + tall_row]
        return lax.broadcasted_iota(jnp.int32, shape, 0) < limit

    def each(self, body):
        self.rows_of(self.rows, body)

    def rows_of(self, rows, body):
        group = 2 if rows % 2 == 0 else 1

        def step(index, carry):
            for part in range(group):
                for slot in range(self.slots):
                    body(slot, index * group + part)
            return carry

        lax.fori_loop(0, rows // group, step, 0)

    def summed(self, body, rows=None):
        rows = rows or self.rows
        group = 2 if rows % 2 == 0 else 1

        def step(index, carry):
            one, two = carry
            for part in range(group):
                for slot in range(self.slots):
                    first, second = body(slot, index * group + part)
                    one, two = one + fold(first), two + fold(second)
            return one, two

        zero = jnp.zeros((8, self.channels), F32)
        one, two = lax.fori_loop(0, rows // group, step, (zero, zero))
        return jnp.sum(one, axis=0, keepdims=True), jnp.sum(two, axis=0, keepdims=True)

    def rims(self, sources, body, group=0):
        for slot in range(self.slots):
            index = group * self.slots + slot
            start = index * self.breadth
            if not isinstance(start, int):
                start = pl.multiple_of(start, 8)
            body(slot, self.near_rim, *[near[pl.ds(start, self.breadth), :] for near, _ in sources])
            body(slot, self.far_rim, *[far[index].astype(F32) for _, far in sources])

    def pack(self, packed, far, rows_of, sums, group=0):
        edges = packed.shape[0] - SUMS

        @pl.when(jnp.equal(group, 0))
        def _():
            packed[edges:, :] = jnp.zeros((SUMS, self.channels), F32)

        packed[pl.ds(edges + 2 * group, 1), :] = sums[0]
        packed[pl.ds(edges + 2 * group + 1, 1), :] = sums[1]
        if far is None:
            return
        for slot in range(self.slots):
            index = group * self.slots + slot
            start = index * self.breadth
            if not isinstance(start, int):
                start = pl.multiple_of(start, 8)
            packed[pl.ds(start, self.breadth), :] = rows_of(slot, self.near_row)
            far[index] = rows_of(slot, self.far_row).astype(far.dtype)

    def pixels(self, slot, row, rows=None):
        start = (slot * (rows or self.rows) + row) * self.breadth
        return pl.ds(pl.multiple_of(start, 8), self.breadth)

    def span(self, slot, rows=None):
        part = (rows or self.rows) * self.breadth
        return slice(slot * part, (slot + 1) * part)


def moments(totals, member, count):
    average = totals[pl.ds(2 * member, 1), :] / count
    variance = totals[pl.ds(2 * member + 1, 1), :] / count - average * average
    return average, lax.rsqrt(variance + EPSILON)


def line(ref, member):
    return ref[pl.ds(member, 1), :]


def sigmoid(values):
    return jax.nn.sigmoid(values)


def silu_slope(values):
    logistic = sigmoid(values)
    return logistic * (1.0 + values * (1.0 - logistic))


def fold(values):
    return jnp.sum(values.reshape(-1, 8, values.shape[-1]), axis=0)


def put_three(ref, slot, row, values, flipped):
    breadth, channels = values.shape
    col = lax.broadcasted_iota(jnp.int32, values.shape, 0)
    before = jnp.where(col == 0, 0.0, pltpu.roll(values, 1, 0))
    after = jnp.where(col == breadth - 1, 0.0, pltpu.roll(values, breadth - 1, 0))
    if flipped:
        before, after = after, before
    ref[slot, row, :, 0:channels] = before.astype(BF16)
    ref[slot, row, :, channels : 2 * channels] = values.astype(BF16)
    ref[slot, row, :, 2 * channels :] = after.astype(BF16)


def weight_copies(source, target, arrived, lead=()):
    third = target.shape[-2] // 3
    return [
        pltpu.make_async_copy(
            source.at[lead + (pl.ds(part * third, third),)],
            target.at[pl.ds(part * third, third)],
            arrived.at[part],
        )
        for part in range(3)
    ]


def forward_conv(three, weight, sums, lead=()):
    slots, rows, breadth, channels = sums.shape[-4:]
    third = weight.shape[0] // 3
    for slot in range(slots):
        total = None
        for step in range(3):
            window = three[slot, step : step + rows].reshape(rows * breadth, third)
            one = dot(window, weight[step * third : (step + 1) * third, :])
            total = one if total is None else total + one
        sums[lead + (slot,)] = total.reshape(rows, breadth, channels)


def backward_conv(three, weight, sums):
    slots, rows, breadth, channels = sums.shape[-4:]
    wide = three.shape[-1] // 3
    for slot in range(slots):
        total = None
        for step in range(3):
            window = three[slot, 2 - step : 2 - step + rows].reshape(rows * breadth, 3 * wide)
            for tap in range(3):
                start = (3 * step + tap) * channels
                one = dot_turned(
                    window[:, tap * wide : (tap + 1) * wide], weight[start : start + channels, :]
                )
                total = one if total is None else total + one
        sums[slot] = total.reshape(rows, breadth, channels)


def conv_sums(frame, sums, lead, packed, far, group=0):
    def body(slot, row):
        values = sums[lead + (slot, row)]
        kept = jnp.where(frame.inside(slot, row + 1), values, 0.0)
        return kept, kept * values

    result = frame.summed(body)
    frame.pack(packed, far, lambda slot, row: sums[lead + (slot, row)], result, group)


def plain_sums(frame, source):
    def body(slot, row):
        values = source[frame.pixels(slot, row), :]
        return values, values * values

    return frame.summed(body)


def activation(values, inside, average, inverse, gain, shift):
    normed = gain * ((values - average) * inverse) + shift
    return jnp.where(inside, normed * sigmoid(normed), 0.0)


class NormBack:
    def __init__(self, totals, back, gain, member, count):
        self.average, self.inverse = moments(totals, member, count)
        self.slope = gain * self.inverse
        self.level = self.slope * back[pl.ds(2 * member, 1), :] / count
        self.along = self.slope * back[pl.ds(2 * member + 1, 1), :] / count

    def __call__(self, grad, values, inside):
        centred = (values - self.average) * self.inverse
        return self.slope * grad - jnp.where(inside, self.level + centred * self.along, 0.0)


def first_kernel(
    info, images, above, below, weight, sums, packed, far, masked, three, held, arrived
):
    slots, rows, breadth, channels = images.shape
    frame = Frame(info, slots, rows, breadth, channels)
    copies = weight_copies(weight, held, arrived, (0,))
    for copy in copies:
        copy.start()

    def put(slot, row, values):
        kept = jnp.where(frame.inside(slot, row), values.astype(F32), 0.0)
        put_three(three, slot, row, kept, False)
        return kept

    def own(slot, row):
        masked[slot, row] = put(slot, row + 1, images[slot, row]).astype(BF16)

    frame.each(own)
    for slot in range(slots):
        put(slot, 0, above[slot])
        put(slot, rows + 1, below[slot])
    for copy in copies:
        copy.wait()
    forward_conv(three, held, sums)
    conv_sums(frame, sums, (), packed, far)


def second_kernel(
    info, count, source, near, outer, totals, gain, shift, weight, sums, packed, far, hidden, three, held, arrived
):
    slots, rows, breadth, channels = source.shape
    frame = Frame(info, slots, rows, breadth, channels)
    copies = weight_copies(weight, held, arrived, (1,))
    for copy in copies:
        copy.start()
    average, inverse = moments(totals, 0, count[0])

    def act(slot, row, values):
        inside = frame.inside(slot, row)
        result = activation(values, inside, average, inverse, line(gain, 0), line(shift, 0))
        put_three(three, slot, row, result, False)
        return result

    def own(slot, row):
        hidden[slot, row] = act(slot, row + 1, source[slot, row]).astype(BF16)

    frame.each(own)
    frame.rims([(near, outer)], act)
    for copy in copies:
        copy.wait()
    forward_conv(three, held, sums)
    conv_sums(frame, sums, (), packed, far)


def lower_kernel(
    info, count, source, near, outer, totals, gain, shift, down, shared, packed, lowered
):
    branch = pl.program_id(0)
    slots, rows, breadth, channels = source.shape
    frame = Frame(info, slots, rows, breadth, channels)

    @pl.when(branch == 0)
    def _():
        average, inverse = moments(totals, 0, count[0])

        def act(slot, row, values):
            inside = frame.inside(slot, row)
            result = activation(values, inside, average, inverse, line(gain, 1), line(shift, 1))
            shared[slot, row] = result.astype(BF16)

        frame.each(lambda slot, row: act(slot, row + 1, source[slot, row]))
        frame.rims([(near, outer)], act)

    for slot in range(slots):
        lowered[frame.span(slot), :] = dot(
            shared[slot, 1 : rows + 1].reshape(rows * breadth, channels), down[0]
        )
    frame.pack(packed, None, None, plain_sums(frame, lowered), branch)


def raise_kernel(
    info, count, shared, down, up, totals, gain, shift, squeezed, packed, wide, raised
):
    branch = pl.program_id(0)
    slots, tall, breadth, channels = shared.shape
    rows = tall - 2
    frame = Frame(info, slots, rows, breadth, channels)
    wide[...] = dot(shared[...].reshape(slots * tall * breadth, channels), down[0])
    average, inverse = moments(totals, branch, count[0])

    def act(slot, row):
        values = wide[frame.pixels(slot, row, tall), :]
        result = activation(
            values, frame.inside(slot, row), average, inverse, line(gain, branch), line(shift, branch)
        )
        squeezed[0, slot, row] = result.astype(BF16)

    frame.rows_of(tall, act)
    for slot in range(slots):
        raised[frame.span(slot), :] = dot(
            squeezed[0, slot, 1 : rows + 1].reshape(rows * breadth, -1), up[0]
        )
    frame.pack(packed, None, None, plain_sums(frame, raised), branch)


def task_weight(branch, weight, held, arrived):
    def copies(which):
        buffer = which % 2
        return weight_copies(weight, held.at[buffer], arrived.at[buffer], (which,))

    @pl.when(branch == 0)
    def _():
        for copy in copies(branch):
            copy.start()

    def ready():
        for copy in copies(branch):
            copy.wait()

        @pl.when(branch + 1 < pl.num_programs(0))
        def _():
            for copy in copies(branch + 1):
                copy.start()

    return ready


def task_kernel(
    info, count, squeezed, up, shared, totals, gain, shift, weight, sums, packed, far, gated,
    wide, three, held, arrived,
):
    branch = pl.program_id(0)
    slots, tall, breadth, channels = shared.shape
    rows = tall - 2
    frame = Frame(info, slots, rows, breadth, channels)
    ready = task_weight(branch, weight, held, arrived)
    wide[...] = dot(squeezed[0].reshape(slots * tall * breadth, -1), up[0])
    average, inverse = moments(totals, branch, count[0])

    def gate(slot, row):
        values = wide[frame.pixels(slot, row, tall), :]
        normed = line(gain, branch) * ((values - average) * inverse) + line(shift, branch)
        result = sigmoid(normed) * shared[slot, row].astype(F32)
        put_three(three, slot, row, result, False)
        return result

    def own(slot, row):
        gated[0, slot, row] = gate(slot, row + 1).astype(BF16)

    frame.each(own)
    for slot in range(slots):
        gate(slot, 0)
        gate(slot, rows + 1)
    ready()
    forward_conv(three, held.at[branch % 2], sums, (0,))
    conv_sums(frame, sums, (0,), packed, far, branch)


def pool_kernel(
    info, count, source, cotangent, totals, gain, shift, maps, slope, packed, far, spread, pairs
):
    branch = pl.program_id(0)
    slots, rows, breadth, channels = source.shape[1:]
    frame = Frame(info, slots, rows, breadth, channels)
    average, inverse = moments(totals, branch, count[0])
    half = breadth // 2
    groups = channels // 128

    def body(slot, pooled):
        block = cotangent[0, slot, pooled].astype(F32) * 0.25
        for group in range(groups):
            lanes = block[:, group * 128 : (group + 1) * 128]
            spread[slot, group, pl.ds(0, half, stride=2), :] = lanes
            spread[slot, group, pl.ds(1, half, stride=2), :] = lanes
        wide = jnp.concatenate([spread[slot, group] for group in range(groups)], axis=1)
        one = two = total = None
        for parity in range(2):
            row = 2 * pooled + parity
            inside = frame.inside(slot, row + 1)
            centred = (source[0, slot, row] - average) * inverse
            normed = line(gain, branch) * centred + line(shift, branch)
            logistic = sigmoid(normed)
            active = jnp.where(inside, normed * logistic, 0.0)
            grad = wide * (logistic * (1.0 + normed * (1.0 - logistic)))
            grad = jnp.where(inside, grad, 0.0)
            slope[0, slot, row] = grad
            along = grad * centred
            if parity == 0:
                one, two, total = grad, along, active
            else:
                one, two, total = one + grad, two + along, total + active
        for group in range(groups):
            lanes = slice(group * 128, (group + 1) * 128)
            pairs[slot, group] = total[:, lanes]
            even = pairs[slot, group, pl.ds(0, half, stride=2), :]
            odd = pairs[slot, group, pl.ds(1, half, stride=2), :]
            maps[0, slot, pooled, :, lanes] = ((even + odd) * 0.25).astype(BF16)
        return one, two

    sums = frame.summed(body, rows // 2)
    frame.pack(packed, far, lambda slot, row: slope[0, slot, row], sums, branch)


def fill_back(
    frame, count, grads, grad_near, grad_far, source, near, outer, totals, back, gain, three, kept, sent, lead, member
):
    norm = NormBack(totals, back, gain, member, count)
    odd = frame.bit(0) == 1
    half = frame.channels // 2

    def put(slot, row, grad, values):
        result = norm(grad, values, frame.inside(slot, row))
        if three is not None:
            put_three(three, slot, row, result, True)
        low, high = result[:, :half], result[:, half:]
        kept[lead + (slot, row)] = jnp.where(odd, high, low).astype(BF16)
        sent[lead + (slot, row)] = jnp.where(odd, low, high).astype(BF16)

    def own(slot, row):
        put(slot, row + 1, grads[lead + (slot, row)], source[lead + (slot, row)])

    frame.each(own)
    frame.rims([(grad_near, grad_far), (near, outer)], put, member if lead else 0)


def conv_grad_kernel(
    info, count, grads, grad_near, grad_far, source, near, outer, totals, back, gain, kept, sent
):
    branch = pl.program_id(0)
    frame = Frame(info, *source.shape[1:])
    fill_back(
        frame, count[0], grads, grad_near, grad_far, source, near, outer,
        totals, back, line(gain, branch), None, kept, sent, (0,), branch,
    )


def fill_halves(frame, kept, sent, three, lead=()):
    odd = frame.bit(0) == 1

    def put(slot, row):
        mine = kept[lead + (slot, row)].astype(F32)
        other = sent[lead + (slot, row)].astype(F32)
        low, high = jnp.where(odd, other, mine), jnp.where(odd, mine, other)
        put_three(three, slot, row, jnp.concatenate([low, high], axis=1), True)

    frame.rows_of(frame.tall, put)


def gate_back_kernel(
    info, count, kept, sent, weight, squeezed, up, shared, up_totals, up_gain, up_shift,
    incoming, shared_grad, packed, three, sums, raised, held, arrived,
):
    branch = pl.program_id(0)
    slots, rows, breadth, channels = sums.shape
    frame = Frame(info, slots, rows, breadth, channels)
    ready = task_weight(branch, weight, held, arrived)
    fill_halves(frame, kept, sent, three, (0,))
    for slot in range(slots):
        raised[frame.span(slot), :] = dot(
            squeezed[0, slot, 1 : rows + 1].reshape(rows * breadth, -1), up[0]
        )
    ready()
    backward_conv(three, held.at[branch % 2], sums)
    average, inverse = moments(up_totals, branch, count[0])

    @pl.when(branch == 0)
    def _():
        shared_grad[...] = jnp.zeros(shared_grad.shape, F32)

    def body(slot, row):
        centred = (raised[frame.pixels(slot, row), :] - average) * inverse
        attention = sigmoid(line(up_gain, branch) * centred + line(up_shift, branch))
        onward = sums[slot, row] * attention
        result = onward * shared[slot, row + 1].astype(F32) * (1.0 - attention)
        incoming[0, slot, row] = result.astype(BF16)
        shared_grad[slot, row] += onward
        return result, result * centred

    frame.pack(packed, None, None, frame.summed(body), branch)


def raise_back_kernel(
    info, count, grads, squeezed, up, shared, down, up_totals, up_back, up_gain, down_totals, down_gain,
    down_shift, raised_grad, incoming, packed, wide, sums,
):
    branch = pl.program_id(0)
    slots, rows, breadth, channels = grads.shape[1:]
    part = rows * breadth
    frame = Frame(info, slots, rows, breadth, channels)
    for slot in range(slots):
        wide[frame.span(slot), :] = dot(squeezed[0, slot, 1 : rows + 1].reshape(part, -1), up[0])
    norm = NormBack(up_totals, up_back, line(up_gain, branch), branch, count[0])

    def back(slot, row):
        result = norm(
            grads[0, slot, row].astype(F32), wide[frame.pixels(slot, row), :], frame.inside(slot, row + 1)
        )
        raised_grad[0, slot, row] = result.astype(BF16)

    frame.each(back)
    for slot in range(slots):
        sums[frame.span(slot), :] = dot_turned(raised_grad[0, slot].reshape(part, channels), up[0])
        wide[frame.span(slot), :] = dot(
            shared[slot, 1 : rows + 1].reshape(part, channels), down[0]
        )
    average2, inverse2 = moments(down_totals, branch, count[0])

    def body(slot, row):
        centred = (wide[frame.pixels(slot, row), :] - average2) * inverse2
        normed = line(down_gain, branch) * centred + line(down_shift, branch)
        result = sums[frame.pixels(slot, row), :] * silu_slope(normed)
        result = jnp.where(frame.inside(slot, row + 1), result, 0.0)
        incoming[0, slot, row] = result
        return result, result * centred

    frame.pack(packed, None, None, frame.summed(body), branch)


def lower_back_kernel(
    info, count, grads, shared, down, down_totals, down_back, down_gain, shared_grad, source, totals, gain,
    shift, lowered_grad, incoming, packed, far, wide, sums,
):
    branch = pl.program_id(0)
    slots, rows, breadth, channels = source.shape
    part = rows * breadth
    frame = Frame(info, slots, rows, breadth, channels)
    for slot in range(slots):
        wide[frame.span(slot), :] = dot(
            shared[slot, 1 : rows + 1].reshape(part, channels), down[0]
        )
    norm = NormBack(down_totals, down_back, line(down_gain, branch), branch, count[0])

    def back(slot, row):
        result = norm(
            grads[0, slot, row], wide[frame.pixels(slot, row), :], frame.inside(slot, row + 1)
        )
        lowered_grad[0, slot, row] = result.astype(BF16)

    frame.each(back)
    for slot in range(slots):
        span = frame.span(slot)
        term = dot_turned(lowered_grad[0, slot].reshape(part, -1), down[0])

        @pl.when(branch == 0)
        def _():
            sums[span, :] = term + shared_grad[slot].reshape(part, channels)

        @pl.when(branch > 0)
        def _():
            sums[span, :] += term

    @pl.when(branch == pl.num_programs(0) - 1)
    def _():
        average2, inverse2 = moments(totals, 0, count[0])

        def body(slot, row):
            centred = (source[slot, row] - average2) * inverse2
            normed = line(gain, 1) * centred + line(shift, 1)
            result = sums[frame.pixels(slot, row), :] * silu_slope(normed)
            result = jnp.where(frame.inside(slot, row + 1), result, 0.0)
            incoming[slot, row] = result
            return result, result * centred

        result = frame.summed(body)
        frame.pack(packed, far, lambda slot, row: incoming[slot, row], result)


def hidden_back_kernel(
    info, count, kept, sent, gain, shift, weight, first, first_totals, incoming, packed, far,
    three, sums, held, arrived,
):
    slots, rows, breadth, channels = sums.shape
    frame = Frame(info, slots, rows, breadth, channels)
    copies = weight_copies(weight, held, arrived, (1,))
    for copy in copies:
        copy.start()
    fill_halves(frame, kept, sent, three)
    for copy in copies:
        copy.wait()
    backward_conv(three, held, sums)
    average, inverse = moments(first_totals, 0, count[0])

    def body(slot, row):
        centred = (first[slot, row] - average) * inverse
        normed = line(gain, 0) * centred + line(shift, 0)
        result = sums[slot, row] * silu_slope(normed)
        result = jnp.where(frame.inside(slot, row + 1), result, 0.0)
        incoming[slot, row] = result
        return result, result * centred

    result = frame.summed(body)
    frame.pack(packed, far, lambda slot, row: incoming[slot, row], result)


def one_grad_kernel(
    info, count, grads, grad_near, grad_far, source, near, outer, totals, back, gain, kept, sent, member
):
    frame = Frame(info, *source.shape)
    fill_back(
        frame, count[0], grads, grad_near, grad_far, source, near, outer,
        totals, back, line(gain, member), None, kept, sent, (), 0,
    )


def input_back_kernel(info, kept, sent, weight, out, three, held, arrived):
    slots, rows, breadth, channels = out.shape
    frame = Frame(info, slots, rows, breadth, channels)
    copies = weight_copies(weight, held, arrived, (0,))
    for copy in copies:
        copy.start()
    fill_halves(frame, kept, sent, three)
    for copy in copies:
        copy.wait()
    backward_conv(three, held, out)

    def mask(slot, row):
        out[slot, row] = jnp.where(frame.inside(slot, row + 1), out[slot, row], 0.0)

    frame.each(mask)


def weight_grad_kernel(source, source_other, grads, grads_other, out, three):
    slots, tall, breadth, channels = grads.shape
    rows = tall - 2

    def put(row, carry):
        for slot in range(slots):
            put_three(three, slot, row, grads[slot, row].astype(F32), True)
            put_three(three, slots + slot, row, grads_other[slot, row].astype(F32), True)
        return carry

    lax.fori_loop(0, tall, put, 0)
    height = source.shape[3]
    for step in range(3):
        for tap in range(3):
            total = None
            for slot in range(2 * slots):
                left = source[slot] if slot < slots else source_other[slot - slots]
                lanes = slice(tap * channels, (tap + 1) * channels)
                window = three[slot, 2 - step : 2 - step + rows, :, lanes]
                one = dot_over_rows(
                    left.reshape(rows * breadth, height), window.reshape(rows * breadth, channels)
                )
                total = one if total is None else total + one
            start = (3 * step + tap) * height
            out[start : start + height, :] = total.astype(BF16)


def split_grad_kernel(info, source, source_other, grads, grads_other, *refs, cuts, bits_at):
    three, whole = refs[-2:]
    weight_grad_kernel(source, source_other, grads, grads_other, whole, three)
    width = whole.shape[1] // len(cuts)
    first = 0
    for index, (low, count) in enumerate(cuts):
        outs = refs[first : first + (1 << count)]
        first += 1 << count
        blocks, height, _ = outs[0].shape
        lanes = slice(index * width, (index + 1) * width)
        for flip, out in enumerate(outs):
            chosen = which_block(info, bits_at, low, count, flip)
            for block in range(blocks):
                start = ((block << count) + chosen) * height
                out[block] = whole[pl.ds(pl.multiple_of(start, 16), height), lanes]


def which_block(info, bits_at, low, count, flip):
    number = 0
    for index in range(count):
        bit = info[bits_at + low + index]
        number = number + ((1 - bit if flip >> index & 1 else bit) << index)
    return number


def spread_kernel(info, *refs, low, count, lanes, members, bits_at):
    terms, outs = refs[: -(1 << count)], refs[-(1 << count) :]
    each = len(terms) // members
    for flip, out in enumerate(outs):
        chosen = which_block(info, bits_at, low, count, flip)
        blocks = out.shape[0] // members
        for member in range(members):
            group = terms[member * each : (member + 1) * each]
            for block in range(blocks):
                place = member * blocks + block
                if each == 1:
                    out[place] = group[0][block, chosen, :, lanes]
                    continue
                total = group[0][block, chosen].astype(F32)
                for term in group[1:]:
                    total = total + term[block, chosen].astype(F32)
                out[place] = total.astype(BF16)


def relay_kernel(value, same):
    pass


def settle_kernel(*refs, plan):
    out = refs[-1]
    start = 0
    for row, height, columns, count in plan:
        terms = refs[start : start + count]
        start += count
        width = terms[0].shape[1]
        for column in range(columns):
            span = slice(column * height, (column + 1) * height)
            total = terms[0][span, :].astype(F32)
            for term in terms[1:]:
                total = total + term[span, :].astype(F32)
            lanes = slice(column * width, (column + 1) * width)
            out[row : row + height, lanes] = total.astype(BF16)


def thin_grad_kernel(info, shared, lowered_grad, raised_grad, squeezed, kept, sent, bits_at):
    slots, tall, _, channels = shared.shape
    odd = info[bits_at] == 1
    half = kept.shape[-1]

    def flat(block):
        return block.reshape(-1, block.shape[-1])

    for index in range(2):
        total = None
        for slot in range(slots):
            if index == 0:
                one = dot_over_rows(flat(shared[slot, 1 : tall - 1]), flat(lowered_grad[0, slot]))
            else:
                one = dot_over_rows(
                    flat(raised_grad[0, slot]), flat(squeezed[0, slot, 1 : tall - 1])
                )
            total = one if total is None else total + one
        low, high = total[:, :half], total[:, half:]
        kept[0, index] = jnp.where(odd, high, low).astype(BF16)
        sent[0, index] = jnp.where(odd, low, high).astype(BF16)


def join_kernel(info, *refs, bits_at):
    odd = info[bits_at] == 1
    upper = info[bits_at + 1]
    outs = refs[8:]

    def join(pieces, outs):
        start = 0
        half = pieces[0].shape[-1]
        for out in outs:
            height = out.shape[2]
            for member in range(out.shape[0]):
                span = slice(start, start + height)
                start += height
                for flip in range(2):
                    mine = pieces[2 * flip][span, :].astype(F32)
                    other = pieces[2 * flip + 1][span, :].astype(F32)
                    row = jnp.where(upper == flip, 0, 1)
                    out[member, row, :, :half] = jnp.where(odd, other, mine)
                    out[member, row, :, half:] = jnp.where(odd, mine, other)

    join(refs[:4], [outs[1]])
    join(refs[4:8], [outs[0], outs[2]])


def outputs_kernel(first, second, down, up, conv, *outs):
    for index in range(2):
        outs[index][0:1, :] = first[1 - index : 2 - index, :]
        outs[index][1:2, :] = second[1 - index : 2 - index, :]
    for place, totals in ((2, down), (4, up), (6, conv)):
        for member in range(outs[place].shape[0]):
            for index in range(2):
                row = 2 * member + 1 - index
                outs[place + index][member : member + 1, :] = totals[row : row + 1, :]


SCALARS = pl.BlockSpec(memory_space=pltpu.SMEM)
ELSEWHERE = pl.BlockSpec(memory_space=pl.ANY)


def fixed(shape):
    zeros = (0,) * len(shape)
    return pl.BlockSpec(tuple(shape), lambda *_: zeros)


def by_branch(shape):
    zeros = (0,) * (len(shape) - 1)
    return pl.BlockSpec((1,) + tuple(shape[1:]), lambda branch, *_: (branch,) + zeros)


def call(name, body, grid, inputs, outputs, scratch, flops, room=16, after=(), aliases={}):
    total = sum(a.size * a.dtype.itemsize for a, _ in inputs)
    if after:
        count, inner = len(inputs), body

        def body(*refs):
            inner(*refs[:count], *refs[count + len(after) :])

        inputs = inputs + [(a, ELSEWHERE) for a in after]
    return pl.pallas_call(
        body,
        name=name,
        grid=grid,
        in_specs=[s for _, s in inputs],
        out_specs=[s for _, _, s in outputs],
        out_shape=[jax.ShapeDtypeStruct(s, d) for s, d, _ in outputs],
        scratch_shapes=scratch,
        compiler_params=pltpu.CompilerParams(
            vmem_limit_bytes=room * MIB, dimension_semantics=("arbitrary",) * len(grid)
        ),
        input_output_aliases=aliases,
        cost_estimate=pl.CostEstimate(flops=flops, bytes_accessed=total, transcendentals=0),
    )(*[a for a, _ in inputs])


def whole(a):
    return (a, fixed(a.shape))


def passed_on(value, after):
    return call(
        "relay",
        relay_kernel,
        (1,),
        [(value, ELSEWHERE)],
        [(value.shape, value.dtype, ELSEWHERE)],
        [],
        0,
        room=4,
        after=after,
        aliases={0: 0},
    )[0]


def branch_of(a):
    return (a, by_branch(a.shape))


def one_of(a, index):
    if index is None:
        return whole(a)
    zeros = (0,) * (len(a.shape) - 1)
    return (a, pl.BlockSpec((None,) + a.shape[1:], lambda *_: (index,) + zeros))


def out(shape, dtype):
    return (tuple(shape), dtype, fixed(shape))


def out_branch(shape, dtype):
    return (tuple(shape), dtype, by_branch(shape))


def branch_weight(a):
    return (pltpu.with_memory_space_constraint(a, pltpu.HBM), by_branch(a.shape))


def in_hbm(a):
    return (pltpu.with_memory_space_constraint(a, pltpu.HBM), ELSEWHERE)


class Halving:
    def __init__(self, reducer, parts, order, rows):
        self.reducer, self.order, self.rows = reducer, list(order), rows
        self.kept, self.sent = parts[0], parts[1:]
        self.columns = 1

    def received(self):
        low, _ = self.order[0]
        return [swapped(a, (flip + 1) << low) for flip, a in enumerate(self.sent)]

    def terms(self):
        return [self.kept] + self.received()

    def step(self):
        terms = self.terms()
        self.order = self.order[1:]
        self.kept, *self.sent = self.reducer.spread([terms], self.rows, self.order)


def merged(halvings, columns=1):
    first = halvings[0]
    groups = [one.terms() for one in halvings]
    order = first.order[1:]
    parts = first.reducer.spread(groups, first.rows, order)
    result = Halving(first.reducer, parts, order, first.rows)
    result.columns = columns
    return result


class Reducer:
    def __init__(self, info, bits_at):
        self.info = info
        self.bits_at = bits_at
        self.bits = places().bit_length() - 1
        self.dp = lax.axis_size("dp")
        self.last = ()
        assert lax.axis_size("rows") == 4

    def call(self, *args, after=(), **kwargs):
        result = call(*args, after=(*after, *self.last), **kwargs)
        self.last = tuple(result[-1:])
        return result

    def relay(self, value):
        return self.call(
            "relay",
            relay_kernel,
            (1,),
            [(value, ELSEWHERE)],
            [(value.shape, value.dtype, ELSEWHERE)],
            [],
            0,
            room=4,
            aliases={0: 0},
        )[0]

    def spread(self, groups, rows, order, after=(), lanes=None):
        low, count = order[0]
        height, width = self.block_rows(rows, order), groups[0][0].shape[-1]
        lanes = lanes or (0, width)
        view = (-1, 1 << count, height, width)
        terms = [term.reshape(view) for group in groups for term in group]
        blocks = terms[0].shape[0]
        steps = 1
        if len(groups) == 1:
            steps = next(n for n in (4, 3, 2, 1) if blocks % n == 0)

        def cut(shape):
            return pl.BlockSpec(
                (shape[0] // steps,) + shape[1:], lambda step: (step,) + (0,) * (len(shape) - 1)
            )

        result = (blocks * len(groups), height, lanes[1] - lanes[0])
        return self.call(
            "spread",
            functools.partial(
                spread_kernel,
                low=low,
                count=count,
                lanes=slice(*lanes),
                members=len(groups),
                bits_at=self.bits_at,
            ),
            (steps,),
            [(self.info, SCALARS)] + [(term, cut(term.shape)) for term in terms],
            [(result, BF16, cut(result))] * (1 << count),
            [],
            0,
            room=8,
            after=after,
        )

    def settle(self, halvings):
        arrays, plan, row = [], [], 0
        for one in halvings:
            flat = (-1, one.kept.shape[-1])
            terms = [term.reshape(flat) for term in one.terms()]
            height = terms[0].shape[0] // one.columns
            plan.append((row, height, one.columns, len(terms)))
            arrays += terms
            row += height
        width = arrays[0].shape[1] * halvings[0].columns
        return self.call(
            "settle",
            functools.partial(settle_kernel, plan=plan),
            (1,),
            [whole(a) for a in arrays],
            [out((row, width), BF16)],
            [],
            0,
            room=8,
        )[0]

    def order(self, axis):
        if axis == "xy":
            return [(low, min(2, self.bits - low)) for low in range(1, self.bits, 2)]
        rest = list(range(3, self.bits))
        order = {"x": [1, 2] + rest, "y": [2, 1] + rest, "z": rest + [1, 2]}[axis]
        return [(bit, 1) for bit in order]

    def block_rows(self, rows, order):
        below = sum(count for low, count in order if low < order[0][0])
        return rows << below

    def pieces(self, piece):
        beside = swapped(piece, 2)
        return [piece, swapped(piece, 1), beside, swapped(beside, 1)]

    def join(self, gathered, pieces, members):
        width = pieces[0].shape[-1]
        results = self.call(
            "join",
            functools.partial(join_kernel, bits_at=self.bits_at),
            (1,),
            [(self.info, SCALARS)] + [whole(piece) for piece in [*gathered, *pieces]],
            [out((count, 2, rows // 2, 2 * width), F32) for count, rows in members],
            [],
            0,
            room=24,
        )
        return [r.reshape(r.shape[0], -1, r.shape[-1]) for r in results]


def local(
    images,
    size_ids,
    shared_conv,
    task_conv,
    task_down,
    task_up,
    shared_gain,
    shared_shift,
    down_gain,
    down_shift,
    up_gain,
    up_shift,
    conv_gain,
    conv_shift,
    cotangent,
):
    slots, rows, breadth, channels = images.shape
    tasks = task_conv.shape[0]
    tall = rows + 2
    part = rows * breadth
    half = channels // 2
    heights_all = jnp.where(size_ids == 0, H_BIG, H_SMALL).astype(jnp.int32)
    breadths_all = jnp.where(size_ids == 0, W_BIG, W_SMALL).astype(jnp.int32)
    count = jnp.sum(heights_all * breadths_all).astype(F32).reshape(1)
    first_slot = lax.axis_index("dp") * slots
    heights = lax.dynamic_slice_in_dim(heights_all, first_slot, slots)
    breadths = lax.dynamic_slice_in_dim(breadths_all, first_slot, slots)
    row_place = lax.axis_index("rows") * rows + jnp.arange(-1, rows + 1, dtype=jnp.int32)
    within = (row_place[None, :] >= 0) & (row_place[None, :] < heights[:, None])
    limits = jnp.where(within, breadths[:, None], 0).astype(jnp.int32).reshape(-1)
    bits_at = slots * tall
    place = lax.axis_index("dp") * lax.axis_size("rows") + lax.axis_index("rows")
    bits = (place >> jnp.arange(places().bit_length() - 1, dtype=jnp.int32)) & 1
    info = jnp.concatenate([limits, bits.astype(jnp.int32)])
    scalars = [(info, SCALARS), (count, SCALARS)]

    map_shape = (slots, rows, breadth, channels)
    tall_shape = (slots, tall, breadth, channels)
    half_shape = (slots, tall, breadth, half)
    conv_flops = 2 * slots * part * 9 * channels * channels
    thin_flops = conv_flops // 9

    def all_tasks(shape):
        return (tasks,) + tuple(shape)

    def sums_only():
        return out((SUMS, channels), F32)

    def packed(groups):
        return [
            out((groups * slots * breadth + SUMS, channels), F32),
            out((groups * slots, breadth, channels), BF16),
        ]

    three = pltpu.VMEM((slots, tall, breadth, 3 * channels), BF16)
    flat = pltpu.VMEM((slots * part, channels), F32)
    flat_tall = pltpu.VMEM((slots * tall * breadth, channels), F32)
    square = pltpu.VMEM(map_shape, F32)
    one_weight = [pltpu.VMEM((9 * channels, channels), BF16), pltpu.SemaphoreType.DMA((3,))]
    two_weights = [pltpu.VMEM((2, 9 * channels, channels), BF16), pltpu.SemaphoreType.DMA((2, 3))]

    count_rows = lax.axis_size("rows")
    image_above = lax.ppermute(
        images[:, rows - 1], "rows", [(i, i + 1) for i in range(count_rows - 1)]
    )
    image_below = lax.ppermute(images[:, 0], "rows", [(i + 1, i) for i in range(count_rows - 1)])
    first_out, first_packed, first_far, masked = call(
        "first_conv",
        first_kernel,
        (1,),
        [scalars[0], whole(images), whole(image_above), whole(image_below), in_hbm(shared_conv)],
        [out(map_shape, F32)] + packed(1) + [out(map_shape, BF16)],
        [three] + one_weight,
        conv_flops,
    )
    first_totals, first_near, first_outer = norm_totals(first_packed, first_far)

    second_out, second_packed, second_far, hidden = call(
        "second_conv",
        second_kernel,
        (1,),
        scalars
        + [whole(a) for a in (first_out, first_near, first_outer, first_totals)]
        + [whole(shared_gain), whole(shared_shift), in_hbm(shared_conv)],
        [out(map_shape, F32)] + packed(1) + [out(map_shape, BF16)],
        [three] + one_weight,
        conv_flops,
    )
    second_totals, second_near, second_outer = norm_totals(second_packed, second_far)

    shared, down_packed = call(
        "lower",
        lower_kernel,
        (tasks,),
        scalars
        + [whole(a) for a in (second_out, second_near, second_outer, second_totals)]
        + [whole(shared_gain), whole(shared_shift), branch_weight(task_down)],
        [out(tall_shape, BF16), sums_only()],
        [flat],
        3 * thin_flops,
    )
    down_totals = norm_totals(down_packed)

    squeezed, up_packed = call(
        "raise",
        raise_kernel,
        (tasks,),
        scalars
        + [whole(shared), branch_weight(task_down), branch_weight(task_up)]
        + [whole(a) for a in (down_totals, down_gain, down_shift)],
        [out_branch(all_tasks(tall_shape), BF16), sums_only()],
        [flat_tall, flat],
        6 * thin_flops,
    )
    up_totals = norm_totals(up_packed)

    conv_out, conv_packed, conv_far, gated = call(
        "task_conv",
        task_kernel,
        (tasks,),
        scalars
        + [branch_of(squeezed), branch_weight(task_up)]
        + [whole(a) for a in (shared, up_totals, up_gain, up_shift)]
        + [in_hbm(task_conv)],
        [out_branch(all_tasks(map_shape), F32)]
        + packed(tasks)
        + [out_branch(all_tasks(map_shape), BF16)],
        [flat_tall, three] + two_weights,
        tasks * conv_flops,
        room=22,
    )
    conv_totals, conv_near, conv_outer = norm_totals(conv_packed, conv_far)

    maps, conv_grad, conv_back_packed, conv_grad_far = call(
        "pool",
        pool_kernel,
        (tasks,),
        scalars
        + [branch_of(conv_out), branch_of(cotangent)]
        + [whole(a) for a in (conv_totals, conv_gain, conv_shift)],
        [
            out_branch(all_tasks((slots, rows // 2, breadth // 2, channels)), BF16),
            out_branch(all_tasks(map_shape), F32),
        ]
        + packed(tasks),
        [pltpu.VMEM((slots, channels // 128, breadth, 128), F32)] * 2,
        thin_flops,
    )
    conv_back, conv_grad_near, conv_grad_outer = norm_totals(conv_back_packed, conv_grad_far)

    reducer = Reducer(info, bits_at)
    dp_count = reducer.dp
    wide_rows = 9 * channels // dp_count

    share_rows = wide_rows // 2

    def weight_whole(source, source_other, kept, sent, after=(), member=None):
        return reducer.call(
            "weight_grad",
            weight_grad_kernel,
            (1,),
            [one_of(a, member) for a in (source, source_other, kept)]
            + [whole(swapped(sent if member is None else sent[member], 1))],
            [out((9 * channels, half), BF16)],
            [pltpu.VMEM((2 * slots, tall, breadth, 3 * half), BF16)],
            conv_flops,
            after=after,
        )[0]

    def weight_sum(source, source_other, kept, sent, axes, after=(), member=None):
        orders = [reducer.order(axis) for axis in axes]
        width = half // len(orders)
        if share_rows % 16:
            total = weight_whole(source, source_other, kept, sent, after, member)
            parts = [
                reducer.spread([[total]], share_rows, order, (), (index * width, (index + 1) * width))
                for index, order in enumerate(orders)
            ]
        else:
            shapes = []
            for order in orders:
                height = reducer.block_rows(share_rows, order)
                shape = ((9 * channels // height) >> order[0][1], height, width)
                shapes += [shape] * (1 << order[0][1])
            results = reducer.call(
                "weight_grad",
                functools.partial(
                    split_grad_kernel, cuts=[order[0] for order in orders], bits_at=bits_at
                ),
                (1,),
                [(info, SCALARS)]
                + [one_of(a, member) for a in (source, source_other, kept)]
            + [whole(swapped(sent if member is None else sent[member], 1))],
                [out(shape, BF16) for shape in shapes],
                [
                    pltpu.VMEM((2 * slots, tall, breadth, 3 * half), BF16),
                    pltpu.VMEM((9 * channels, half), BF16),
                ],
                conv_flops,
                after=after,
            )
            parts = []
            for order in orders:
                parts.append(results[: 1 << order[0][1]])
                results = results[1 << order[0][1] :]
        return [Halving(reducer, part, order, share_rows) for part, order in zip(parts, orders)]

    masked_other, hidden_other, gated_other = (swapped(a, 1) for a in (masked, hidden, gated))

    conv_kept, conv_sent = reducer.call(
        "conv_grad",
        conv_grad_kernel,
        (tasks,),
        scalars
        + [branch_of(conv_grad), whole(conv_grad_near), whole(conv_grad_outer)]
        + [branch_of(conv_out), whole(conv_near), whole(conv_outer)]
        + [whole(a) for a in (conv_totals, conv_back, conv_gain)],
        [out_branch(all_tasks(half_shape), BF16)] * 2,
        [],
        0,
    )

    def step(*halvings):
        for one in halvings:
            one.step()

    task_grads = (gated, gated_other, conv_kept, conv_sent)
    early = [weight_sum(*task_grads, ["xy"[t]], member=t)[0] for t in range(2)]
    up_grad_in, shared_grad, up_back_packed = reducer.call(
        "gate_back",
        gate_back_kernel,
        (tasks,),
        scalars
        + [branch_of(conv_kept), branch_of(conv_sent)]
        + [in_hbm(task_conv), branch_of(squeezed), branch_weight(task_up)]
        + [whole(a) for a in (shared, up_totals, up_gain, up_shift)],
        [
            out_branch(all_tasks(map_shape), BF16),
            out(map_shape, F32),
            sums_only(),
        ],
        [three, square, flat] + two_weights,
        tasks * conv_flops,
        room=22,
        after=[masked_other, hidden_other],
    )
    step(*early)
    up_back = norm_totals(reducer.relay(up_back_packed))
    raised_grad, down_grad_in, down_back_packed = reducer.call(
        "raise_back",
        raise_back_kernel,
        (tasks,),
        scalars
        + [branch_of(up_grad_in), branch_of(squeezed), branch_weight(task_up), whole(shared)]
        + [branch_weight(task_down)]
        + [
            whole(a)
            for a in (up_totals, up_back, up_gain, down_totals, down_gain, down_shift)
        ],
        [
            out_branch(all_tasks(map_shape), BF16),
            out_branch(all_tasks(map_shape), F32),
            sums_only(),
        ],
        [flat, flat],
        9 * thin_flops,
    )
    early = merged(early)
    down_back = norm_totals(reducer.relay(down_back_packed))
    late = weight_sum(*task_grads, "xy", after=[down_back], member=2)

    lowered_grad, second_grad, second_back_packed, second_grad_far = reducer.call(
        "lower_back",
        lower_back_kernel,
        (tasks,),
        scalars
        + [branch_of(down_grad_in), whole(shared), branch_weight(task_down)]
        + [whole(a) for a in (down_totals, down_back, down_gain, shared_grad, second_out)]
        + [whole(a) for a in (second_totals, shared_gain, shared_shift)],
        [out_branch(all_tasks(map_shape), BF16), out(map_shape, F32)] + packed(1),
        [flat, flat],
        6 * thin_flops,
    )
    square_shape = (tasks, 2, channels, half)
    thin_kept, thin_sent = reducer.call(
        "thin_grad",
        functools.partial(thin_grad_kernel, bits_at=bits_at),
        (tasks,),
        [(info, SCALARS), whole(shared)]
        + [branch_of(a) for a in (lowered_grad, raised_grad, squeezed)],
        [out_branch(square_shape, BF16)] * 2,
        [],
        6 * thin_flops,
    )
    thin_got = swapped(thin_sent, 1)
    step(early, *late)
    second_back, second_grad_near, second_grad_outer = norm_totals(
        reducer.relay(second_back_packed), second_grad_far
    )

    second_kept, second_sent = reducer.call(
        "second_grad",
        functools.partial(one_grad_kernel, member=1),
        (1,),
        scalars
        + [
            whole(a)
            for a in (
                second_grad, second_grad_near, second_grad_outer, second_out, second_near, second_outer,
                second_totals, second_back, shared_gain,
            )
        ],
        [out(half_shape, BF16)] * 2,
        [],
        0,
    )
    second_sum = weight_sum(hidden, hidden_other, second_kept, second_sent, "xy")
    late = merged(late, 2)
    first_grad, first_back_packed, first_grad_far = reducer.call(
        "hidden_back",
        hidden_back_kernel,
        (1,),
        scalars
        + [whole(second_kept), whole(second_sent), whole(shared_gain), whole(shared_shift)]
        + [in_hbm(shared_conv), whole(first_out), whole(first_totals)],
        [out(map_shape, F32)] + packed(1),
        [three, square] + one_weight,
        conv_flops,
    )
    step(*second_sum, late)
    first_back, first_grad_near, first_grad_outer = norm_totals(
        reducer.relay(first_back_packed), first_grad_far
    )

    thin_order = reducer.order("y")
    thin_rows = channels // dp_count // 2
    thin_parts = reducer.spread([[thin_kept, thin_got]], thin_rows, thin_order, [first_back])
    thin = Halving(reducer, thin_parts, thin_order, thin_rows)
    first_kept, first_sent = reducer.call(
        "first_grad",
        functools.partial(one_grad_kernel, member=0),
        (1,),
        scalars
        + [
            whole(a)
            for a in (
                first_grad, first_grad_near, first_grad_outer, first_out, first_near, first_outer,
                first_totals, first_back, shared_gain,
            )
        ],
        [out(half_shape, BF16)] * 2,
        [],
        0,
    )
    second_sum = merged(second_sum, 2)
    first_sum = weight_sum(masked, masked_other, first_kept, first_sent, ["xy"])

    task_share = reducer.settle([early, late])
    beside = swapped(task_share, 2)
    (input_grad,) = reducer.call(
        "input_back",
        input_back_kernel,
        (1,),
        [scalars[0], whole(first_kept), whole(first_sent), in_hbm(shared_conv)],
        [out(map_shape, F32)],
        [three] + one_weight,
        8 * conv_flops,
    )

    reducer.last = (pltpu.with_memory_space_constraint(input_grad, pltpu.HBM),)
    step(thin, *first_sum, second_sum)
    beside = reducer.relay(beside)
    step(thin, thin)
    task_pieces = [task_share, swapped(task_share, 1), beside, swapped(beside, 1)]
    shared_sums, task_sums, thin_sums = reducer.join(
        task_pieces,
        reducer.pieces(reducer.settle(first_sum + [second_sum, thin])),
        [(2, wide_rows), (tasks, wide_rows), (2 * tasks, channels // dp_count)],
    )

    pair_shape = (2, channels)
    many_shape = (tasks, channels)
    small = call(
        "outputs",
        outputs_kernel,
        (1,),
        [whole(a) for a in (first_back, second_back, down_back, up_back, conv_back)],
        [out(pair_shape, F32)] * 2 + [out(many_shape, F32)] * 6,
        [],
        0,
        room=4,
    )
    return (
        maps,
        input_grad,
        shared_sums,
        task_sums,
        thin_sums[0::2],
        thin_sums[1::2].transpose(0, 2, 1),
        *small,
    )


def solution(mesh):
    placed = (P("dp", "rows", None, None),) + (P(),) * 13 + (P(None, "dp", "rows", None, None),)
    return jax.shard_map(
        local,
        mesh=mesh,
        in_specs=placed,
        out_specs=(
            P(None, "dp", "rows", None, None),
            P("dp", "rows", None, None),
            P(None, "dp", None),
            P(None, "dp", None),
            P(None, "dp", None),
            P(None, None, "dp"),
        )
        + (P(),) * 8,
        check_vma=False,
    )
```
